32 devices in a mesh: ctx: 16 (over z, x, core), ep: 2 (over y).
Axes of the slice: x: 2, y: 2, z: 4, core: 2. Of those that a mesh axis runs over, the one named last changes fastest.
Arguments:
- resid_in: bfloat16 [4096, 1024], P(('ctx', 'ep')), may hold values from -6 to 6
- out_grad: bfloat16 [4096, 1024], P(('ctx', 'ep')), may hold values from -6 to 6
- attn_gain: float32 [1024], replicated, may hold values from 0.5 to 1.5
- q_weight: bfloat16 [1024, 1024], P(None, 'ep'), may hold values from -0.1875 to 0.1875
- key_value_weight: bfloat16 [2, 1024, 512], P(None, None, 'ep'), may hold values from -0.1875 to 0.1875
- o_weight: bfloat16 [1024, 1024], P('ep'), may hold values from -1.5 to 1.5
- moe_gain: float32 [1024], replicated, may hold values from 0.5 to 1.5
- router: bfloat16 [1024, 16], replicated, may hold values from -0.09375 to 0.09375
- expert_in: bfloat16 [16, 1024, 1024], P('ep'), may hold values from -0.1875 to 0.1875
- expert_out: bfloat16 [16, 512, 1024], P('ep'), may hold values from -1 to 1
- qkv_down: bfloat16 [1024, 96], replicated, may hold values from -0.1875 to 0.1875
- q_up: bfloat16 [32, 1024], P(None, 'ep'), may hold values from -0.75 to 0.75
- key_value_up_factor: bfloat16 [2, 32, 512], P(None, None, 'ep'), may hold values from -0.75 to 0.75
- o_down: bfloat16 [1024, 32], P('ep'), may hold values from -1.5 to 1.5
- o_up: bfloat16 [32, 1024], replicated, may hold values from -0.75 to 0.75
- expert_in_down: bfloat16 [16, 1024, 64], P('ep'), may hold values from -0.1875 to 0.1875
- expert_in_up: bfloat16 [16, 2, 32, 512], P('ep'), may hold values from -0.75 to 0.75
- expert_out_down: bfloat16 [16, 512, 32], P('ep'), may hold values from -0.5 to 0.5
- expert_out_up: bfloat16 [16, 32, 1024], P('ep'), may hold values from -0.75 to 0.75
- expert_ids: int32 [4096, 8], P(('ctx', 'ep')), may hold values from 0 to 15, all different within a row; in each aligned block of 128 rows (0 to 127, 128 to 255, ...) at most 96 rows name the same one
- doc_starts: int32 [8], replicated, may hold values from 0 to 4095, as said below
- doc_adapter: int32 [8], replicated, may hold values from 0 to 1
Outputs:
- block_out: bfloat16 [4096, 1024], P(('ctx', 'ep'))
- in_grad: bfloat16 [4096, 1024], P(('ctx', 'ep'))
- grad_qkv_down: float32 [1024, 96], replicated
- grad_q_up: float32 [32, 1024], P(None, 'ep')
- grad_kv_up: float32 [2, 32, 512], P(None, None, 'ep')
- grad_o_down: float32 [1024, 32], P('ep')
- grad_o_up: float32 [32, 1024], replicated
- grad_expert_in_down: float32 [16, 1024, 64], P('ep')
- grad_expert_in_up: float32 [16, 2, 32, 512], P('ep')
- grad_expert_out_down: float32 [16, 512, 32], P('ep')
- grad_expert_out_up: float32 [16, 32, 1024], P('ep')
The draws below stay inside these ranges and needn't reach their ends.
Inputs may be any that keep to these rules, and one draw needn't show every extreme that they name: `expert_ids`: each row names 8 different experts; among the rows of one device no expert is named by more than 96 rows, and in every draw some device has an expert named by exactly 96 rows. `doc_starts`: strictly increasing, the first is 0; one document begins within the first 256 tokens and ends within the last 256 tokens.
All inputs are finite; a program needn't handle non-finite values.
Results may differ from the reference program's by a relative error of at most 0.035.
Values may be sent and summed in bfloat16 or wider, within the bound.
A program may use at most 128 MiB of HBM per device.

```python
import math
import jax
import jax.numpy as jnp
import numpy as np
from jax import lax

MODEL_WIDTH = 1024
QUERY_HEADS = 16
KEY_VALUE_HEADS = 8
HEAD_WIDTH = 64
FF = 512
TOPK = 8
ADAPTER_RANK = 16
ADAPTER_CHOICES = 2
NDOCS = 8
BLOCK = 256
ROWS = 128
STREAM_TOKENS = 4096
EXPERTS = 16
CAP = 96


def draw_doc_starts(key, part):
    key = jax.random.fold_in(key, 7)
    first_key, second_key = jax.random.split(key)
    leading = (NDOCS - 1) // 2
    trailing = NDOCS - 1 - leading
    opening = jnp.sort(jax.random.choice(first_key, BLOCK - 1, (leading,), replace=False) + 1)
    closing = jnp.sort(jax.random.choice(second_key, BLOCK - 1, (trailing,), replace=False) + 1) + STREAM_TOKENS - BLOCK
    return jnp.concatenate([jnp.zeros((1,), jnp.int32), opening.astype(jnp.int32), closing.astype(jnp.int32)])


def set_ends(values, stream_key, low, high):
    place = [jax.random.randint(jax.random.fold_in(stream_key, axis), (), 0, length) for axis, length in enumerate(values.shape)]
    widest = values.shape.index(max(values.shape))
    beside = place[:widest] + [(place[widest] + 1) % values.shape[widest]] + place[widest + 1:]
    return values.at[tuple(place)].set(low).at[tuple(beside)].set(high)


def levels(stream_key, shape, shards, smallest, top_value):
    level = 1.0
    for position, shards_of in shards:
        steps = jax.random.uniform(jax.random.fold_in(jax.random.fold_in(stream_key, 6), position), (shards_of,), jnp.float32, smallest / len(shards), top_value / len(shards))
        level = level * jnp.repeat(jnp.exp(steps), shape[position] // shards_of).reshape((-1,) + (1,) * (len(shape) - 1 - position))
    return level


def routed_block(rng, own, number, rows, number_of, top, reach, skew):
    order = jax.random.permutation(rng, number_of)
    heavy_load, common = load_shares(number_of, rows * top, reach, skew, True), load_shares(number_of, rows * top, reach, skew, False)
    places = jnp.arange(number_of)

    def named(sizes, offset_by):
        used = int((sizes > 0).sum())
        fixed = max(1, used // 4)
        moved = fixed + (places - fixed + offset_by * (used - fixed)) % max(1, number_of - fixed)
        return jnp.zeros((number_of,), jnp.int32).at[order[jnp.where(places < fixed, places, moved)]].set(jnp.asarray(sizes, jnp.int32))

    sizes = jnp.where(number % 4 == 0, named(heavy_load, number // 4), named(common, number - number // 4 - 1))
    mixed = jax.random.permutation(jax.random.fold_in(own, 3), number_of)
    source_of, sink = mixed[0:number_of // 2 * 2:2], mixed[1:number_of // 2 * 2:2]
    room = jnp.minimum(sizes[source_of] - 1, reach - sizes[sink]) // 2
    room = jnp.where((source_of == order[0]) | (sink == order[0]) | (sizes[sink] == 0), 0, jnp.maximum(room, 0))
    moved = jax.random.randint(jax.random.fold_in(own, 4), (number_of // 2,), 0, 1 << 20) % (room + 1)
    sizes = sizes.at[source_of].add(-moved).at[sink].add(moved)
    items = jnp.searchsorted(jnp.cumsum(sizes), jnp.arange(rows * top), side="right").astype(jnp.int32)
    grid = items.reshape(top, rows).T
    grid = grid[jax.random.permutation(jax.random.fold_in(own, 1), rows)]
    offset_by = jax.random.randint(jax.random.fold_in(own, 2), (rows, 1), 0, top)
    return jnp.take_along_axis(grid, (jnp.arange(top)[None, :] + offset_by) % top, axis=1)


def load_shares(number_of, total, reach, skew, full):
    weights = [(1 << 20) // math.isqrt(grade ** skew) + 1 for grade in range(1, number_of + 1)]
    largest = reach if full else min(reach, max(-(-total // number_of), total * weights[0] // sum(weights)))
    least = 1 if total - largest >= number_of - 1 else 0
    holding, spare = [largest] + [least] * (number_of - 1), total - largest - least * (number_of - 1)
    while spare > 0:
        free = [i for i in range(1, number_of) if holding[i] < largest] or [i for i in range(1, number_of) if holding[i] < reach]
        whole, remaining = sum([weights[i] for i in free]), spare
        for i in free:
            addition = min(reach - holding[i], max(1, remaining * weights[i] // whole), spare)
            holding[i] = holding[i] + addition
            spare = spare - addition
    return np.array(holding)


def noise(rng, extent, scale, limit, cuts=(), held_as=jnp.bfloat16):
    level = levels(rng, extent, cuts, -0.22, 0.18) if cuts else 1.0
    values = jax.random.normal(rng, extent, jnp.float32) * scale * level
    return jnp.minimum(jnp.maximum(values, -limit), limit).astype(held_as)


def setup_inputs(seed: int = 0) -> dict:
    splits = jax.random.split(jax.random.key(seed), 23)
    resid_in = noise(splits[0], (STREAM_TOKENS, MODEL_WIDTH), 1.0, 6.0, ((0, 32),))
    out_grad = noise(splits[1], (STREAM_TOKENS, MODEL_WIDTH), 1.0, 6.0, ((0, 32),))
    attn_gain = jnp.clip(1.0 + 0.1 * jax.random.normal(splits[2], (MODEL_WIDTH,), jnp.float32), 0.5, 1.5)
    q_weight = noise(splits[3], (MODEL_WIDTH, QUERY_HEADS * HEAD_WIDTH), MODEL_WIDTH ** -0.5, 0.1875, ((1, 2),))
    key_value_weight = noise(splits[4], (2, MODEL_WIDTH, KEY_VALUE_HEADS * HEAD_WIDTH), MODEL_WIDTH ** -0.5, 0.1875, ((2, 2),))
    o_weight = noise(splits[5], (QUERY_HEADS * HEAD_WIDTH, MODEL_WIDTH), (QUERY_HEADS * HEAD_WIDTH // 64) ** -0.5, 1.5, ((0, 2),))
    moe_gain = jnp.clip(1.0 + 0.1 * jax.random.normal(splits[6], (MODEL_WIDTH,), jnp.float32), 0.5, 1.5)
    router = noise(splits[7], (MODEL_WIDTH, EXPERTS), (4 * MODEL_WIDTH) ** -0.5, 0.09375)
    expert_in = noise(splits[8], (EXPERTS, MODEL_WIDTH, 2 * FF), MODEL_WIDTH ** -0.5, 0.1875, ((0, 2),))
    expert_out = noise(splits[9], (EXPERTS, FF, MODEL_WIDTH), (FF // 16) ** -0.5, 1.0, ((0, 2),))
    qkv_down = noise(splits[10], (MODEL_WIDTH, 3 * ADAPTER_CHOICES * ADAPTER_RANK), MODEL_WIDTH ** -0.5, 0.1875)
    q_up = noise(splits[11], (ADAPTER_CHOICES * ADAPTER_RANK, QUERY_HEADS * HEAD_WIDTH), (4 * ADAPTER_RANK) ** -0.5, 0.75, ((1, 2),))
    key_value_up_factor = noise(splits[12], (2, ADAPTER_CHOICES * ADAPTER_RANK, KEY_VALUE_HEADS * HEAD_WIDTH), (4 * ADAPTER_RANK) ** -0.5, 0.75, ((2, 2),))
    o_down = noise(splits[13], (QUERY_HEADS * HEAD_WIDTH, ADAPTER_CHOICES * ADAPTER_RANK), (QUERY_HEADS * HEAD_WIDTH // 64) ** -0.5, 1.5, ((0, 2),))
    o_up = noise(splits[14], (ADAPTER_CHOICES * ADAPTER_RANK, MODEL_WIDTH), (4 * ADAPTER_RANK) ** -0.5, 0.75)
    expert_in_down = noise(splits[15], (EXPERTS, MODEL_WIDTH, 2 * ADAPTER_CHOICES * ADAPTER_RANK), MODEL_WIDTH ** -0.5, 0.1875, ((0, 2),))
    expert_in_up = noise(splits[16], (EXPERTS, 2, ADAPTER_CHOICES * ADAPTER_RANK, FF), (4 * ADAPTER_RANK) ** -0.5, 0.75, ((0, 2),))
    expert_out_down = noise(splits[17], (EXPERTS, FF, ADAPTER_CHOICES * ADAPTER_RANK), (FF // 4) ** -0.5, 0.5, ((0, 2),))
    expert_out_up = noise(splits[18], (EXPERTS, ADAPTER_CHOICES * ADAPTER_RANK, MODEL_WIDTH), (4 * ADAPTER_RANK) ** -0.5, 0.75, ((0, 2),))
    expert_ids_keys = jax.random.split(jax.random.fold_in(splits[19], 1), STREAM_TOKENS // ROWS)
    expert_ids_turns = jax.random.permutation(jax.random.fold_in(splits[19], 3), STREAM_TOKENS // ROWS)
    expert_ids = jax.vmap(lambda own, number: routed_block(jax.random.fold_in(splits[19], 2), own, number, ROWS, EXPERTS, TOPK, CAP, 1))(expert_ids_keys, expert_ids_turns).reshape((STREAM_TOKENS, TOPK))
    doc_starts = draw_doc_starts(jax.random.fold_in(splits[22], 71), 0)
    doc_adapter = set_ends(jax.random.randint(splits[21], (NDOCS,), 0, ADAPTER_CHOICES), jax.random.fold_in(splits[21], 1), 0, ADAPTER_CHOICES - 1).astype(jnp.int32)
    return {"resid_in": resid_in, "out_grad": out_grad, "attn_gain": attn_gain, "q_weight": q_weight, "key_value_weight": key_value_weight, "o_weight": o_weight, "moe_gain": moe_gain, "router": router, "expert_in": expert_in, "expert_out": expert_out, "qkv_down": qkv_down, "q_up": q_up, "key_value_up_factor": key_value_up_factor, "o_down": o_down, "o_up": o_up, "expert_in_down": expert_in_down, "expert_in_up": expert_in_up, "expert_out_down": expert_out_down, "expert_out_up": expert_out_up, "expert_ids": expert_ids, "doc_starts": doc_starts, "doc_adapter": doc_adapter}


highest = lax.Precision.HIGHEST
norm_eps = 1e-06
masked_score = -1e+30

@jax.custom_vjp
def low(v):
    return lax.optimization_barrier(v.astype(jnp.bfloat16)).astype(jnp.float32)

@jax.custom_vjp
def low_back(v):
    return v

def low_keep(v):
    return (low(v), None)

def low_pass(kept, grad):
    return (grad,)

def back_keep(v):
    return (v, None)

def back_low(kept, grad):
    return (low(grad),)
low.defvjp(low_keep, low_pass)
low_back.defvjp(back_keep, back_low)

def matrix_product(left, right):
    return jnp.dot(left, right, precision=highest, preferred_element_type=jnp.float32)

def rms_scale(values, gain):
    return values * lax.rsqrt(lax.optimization_barrier(jnp.mean(values * values, axis=-1, keepdims=True)) + norm_eps) * gain

def rope_tables(in_doc, width):
    half_width = width // 2
    steps_index = jnp.arange(half_width, dtype=jnp.float32)
    freq_table = jnp.power(10000.0, -2.0 * steps_index / width)
    angles = in_doc.astype(jnp.float32)[:, None] * freq_table[None, :]
    cosine_table = jnp.cos(angles)
    sine_table = jnp.sin(angles)
    return (jnp.concatenate([cosine_table, cosine_table], axis=1), jnp.concatenate([sine_table, sine_table], axis=1))

def rotary_apply(values, cosine_table, sine_table):
    half_width = values.shape[-1] // 2
    turned = jnp.concatenate([-values[..., half_width:], values[..., :half_width]], axis=-1)
    return values * cosine_table[:, None, :] + turned * sine_table[:, None, :]

def doc_layout(positions, doc_starts, doc_adapter):
    opened = doc_starts[None, :] <= positions[:, None]
    own_start = lax.optimization_barrier(jnp.max(jnp.where(opened, doc_starts[None, :], 0), axis=1)).astype(jnp.int32)
    doc_index = lax.optimization_barrier(jnp.sum(opened.astype(jnp.int32), axis=1)).astype(jnp.int32) - 1
    picked = jnp.arange(doc_starts.shape[0], dtype=jnp.int32)[None, :] == doc_index[:, None]
    adapter = lax.optimization_barrier(jnp.sum(jnp.where(picked, doc_adapter[None, :], 0), axis=1)).astype(jnp.int32)
    return (doc_index, positions - own_start, adapter)

def attend(query_heads_rows, key_head_rows, value_head_rows, doc_index):
    query_block_index = min(512, STREAM_TOKENS)
    query_group_width = QUERY_HEADS // KEY_VALUE_HEADS
    positions_all = jnp.arange(STREAM_TOKENS, dtype=jnp.int32)

    def one_block(block_first_row):
        query_block_rows = lax.dynamic_slice_in_dim(query_heads_rows, block_first_row, query_block_index, 0).reshape(query_block_index, KEY_VALUE_HEADS, query_group_width, HEAD_WIDTH)
        query_spots = lax.dynamic_slice_in_dim(positions_all, block_first_row, query_block_index, 0)
        query_docs = lax.dynamic_slice_in_dim(doc_index, block_first_row, query_block_index, 0)
        scores = low_back(jnp.einsum('qkgd,nkd->kgqn', query_block_rows, key_head_rows, precision=highest) * 0.125)
        visible = (positions_all[None, :] <= query_spots[:, None]) & (doc_index[None, :] == query_docs[:, None])
        weights = low(jax.nn.softmax(jnp.where(visible, scores, masked_score), axis=-1))
        return jnp.einsum('kgqn,nkd->qkgd', weights, value_head_rows, precision=highest).reshape(query_block_index, QUERY_HEADS * HEAD_WIDTH)
    block_starts = jnp.arange(0, STREAM_TOKENS, query_block_index, dtype=jnp.int32)
    return lax.map(jax.checkpoint(one_block), block_starts).reshape(STREAM_TOKENS, QUERY_HEADS * HEAD_WIDTH)

def forward(adjusted, frozen, expert_ids, doc_index, mask_rank, in_doc):
    resid, qkv_down, q_up, key_value_up_factor, o_down, o_up, expert_in_down, expert_in_up, expert_out_down, expert_out_up = adjusted
    attn_gain, q_weight, key_value_weight, o_weight, moe_gain, router, expert_in, expert_out = frozen
    adapter_rank_span = ADAPTER_CHOICES * ADAPTER_RANK
    normed_input = low(rms_scale(resid, attn_gain))
    adapter_middles = low_back(low(matrix_product(normed_input, qkv_down) * jnp.tile(mask_rank, (1, 3))))
    q_linear = low_back(matrix_product(normed_input, q_weight) + matrix_product(adapter_middles[:, :adapter_rank_span], q_up))
    key_projected = low_back(matrix_product(normed_input, key_value_weight[0]) + matrix_product(adapter_middles[:, adapter_rank_span:2 * adapter_rank_span], key_value_up_factor[0]))
    value_head_rows = low_back(low(matrix_product(normed_input, key_value_weight[1]) + matrix_product(adapter_middles[:, 2 * adapter_rank_span:], key_value_up_factor[1]))).reshape(STREAM_TOKENS, KEY_VALUE_HEADS, HEAD_WIDTH)
    cosine_table, sine_table = rope_tables(in_doc, HEAD_WIDTH)
    query_heads_rows = low_back(low(rotary_apply(q_linear.reshape(STREAM_TOKENS, QUERY_HEADS, HEAD_WIDTH), cosine_table, sine_table)))
    key_head_rows = low_back(low(rotary_apply(key_projected.reshape(STREAM_TOKENS, KEY_VALUE_HEADS, HEAD_WIDTH), cosine_table, sine_table)))
    attended = low_back(low(attend(query_heads_rows, key_head_rows, value_head_rows, doc_index)))
    mid_attn = low_back(low(matrix_product(attended, o_down) * mask_rank))
    resid_mid = resid + low_back(matrix_product(attended, o_weight) + matrix_product(mid_attn, o_up))
    normed_moe = low(rms_scale(resid_mid, moe_gain))
    logits = low_back(matrix_product(normed_moe, router))
    chosen = jnp.take_along_axis(logits, expert_ids, axis=1)
    gate_probs = jax.nn.softmax(chosen, axis=-1)
    expert_range = jnp.arange(EXPERTS, dtype=jnp.int32)
    share_table = lax.optimization_barrier(jnp.sum(jnp.where(expert_ids[:, :, None] == expert_range[None, None, :], gate_probs[:, :, None], 0.0), axis=1))
    double_mask = jnp.concatenate([mask_rank, mask_rank], axis=1)

    def one_expert(running, stacked):
        weight_in, weight_out, in_down, in_up, out_down, out_up, share = stacked
        copies = low_back(normed_moe)
        mid_in = low_back(low(matrix_product(copies, in_down) * double_mask))
        lifted = jnp.concatenate([matrix_product(mid_in[:, :adapter_rank_span], in_up[0]), matrix_product(mid_in[:, adapter_rank_span:], in_up[1])], axis=1)
        joint = low_back(matrix_product(copies, weight_in) + lifted)
        hidden = low(jax.nn.silu(joint[:, :FF]) * joint[:, FF:])
        mid_out = low_back(low(matrix_product(hidden, out_down) * mask_rank))
        result = low_back(low(matrix_product(hidden, weight_out) + matrix_product(mid_out, out_up)))
        return (running + share[:, None] * result, None)
    mixed, unused_out = lax.scan(jax.checkpoint(one_expert), jnp.zeros_like(resid), (expert_in, expert_out, expert_in_down, expert_in_up, expert_out_down, expert_out_up, share_table.T))
    return resid_mid + mixed

def reference(resid_in, out_grad, attn_gain, q_weight, key_value_weight, o_weight, moe_gain, router, expert_in, expert_out, qkv_down, q_up, key_value_up_factor, o_down, o_up, expert_in_down, expert_in_up, expert_out_down, expert_out_up, expert_ids, doc_starts, doc_adapter):
    positions = jnp.arange(STREAM_TOKENS, dtype=jnp.int32)
    doc_index, in_doc, adapter = doc_layout(positions, doc_starts, doc_adapter)
    chosen_one = (adapter[:, None] == jnp.arange(ADAPTER_CHOICES, dtype=jnp.int32)[None, :]).astype(jnp.float32)
    mask_rank = jnp.repeat(chosen_one, ADAPTER_RANK, axis=1)
    frozen = tuple((member.astype(jnp.float32) for member in (attn_gain, q_weight, key_value_weight, o_weight, moe_gain, router, expert_in, expert_out)))
    adjusted = tuple((member.astype(jnp.float32) for member in (resid_in, qkv_down, q_up, key_value_up_factor, o_down, o_up, expert_in_down, expert_in_up, expert_out_down, expert_out_up)))

    def run_block(*adjusted_args):
        return forward(adjusted_args, frozen, expert_ids, doc_index, mask_rank, in_doc)
    result, pullback = jax.vjp(run_block, *adjusted)
    gradients = pullback(out_grad.astype(jnp.float32))
    return (result.astype(jnp.bfloat16), gradients[0].astype(jnp.bfloat16), gradients[1], gradients[2], gradients[3], gradients[4], gradients[5], gradients[6], gradients[7], gradients[8], gradients[9])
```

```python
import functools

import jax
import jax.numpy as jnp
from jax import lax
from jax.experimental import pallas as pl
from jax.experimental.pallas import tpu as pltpu
from jax.sharding import PartitionSpec as P

MESH = pl.DeviceIdType.MESH
VMEM = pl.BlockSpec(memory_space=pltpu.VMEM)
SMEM = pl.BlockSpec(memory_space=pltpu.SMEM)
HBM = pl.BlockSpec(memory_space=pl.ANY)
F32 = jnp.float32
BF16 = jnp.bfloat16

HEAD = 64
FF = 512
RANK = 16
SPAN = 32
EPS = 1e-06
LOW = -1e30
SCALE = 0.125

NN = (((1,), (0,)), ((), ()))
NT = (((1,), (1,)), ((), ()))
TN = (((0,), (0,)), ((), ()))


def dot(left, right, dims=NN):
    return lax.dot_general(left, right, dims, preferred_element_type=F32)


def iota(shape, dim):
    return lax.broadcasted_iota(jnp.int32, shape, dim)


def rms(values, gain):
    return values * lax.rsqrt(jnp.mean(values * values, axis=-1, keepdims=True) + EPS) * gain


def rms_back(values, gain, upstream):
    factor = lax.rsqrt(jnp.mean(values * values, axis=-1, keepdims=True) + EPS)
    scaled = upstream * gain
    return factor * scaled - values * factor * factor * factor * jnp.mean(
        scaled * values, axis=-1, keepdims=True
    )


def rotate(values, cosine, sine, sign):
    width = values.shape[1]
    copies = width // 128
    cosine = jnp.concatenate([cosine] * copies, axis=1)
    sine = jnp.concatenate([sine] * copies, axis=1)
    first = iota(values.shape, 1) % HEAD < HEAD // 2
    ahead = pltpu.roll(values, width - HEAD // 2, 1)
    behind = pltpu.roll(values, HEAD // 2, 1)
    return values * cosine + sign * jnp.where(first, -ahead, behind) * sine


def doc_scan(positions, starts_ref, adapters_ref):
    own_start = jnp.zeros(positions.shape, jnp.int32)
    adapter = jnp.zeros(positions.shape, jnp.int32)
    for number in range(starts_ref.shape[0]):
        opened = starts_ref[number] <= positions
        own_start = jnp.where(opened, starts_ref[number], own_start)
        adapter = jnp.where(opened, adapters_ref[number], adapter)
    return own_start, adapter


def place():
    me = lax.axis_index("ctx")
    ep = lax.axis_index("ep")
    return me, ep, me // 4, (me // 2) % 2, me % 2


def block_of(z, x, c):
    return (z * 2 + x) * 2 + c


def signal(device):
    pl.semaphore_signal(
        pltpu.get_barrier_semaphore(), inc=1, device_id=device, device_id_type=MESH
    )


def greet(planes, me, ep, z, x, c):
    signal({"ctx": me, "ep": 1 - ep})
    signal({"ctx": block_of(z, x, 1 - c), "ep": ep})
    signal({"ctx": block_of(z, 1 - x, c), "ep": ep})

    @pl.when(z > 0)
    def _():
        signal({"ctx": me - 4, "ep": ep})

    @pl.when(z < planes - 1)
    def _():
        signal({"ctx": me + 4, "ep": ep})

    count = 3 + jnp.where(z > 0, 1, 0) + jnp.where(z < planes - 1, 1, 0)
    pl.semaphore_wait(pltpu.get_barrier_semaphore(), count)


def remote(src, dst, send, recv, device):
    return pltpu.make_async_remote_copy(
        src_ref=src,
        dst_ref=dst,
        send_sem=send,
        recv_sem=recv,
        device_id=device,
        device_id_type=MESH,
    )


def rows_at(ref, start, count):
    return ref.at[pl.ds(pl.multiple_of(start, count), count)]


def pad_query(rows, target, lane_scale=None):
    count = rows.shape[0]
    upper = iota((count, 128), 1) >= HEAD
    for group in range(4):
        tile = rows[:, 128 * group : 128 * group + 128]
        turned = pltpu.roll(tile, HEAD, 1)
        keep = upper if group % 2 else jnp.logical_not(upper)
        low, high = (turned, tile) if group % 2 else (tile, turned)
        target[group, :count, :] = jnp.where(keep, low, 0.0).astype(BF16)
        target[group, count:, :] = jnp.where(keep, high, 0.0).astype(BF16)


def pad_query_t(columns, target):
    for group in range(4):
        both = jnp.concatenate(
            [
                columns[128 * group : 128 * group + 64],
                columns[128 * group + 64 : 128 * group + 128],
            ],
            axis=1,
        ).astype(BF16)
        blank = jnp.zeros(both.shape, BF16)
        own = HEAD * (group % 2)
        target[group, own : own + HEAD, :] = both
        target[group, HEAD - own : 2 * HEAD - own, :] = blank


def attend_kernel(
    planes,
    resid_ref, grad_ref, ids_ref, starts_ref, adapters_ref, attn_gain_ref, moe_gain_ref,
    q_w_ref, kv_w_ref, o_w_ref, qkv_down_ref, q_up_ref, kv_up_ref, o_down_ref, o_up_ref, router_ref,
    cos_ref, sin_ref,
    x_all, g_all, gates_ref, x2_ref, h2_ref, query_ref, kvall, mids_ref, lse_ref, att_ref, mid_o_ref, mask_ref,
    hot_all, ow_all, od_all, att_all, qt, m_s, l_s, acc,
    pair_send, pair_recv, ring_send, ring_recv,
):
    me, ep, z, x, c = place()
    pair = {"ctx": me, "ep": 1 - ep}
    up = {"ctx": jnp.minimum(me + 4, 4 * planes - 1), "ep": ep}
    across = {"ctx": block_of(z, 1 - x, c), "ep": ep}
    beside = {"ctx": block_of(z, x, 1 - c), "ep": ep}
    rows = resid_ref.shape[0]
    block = 2 * rows
    mine = ep * rows
    theirs = rows - mine
    greet(planes, me, ep, z, x, c)

    def swap(number, src, dst):
        return remote(src, dst, pair_send.at[number], pair_recv.at[number], pair)

    send_x = swap(0, resid_ref, rows_at(x_all, mine, rows))
    send_x.start()

    hot = jnp.zeros((rows, 128), F32)
    lanes = iota((rows, 128), 1)
    for choice in range(ids_ref.shape[1]):
        hot = hot + jnp.where(ids_ref[:, choice : choice + 1] == lanes, 1.0, 0.0)
    hot_all[pl.ds(pl.multiple_of(mine, rows), rows), :] = hot.astype(BF16)
    x_all[pl.ds(pl.multiple_of(mine, rows), rows), :] = resid_ref[...]
    g_all[pl.ds(pl.multiple_of(mine, rows), rows), :] = grad_ref[...]
    ow_all[ep] = o_w_ref[...]
    od_all[ep] = o_down_ref[...]

    position = me * block + iota((block, 128), 0)
    unused, adapter = doc_scan(position, starts_ref, adapters_ref)
    mask_ref[...] = jnp.where((iota((block, 128), 1) % SPAN) // RANK == adapter, 1.0, 0.0)
    row_pos = me * block + iota((8, 2 * block), 1) % block
    row_start, unused = doc_scan(row_pos, starts_ref, adapters_ref)

    def project(start):
        here = pl.ds(pl.multiple_of(start, rows), rows)
        h1 = rms(x_all[here, :].astype(F32), attn_gain_ref[...]).astype(BF16)
        mids = (dot(h1, qkv_down_ref[...]) * mask_ref[here, :96]).astype(BF16)
        mids_ref[here, :] = mids
        cosine, sine = cos_ref[here, :], sin_ref[here, :]
        q_lin = dot(h1, q_w_ref[...]) + dot(mids[:, :SPAN], q_up_ref[...])
        query_ref[here, :] = rotate(q_lin, cosine, sine, 1.0).astype(BF16)
        k_lin = dot(h1, kv_w_ref[0]) + dot(mids[:, SPAN : 2 * SPAN], kv_up_ref[0])
        kvall[me, 0, here, :] = rotate(k_lin, cosine, sine, 1.0).astype(BF16)
        kvall[me, 1, here, :] = (
            dot(h1, kv_w_ref[1]) + dot(mids[:, 2 * SPAN :], kv_up_ref[1])
        ).astype(BF16)

    project(mine)
    send_x.wait_recv()
    send_hot = swap(1, rows_at(hot_all, mine, rows), rows_at(hot_all, mine, rows))
    send_g = swap(2, grad_ref, rows_at(g_all, mine, rows))
    send_ow = swap(3, o_w_ref, ow_all.at[ep])
    send_od = swap(4, o_down_ref, od_all.at[ep])
    for copy in (send_hot, send_od, send_g, send_ow):
        copy.start()
    project(theirs)

    def ring(number, way, target):
        return remote(
            kvall.at[number], kvall.at[number], ring_send.at[way, number], ring_recv.at[number], target
        )

    def forward_own(p):
        number = block_of(p, x, c)

        @pl.when(z < planes - 1)
        def _():
            ring(number, 0, up).start()

        ring(number, 1, across).start()
        ring(number, 2, beside).start()

    def forward_across(p):
        number = block_of(p, 1 - x, c)
        ring(number, 1, across).wait_recv()
        ring(number, 2, beside).start()

    def arrive_beside(p):
        for column in (0, 1):
            ring(block_of(p, column, 1 - c), 2, beside).wait_recv()

    forward_own(z)
    pad_query_t((query_ref[...].astype(F32) * SCALE).T, qt)
    m_s[...] = jnp.full(m_s.shape, LOW, F32)
    l_s[...] = jnp.zeros(l_s.shape, F32)
    acc[...] = jnp.zeros(acc.shape, F32)
    forward_across(z)
    arrive_beside(z)

    start_row = row_start[:1]
    pos_row = row_pos[:1]

    def head_step(p, group, masked):
        tile = slice(128 * (group // 2), 128 * (group // 2) + 128)
        scores = []
        for b in range(4):
            s = dot(kvall[4 * p + b, 0, :, tile], qt[group])
            if masked:
                key = (4 * p + b) * block + iota(s.shape, 0)
                s = jnp.where((key <= pos_row) & (key >= start_row), s, LOW)
            scores.append(s)
        peak = functools.reduce(
            jnp.maximum, [jnp.max(s, axis=0, keepdims=True) for s in scores]
        )
        if not masked:
            sees = start_row <= 4 * p * block
            peak = jnp.where(sees, peak, LOW)
        old = m_s[group]
        new = jnp.maximum(old, peak)
        m_s[group] = new
        base = new if masked else jnp.where(sees, new, -LOW)
        decay = jnp.exp(old - new)
        total = l_s[group] * decay
        grown = acc[group] * decay
        for b in range(4):
            w = jnp.exp(scores[b] - base)
            total = total + jnp.sum(w, axis=0, keepdims=True)
            added = dot(kvall[4 * p + b, 1, :, tile], w.astype(BF16), TN)
            grown = grown + added[HEAD * (group % 2) : HEAD * (group % 2) + HEAD]
        l_s[group] = total
        acc[group] = grown

    def plane_step(turn, carry):
        p = z - turn
        edge = (turn == 0) | (p == 0)

        def heads(group):
            @pl.when(edge)
            def _():
                head_step(p, group, True)

            @pl.when(jnp.logical_not(edge))
            def _():
                head_step(p, group, False)

        heads(0)

        @pl.when(p > 0)
        def _():
            number = block_of(p - 1, x, c)
            ring(number, 0, up).wait_recv()
            forward_own(p - 1)

        heads(1)
        heads(2)

        @pl.when(p > 0)
        def _():
            forward_across(p - 1)

        heads(3)

        @pl.when(p > 0)
        def _():
            arrive_beside(p - 1)

        return carry

    lax.fori_loop(0, z + 1, plane_step, 0)

    columns = []
    for group in range(4):
        lse_ref[group] = m_s[group] + jnp.log(l_s[group])
        done = acc[group] / l_s[group]
        columns += [done[:, :block], done[:, block:]]
    attended = jnp.concatenate(columns, axis=0).T
    att_ref[...] = attended
    att_all[ep] = attended.astype(BF16)
    send_att = swap(5, att_all.at[ep], att_all.at[ep])
    send_att.start()
    for copy in (send_hot, send_od, send_g, send_ow):
        copy.wait_recv()
    send_att.wait_recv()
    left, right = att_all[0], att_all[1]
    mid_o = ((dot(left, od_all[0]) + dot(right, od_all[1])) * mask_ref[:, :SPAN]).astype(BF16)
    mid_o_ref[...] = mid_o
    x2 = (
        x_all[...].astype(F32)
        + (dot(left, ow_all[0]) + dot(right, ow_all[1]))
        + dot(mid_o, o_up_ref[...])
    )
    x2_ref[...] = x2
    h2 = rms(x2, moe_gain_ref[...]).astype(BF16)
    h2_ref[...] = h2
    logits = dot(h2, router_ref[...])
    chosen = hot_all[:, : logits.shape[1]].astype(F32) > 0.5
    logits = jnp.where(chosen, logits, LOW)
    grown = jnp.where(chosen, jnp.exp(logits - jnp.max(logits, axis=1, keepdims=True)), 0.0)
    gates_ref[...] = grown / jnp.sum(grown, axis=1, keepdims=True)

    for copy in (send_x, send_hot, send_g, send_ow, send_od, send_att):
        copy.wait_send()

    def drain(p, carry):
        @pl.when(z < planes - 1)
        def _():
            ring(block_of(p, x, c), 0, up).wait_send()

        ring(block_of(p, x, c), 1, across).wait_send()
        ring(block_of(p, x, c), 2, beside).wait_send()
        ring(block_of(p, 1 - x, c), 2, beside).wait_send()
        return carry

    lax.fori_loop(0, z + 1, drain, 0)


def expert_kernel(
    h2_ref, g_all, gates_ref, x2_ref, mask_ref, mid_o_ref, moe_gain_ref, router_ref, o_up_ref,
    in_hbm, out_hbm, in_down_hbm, in_up_hbm, out_down_hbm, out_up_hbm,
    block_out_ref, d_x2_ref, d_attn_ref, d_mid_o_ref, grads_ref, grad_o_up_ref,
    w_in, w_out, w_in_down, w_in_up, w_out_down, w_out_up, acc_out, acc_h2, dgates, trade, out_trade, dg_trade,
    load_sem, pair_send, pair_recv,
):
    me, ep, z, x, c = place()
    pair = {"ctx": me, "ep": 1 - ep}
    experts = in_hbm.shape[0]
    block = h2_ref.shape[0]
    rows = block // 2
    mine = ep * rows
    theirs = rows - mine
    halves = (
        (in_hbm, w_in), (out_hbm, w_out), (in_down_hbm, w_in_down),
        (in_up_hbm, w_in_up), (out_down_hbm, w_out_down), (out_up_hbm, w_out_up),
    )

    def loads(e):
        return [
            pltpu.make_async_copy(source.at[e], held.at[e], load_sem.at[e, number])
            for number, (source, held) in enumerate(halves)
        ]

    def begin(e, carry):
        for copy in loads(e):
            copy.start()
        return carry

    lax.fori_loop(0, experts, begin, 0)
    signal(pair)
    acc_out[...] = jnp.zeros(acc_out.shape, F32)
    acc_h2[...] = jnp.zeros(acc_h2.shape, F32)
    dgates[...] = jnp.zeros(dgates.shape, F32)
    pl.semaphore_wait(pltpu.get_barrier_semaphore(), 1)
    gates = gates_ref[...]
    own_gates = jnp.where(ep == 0, gates[:, :experts], gates[:, experts:])
    lanes = iota((block, experts), 1)

    def one(e, carry):
        for copy in loads(e):
            copy.wait()
        h2, g = h2_ref[...], g_all[...]
        mask = mask_ref[...]
        gate = jnp.sum(jnp.where(lanes == e, own_gates, 0.0), axis=1, keepdims=True)
        mid_in = (dot(h2, w_in_down[e]) * mask[:, : 2 * SPAN]).astype(BF16)
        gate_part = dot(h2, w_in[e, :, :FF]) + dot(mid_in[:, :SPAN], w_in_up[e, 0])
        up_part = dot(h2, w_in[e, :, FF:]) + dot(mid_in[:, SPAN:], w_in_up[e, 1])
        squash = 1.0 / (1.0 + jnp.exp(-gate_part))
        silu = gate_part * squash
        act_full = silu * up_part
        act = act_full.astype(BF16)
        mid_out = dot(act, w_out_down[e]) * mask[:, :SPAN]
        lifted = (dot(g, w_out_up[e], NT) * mask[:, :SPAN]).astype(BF16)
        d_act = dot(g, w_out[e], NT) + dot(lifted, w_out_down[e], NT)
        d_gate = jnp.sum(act.astype(F32) * d_act, axis=1, keepdims=True)
        dgates[...] += jnp.where(iota(dgates.shape, 1) == e, d_gate, 0.0)
        d_act = d_act * gate
        d_up = (d_act * silu).astype(BF16)
        d_gp = (d_act * up_part * squash * (1.0 + gate_part * (1.0 - squash))).astype(BF16)
        d_mid_in = (
            jnp.concatenate([dot(d_gp, w_in_up[e, 0], NT), dot(d_up, w_in_up[e, 1], NT)], axis=1)
            * mask[:, : 2 * SPAN]
        ).astype(BF16)
        scaled_mid = (mid_out * gate).astype(BF16)
        acc_out[...] += dot((act.astype(F32) * gate).astype(BF16), w_out[e]) + dot(scaled_mid, w_out_up[e])
        acc_h2[...] += (
            dot(d_gp, w_in[e, :, :FF], NT) + dot(d_up, w_in[e, :, FF:], NT) + dot(d_mid_in, w_in_down[e], NT)
        )
        grads_ref[e, 0:64, :] = dot(d_mid_in, h2, TN).astype(BF16)
        grads_ref[e, 64:96, :FF] = dot(mid_in[:, :SPAN], d_gp, TN).astype(BF16)
        grads_ref[e, 64:96, FF:] = dot(mid_in[:, SPAN:], d_up, TN).astype(BF16)
        down = dot((lifted.astype(F32) * gate).astype(BF16), act, TN).astype(BF16)
        grads_ref[e, 96:112, :FF] = down[:16]
        grads_ref[e, 96:112, FF:] = down[16:]
        grads_ref[e, 112:144, :] = dot(scaled_mid, g, TN).astype(BF16)
        return carry

    lax.fori_loop(0, experts, one, 0)

    def swap(number, src, dst):
        return remote(src, dst, pair_send.at[number], pair_recv.at[number], pair)

    dg_trade[ep] = dgates[...].T[:8]
    send_dg = swap(0, dg_trade.at[ep], dg_trade.at[ep])
    send_dg.start()
    trade[ep] = acc_h2[...].astype(BF16)
    send_h2 = swap(1, trade.at[ep], trade.at[ep])
    send_h2.start()
    out_trade[0] = acc_out[pl.ds(pl.multiple_of(theirs, rows), rows), :].astype(BF16)
    send_out = swap(2, out_trade.at[0], out_trade.at[1])
    send_out.start()
    send_dg.wait_recv()
    table = jnp.concatenate([dg_trade[0], dg_trade[1], jnp.zeros((112, block), F32)], axis=0).T
    d_gates = table[:, : 2 * experts]
    d_logits = (gates * (d_gates - jnp.sum(gates * d_gates, axis=1, keepdims=True))).astype(BF16)
    from_router = dot(d_logits, router_ref[...], NT)
    send_h2.wait_recv()
    d_h2 = trade[0].astype(F32) + trade[1].astype(F32) + from_router
    d_x2 = g_all[...].astype(F32) + rms_back(x2_ref[...], moe_gain_ref[...], d_h2)
    d_attn = d_x2.astype(BF16)
    d_attn_ref[...] = d_attn
    d_x2_ref[...] = d_x2
    d_mid_o = (dot(d_attn, o_up_ref[...], NT) * mask_ref[:, :SPAN]).astype(BF16)
    d_mid_o_ref[...] = d_mid_o
    grad_o_up_ref[...] = dot(mid_o_ref[...], d_attn, TN)
    send_out.wait_recv()
    here = pl.ds(pl.multiple_of(mine, rows), rows)
    block_out_ref[...] = (x2_ref[here, :] + (acc_out[here, :] + out_trade[1].astype(F32))).astype(BF16)
    for copy in (send_dg, send_h2, send_out):
        copy.wait_send()


def back_kernel(
    planes,
    x_all, query_ref, kv_hbm, mids_ref, lse_ref, att_ref, d_attn_ref, d_mid_o_ref, d_x2_ref, mask_ref,
    starts_ref, adapters_ref, attn_gain_ref,
    q_w_ref, kv_w_ref, o_w_ref, qkv_down_ref, q_up_ref, kv_up_ref, o_down_ref, cos_ref, sin_ref,
    in_grad_ref, grad_down_ref, grad_q_up_ref, grad_kv_up_ref, grad_o_down_ref,
    kvall, qt, qn, dt, dn, dqt, delta, from_beside, from_across, from_up, to_across, to_down, trade, mid_trade,
    kv_sem, pair_send, pair_recv, beside_send, beside_recv, across_send, across_recv, down_send, down_recv,
):
    me, ep, z, x, c = place()
    pair = {"ctx": me, "ep": 1 - ep}
    down = {"ctx": jnp.maximum(me - 4, 0), "ep": ep}
    across = {"ctx": block_of(z, 1 - x, c), "ep": ep}
    beside = {"ctx": block_of(z, x, 1 - c), "ep": ep}
    block = x_all.shape[0]
    rows = block // 2
    mine = ep * rows
    theirs = rows - mine
    load = pltpu.make_async_copy(kv_hbm, kvall, kv_sem)
    load.start()
    greet(planes, me, ep, z, x, c)

    pad_query(query_ref[...].astype(F32), qn)
    pad_query_t((query_ref[...].astype(F32) * SCALE).T, qt)
    d_att = (
        dot(d_attn_ref[...], o_w_ref[...], NT) + dot(d_mid_o_ref[...], o_down_ref[...], NT)
    ).astype(BF16)
    d_att_full = d_att.astype(F32)
    pad_query(d_att_full, dn)
    pad_query_t(d_att_full.T, dt)
    product = (d_att_full * att_ref[...]).T
    for group in range(4):
        for half in (0, 1):
            start = 128 * group + 64 * half
            delta[group, :, half * block : half * block + block] = jnp.sum(
                product[start : start + 64], axis=0, keepdims=True
            )
    grad_o_down_ref[...] = dot(d_mid_o_ref[...], att_ref[...].astype(BF16), TN)
    dqt[...] = jnp.zeros(dqt.shape, F32)
    row_pos = me * block + iota((8, 2 * block), 1) % block
    row_start, unused = doc_scan(row_pos, starts_ref, adapters_ref)
    start_row, pos_row = row_start[:1], row_pos[:1]
    load.wait()

    def block_step(number, masked):
        new_k, new_v = [], []
        for group in range(4):
            tile = slice(128 * (group // 2), 128 * (group // 2) + 128)
            keys = kvall[number, 0, :, tile]
            s = dot(keys, qt[group])
            base = lse_ref[group]
            if masked:
                key = number * block + iota(s.shape, 0)
                w = jnp.where((key <= pos_row) & (key >= start_row), jnp.exp(s - base), 0.0)
            else:
                w = jnp.exp(s - jnp.where(start_row <= number * block, base, -LOW))
            d_w = dot(kvall[number, 1, :, tile], dt[group])
            d_s = (w * (d_w - delta[group])).astype(BF16)
            new_k.append(dot(d_s, qn[group]))
            new_v.append(dot(w.astype(BF16), dn[group]))
            dqt[group] += dot(keys, d_s, TN)[HEAD * (group % 2) : HEAD * (group % 2) + HEAD]
        for half in (0, 1):
            tile = slice(128 * half, 128 * half + 128)
            kvall[number, 0, :, tile] = ((new_k[2 * half] + new_k[2 * half + 1]) * SCALE).astype(BF16)
            kvall[number, 1, :, tile] = (new_v[2 * half] + new_v[2 * half + 1]).astype(BF16)

    def compute(number):
        edge = (number == 0) | (number == me)

        @pl.when(edge)
        def _():
            block_step(number, True)

        @pl.when((number < me) & jnp.logical_not(edge))
        def _():
            block_step(number, False)

        @pl.when(number > me)
        def _():
            kvall[number] = jnp.zeros(kvall.shape[1:], BF16)

    def to_beside(p, column):
        return remote(
            kvall.at[block_of(p, column, 1 - c)], from_beside.at[p, column],
            beside_send.at[p, column], beside_recv.at[p, column], beside,
        )

    def over(p):
        return remote(to_across.at[p], from_across.at[p], across_send.at[p], across_recv.at[p], across)

    def lower(p):
        return remote(to_down.at[p], from_up.at[p], down_send.at[p], down_recv.at[p], down)

    def finish(p):
        over(p).wait_recv()
        total = (
            kvall[block_of(p, x, c)].astype(F32)
            + from_beside[p, x].astype(F32)
            + from_across[p].astype(F32)
        )
        to_down[p] = total.astype(BF16)

        @pl.when(z < planes - 1)
        def _():
            lower(p).wait_recv()
            to_down[p] = (total + from_up[p].astype(F32)).astype(BF16)

        @pl.when(p < z)
        def _():
            lower(p).start()

    def plane_step(p, carry):
        compute(block_of(p, 1 - x, 1 - c))
        to_beside(p, 1 - x).start()
        compute(block_of(p, x, 1 - c))
        to_beside(p, x).start()

        @pl.when(p > 0)
        def _():
            finish(p - 1)

        compute(block_of(p, 1 - x, c))
        to_beside(p, 1 - x).wait_recv()
        to_across[p] = (
            kvall[block_of(p, 1 - x, c)].astype(F32) + from_beside[p, 1 - x].astype(F32)
        ).astype(BF16)
        over(p).start()
        compute(block_of(p, x, c))
        to_beside(p, x).wait_recv()
        return carry

    lax.fori_loop(0, z + 1, plane_step, 0)
    finish(z)
    d_key = to_down[z, 0].astype(F32)
    d_value = to_down[z, 1]

    cosine, sine = cos_ref[...], sin_ref[...]
    parts = []
    for group in range(4):
        both = dqt[group]
        parts += [both[:, :block], both[:, block:]]
    d_query = jnp.concatenate(parts, axis=0).T * SCALE
    d_q = rotate(d_query.astype(BF16).astype(F32), cosine, sine, -1.0).astype(BF16)
    d_k = rotate(d_key, cosine, sine, -1.0).astype(BF16)
    mids_part = jnp.concatenate(
        [dot(d_q, q_up_ref[...], NT), dot(d_k, kv_up_ref[0], NT), dot(d_value, kv_up_ref[1], NT)], axis=1
    )

    def swap(number, src, dst):
        return remote(src, dst, pair_send.at[number], pair_recv.at[number], pair)

    mid_trade[ep] = mids_part.astype(BF16)
    send_mid = swap(0, mid_trade.at[ep], mid_trade.at[ep])
    send_mid.start()

    def norm_part(start):
        here = pl.ds(pl.multiple_of(start, rows), rows)
        return here

    here, there = norm_part(mine), norm_part(theirs)
    full = dot(d_q, q_w_ref[...], NT) + dot(d_k, kv_w_ref[0], NT) + dot(d_value, kv_w_ref[1], NT)
    first, second = full[:rows], full[rows:]
    trade[0] = jnp.where(ep == 0, second, first).astype(BF16)
    send_norm = swap(1, trade.at[0], trade.at[1])
    send_norm.start()
    grad_q_up_ref[...] = dot(mids_ref[:, :SPAN], d_q, TN)
    grad_kv_up_ref[0] = dot(mids_ref[:, SPAN : 2 * SPAN], d_k, TN)
    grad_kv_up_ref[1] = dot(mids_ref[:, 2 * SPAN :], d_value, TN)
    h1 = rms(x_all[...].astype(F32), attn_gain_ref[...]).astype(BF16)
    send_mid.wait_recv()
    d_mids = (
        (mid_trade[0].astype(F32) + mid_trade[1].astype(F32)) * mask_ref[:, : 3 * SPAN]
    ).astype(BF16)
    grad_down_ref[...] = dot(d_mids, h1, TN)
    from_mids = dot(d_mids, qkv_down_ref[...], NT)
    own = jnp.where(ep == 0, first + from_mids[:rows], second + from_mids[rows:])
    send_norm.wait_recv()
    own = own + trade[1].astype(F32)
    in_grad_ref[...] = (
        d_x2_ref[here, :] + rms_back(x_all[here, :].astype(F32), attn_gain_ref[...], own)
    ).astype(BF16)
    send_mid.wait_send()
    send_norm.wait_send()

    def drain(p, carry):
        to_beside(p, 0).wait_send()
        to_beside(p, 1).wait_send()
        over(p).wait_send()

        @pl.when(p < z)
        def _():
            lower(p).wait_send()

        return carry

    lax.fori_loop(0, z + 1, drain, 0)


def per_device(
    resid_in, out_grad, attn_gain, q_weight, key_value_weight, o_weight, moe_gain, router, expert_in,
    expert_out, qkv_down, q_up, key_value_up_factor, o_down, o_up, expert_in_down, expert_in_up,
    expert_out_down, expert_out_up, expert_ids, doc_starts, doc_adapter,
):
    blocks = lax.axis_size("ctx")
    planes = blocks // 4
    rows, width = resid_in.shape
    block = 2 * rows
    me, ep = lax.axis_index("ctx"), lax.axis_index("ep")
    positions = me * block + jnp.arange(block, dtype=jnp.int32)
    opened = doc_starts[None, :] <= positions[:, None]
    in_doc = positions - jnp.max(jnp.where(opened, doc_starts[None, :], 0), axis=1)
    steps = jnp.arange(HEAD // 2, dtype=F32)
    angles = in_doc.astype(F32)[:, None] * jnp.power(10000.0, -2.0 * steps / HEAD)[None, :]
    cosine, sine = jnp.tile(jnp.cos(angles), (1, 4)), jnp.tile(jnp.sin(angles), (1, 4))
    attn_gain, moe_gain = attn_gain[None, :], moe_gain[None, :]
    heads = q_weight.shape[1]
    kv = key_value_weight.shape[2]
    experts = expert_in.shape[0]

    def shape(dims, kind=F32):
        return jax.ShapeDtypeStruct(dims, kind)

    def dma(*dims):
        return pltpu.SemaphoreType.DMA(dims)

    x_all, g_all, gates, x2, h2, query, kvall, mids, lse, att, mid_o, mask = pl.pallas_call(
        functools.partial(attend_kernel, planes),
        out_shape=[
            shape((block, width), BF16), shape((block, width), BF16), shape((block, 2 * experts)),
            shape((block, width)), shape((block, width), BF16), shape((block, heads), BF16),
            shape((blocks, 2, block, kv), BF16), shape((block, 3 * SPAN), BF16), shape((4, 1, 2 * block)),
            shape((block, heads)), shape((block, SPAN), BF16), shape((block, 128)),
        ],
        in_specs=[VMEM] * 3 + [SMEM] * 2 + [VMEM] * 13,
        out_specs=[VMEM] * 12,
        scratch_shapes=[
            pltpu.VMEM((block, 128), BF16), pltpu.VMEM((2, heads, width), BF16),
            pltpu.VMEM((2, heads, SPAN), BF16), pltpu.VMEM((2, block, heads), BF16),
            pltpu.VMEM((4, 128, 2 * block), BF16), pltpu.VMEM((4, 1, 2 * block), F32),
            pltpu.VMEM((4, 1, 2 * block), F32), pltpu.VMEM((4, HEAD, 2 * block), F32),
            dma(6), dma(6), dma(3, blocks), dma(blocks),
        ],
        compiler_params=pltpu.CompilerParams(
            collective_id=1, has_side_effects=True, vmem_limit_bytes=60 << 20
        ),
        name="attend",
    )(
        resid_in, out_grad, expert_ids, doc_starts, doc_adapter, attn_gain, moe_gain, q_weight,
        key_value_weight, o_weight, qkv_down, q_up, key_value_up_factor, o_down, o_up, router, cosine, sine,
    )

    block_out, d_x2, d_attn, d_mid_o, grads, grad_o_up = pl.pallas_call(
        expert_kernel,
        out_shape=[
            shape((rows, width), BF16), shape((block, width)), shape((block, width), BF16),
            shape((block, SPAN), BF16), shape((experts, 144, width), BF16), shape((SPAN, width)),
        ],
        in_specs=[VMEM] * 9 + [HBM] * 6,
        out_specs=[VMEM] * 6,
        scratch_shapes=[
            pltpu.VMEM(expert_in.shape, BF16), pltpu.VMEM(expert_out.shape, BF16),
            pltpu.VMEM(expert_in_down.shape, BF16), pltpu.VMEM(expert_in_up.shape, BF16),
            pltpu.VMEM(expert_out_down.shape, BF16), pltpu.VMEM(expert_out_up.shape, BF16),
            pltpu.VMEM((block, width), F32), pltpu.VMEM((block, width), F32), pltpu.VMEM((block, 128), F32),
            pltpu.VMEM((2, block, width), BF16), pltpu.VMEM((2, rows, width), BF16),
            pltpu.VMEM((2, 8, block), F32), dma(experts, 6), dma(3), dma(3),
        ],
        compiler_params=pltpu.CompilerParams(
            collective_id=2, has_side_effects=True, vmem_limit_bytes=60 << 20
        ),
        name="experts",
    )(
        h2, g_all, gates, x2, mask, mid_o, moe_gain, router, o_up, expert_in, expert_out,
        expert_in_down, expert_in_up, expert_out_down, expert_out_up,
    )

    in_grad, grad_down, grad_q_up, grad_kv_up, grad_o_down = pl.pallas_call(
        functools.partial(back_kernel, planes),
        out_shape=[
            shape((rows, width), BF16), shape((3 * SPAN, width)), shape((SPAN, heads)),
            shape((2, SPAN, kv)), shape((SPAN, heads)),
        ],
        in_specs=[VMEM] * 2 + [HBM] + [VMEM] * 7 + [SMEM] * 2 + [VMEM] * 10,
        out_specs=[VMEM] * 5,
        scratch_shapes=[
            pltpu.VMEM((blocks, 2, block, kv), BF16), pltpu.VMEM((4, 128, 2 * block), BF16),
            pltpu.VMEM((4, 2 * block, 128), BF16), pltpu.VMEM((4, 128, 2 * block), BF16),
            pltpu.VMEM((4, 2 * block, 128), BF16), pltpu.VMEM((4, HEAD, 2 * block), F32),
            pltpu.VMEM((4, 1, 2 * block), F32), pltpu.VMEM((planes, 2, 2, block, kv), BF16),
            pltpu.VMEM((planes, 2, block, kv), BF16), pltpu.VMEM((planes, 2, block, kv), BF16),
            pltpu.VMEM((planes, 2, block, kv), BF16), pltpu.VMEM((planes, 2, block, kv), BF16),
            pltpu.VMEM((2, rows, width), BF16), pltpu.VMEM((2, block, 3 * SPAN), BF16),
            pltpu.SemaphoreType.DMA, dma(2), dma(2), dma(planes, 2), dma(planes, 2),
            dma(planes), dma(planes), dma(planes), dma(planes),
        ],
        compiler_params=pltpu.CompilerParams(
            collective_id=3, has_side_effects=True, vmem_limit_bytes=60 << 20
        ),
        name="back",
    )(
        x_all, query, kvall, mids, lse, att, d_attn, d_mid_o, d_x2, mask, doc_starts, doc_adapter,
        attn_gain, q_weight, key_value_weight, o_weight, qkv_down, q_up, key_value_up_factor, o_down,
        cosine, sine,
    )

    grads, grad_q_up, grad_kv_up, grad_o_down = lax.psum((grads, grad_q_up, grad_kv_up, grad_o_down), "ctx")
    grad_o_up, grad_down = lax.psum(
        (jnp.where(ep == 0, grad_o_up, 0.0), jnp.where(ep == 0, grad_down, 0.0)), ("ctx", "ep")
    )
    grads = grads.astype(F32)
    ein_down = jnp.swapaxes(grads[:, :64], 1, 2)
    ein_up = jnp.stack([grads[:, 64:96, :FF], grads[:, 64:96, FF:]], axis=1)
    eout_down = jnp.swapaxes(
        jnp.concatenate([grads[:, 96:112, :FF], grads[:, 96:112, FF:]], axis=1), 1, 2
    )
    eout_up = grads[:, 112:144]
    return (
        block_out, in_grad, grad_down.T, grad_q_up, grad_kv_up, grad_o_down.T, grad_o_up,
        ein_down, ein_up, eout_down, eout_up,
    )


def solution(mesh):
    placed = (
        P(("ctx", "ep"), None),
        P(("ctx", "ep"), None),
        P(),
        P(None, "ep"),
        P(None, None, "ep"),
        P("ep", None),
        P(),
        P(),
        P("ep", None, None),
        P("ep", None, None),
        P(),
        P(None, "ep"),
        P(None, None, "ep"),
        P("ep", None),
        P(),
        P("ep", None, None),
        P("ep", None, None, None),
        P("ep", None, None),
        P("ep", None, None),
        P(("ctx", "ep"), None),
        P(),
        P(),
    )
    return jax.shard_map(
        per_device,
        mesh=mesh,
        in_specs=placed,
        out_specs=(
            P(("ctx", "ep"), None),
            P(("ctx", "ep"), None),
            P(),
            P(None, "ep"),
            P(None, None, "ep"),
            P("ep", None),
            P(),
            P("ep", None, None),
            P("ep", None, None, None),
            P("ep", None, None),
            P("ep", None, None),
        ),
        check_vma=False,
    )
```

```python
import functools

import jax
import jax.numpy as jnp
import numpy as np
from jax import lax
from jax.experimental import pallas as pl
from jax.experimental.pallas import tpu as pltpu
from jax.sharding import PartitionSpec as P

MESH = pl.DeviceIdType.MESH
VMEM = pl.BlockSpec(memory_space=pltpu.VMEM)
SMEM = pl.BlockSpec(memory_space=pltpu.SMEM)
HBM = pl.BlockSpec(memory_space=pl.ANY)
F32 = jnp.float32
BF16 = jnp.bfloat16

HEAD = 64
FF = 512
RANK = 16
SPAN = 32
EPS = 1e-06
LOW = -1e30
SCALE = 0.125

NN = (((1,), (0,)), ((), ()))
NT = (((1,), (1,)), ((), ()))
TN = (((0,), (0,)), ((), ()))


def dot(left, right, dims=NN):
    return lax.dot_general(left, right, dims, preferred_element_type=F32)


def iota(shape, dim):
    return lax.broadcasted_iota(jnp.int32, shape, dim)


def rms(values, gain):
    return values * lax.rsqrt(jnp.mean(values * values, axis=-1, keepdims=True) + EPS) * gain


def rms_back(values, gain, upstream):
    factor = lax.rsqrt(jnp.mean(values * values, axis=-1, keepdims=True) + EPS)
    scaled = upstream * gain
    return factor * scaled - values * factor * factor * factor * jnp.mean(
        scaled * values, axis=-1, keepdims=True
    )


def rotate(values, cosine, sine, sign):
    width = values.shape[1]
    copies = width // 128
    cosine = jnp.concatenate([cosine] * copies, axis=1)
    sine = jnp.concatenate([sine] * copies, axis=1)
    first = iota(values.shape, 1) % HEAD < HEAD // 2
    ahead = pltpu.roll(values, width - HEAD // 2, 1)
    behind = pltpu.roll(values, HEAD // 2, 1)
    return values * cosine + sign * jnp.where(first, -ahead, behind) * sine


def doc_scan(positions, starts_ref, adapters_ref):
    own_start = jnp.zeros(positions.shape, jnp.int32)
    adapter = jnp.zeros(positions.shape, jnp.int32)
    for number in range(starts_ref.shape[0]):
        opened = starts_ref[number] <= positions
        own_start = jnp.where(opened, starts_ref[number], own_start)
        adapter = jnp.where(opened, adapters_ref[number], adapter)
    return own_start, adapter


def place():
    me = lax.axis_index("ctx")
    ep = lax.axis_index("ep")
    return me, ep, me // 4, (me // 2) % 2, me % 2


def block_of(z, x, c):
    return (z * 2 + x) * 2 + c


def signal(device):
    pl.semaphore_signal(
        pltpu.get_barrier_semaphore(), inc=1, device_id=device, device_id_type=MESH
    )


def remote(src, dst, send, recv, device):
    return pltpu.make_async_remote_copy(
        src_ref=src,
        dst_ref=dst,
        send_sem=send,
        recv_sem=recv,
        device_id=device,
        device_id_type=MESH,
    )


def span(start, count):
    return pl.ds(pl.multiple_of(start, count), count)


def pad_query(rows, target):
    count = rows.shape[0]
    upper = iota((count, 128), 1) >= HEAD
    for group in range(4):
        tile = rows[:, 128 * group : 128 * group + 128]
        turned = pltpu.roll(tile, HEAD, 1)
        keep = upper if group % 2 else jnp.logical_not(upper)
        low, high = (turned, tile) if group % 2 else (tile, turned)
        target[group, :count, :] = jnp.where(keep, low, 0.0).astype(BF16)
        target[group, count:, :] = jnp.where(keep, high, 0.0).astype(BF16)


def pad_query_t(columns, target):
    for group in range(4):
        both = jnp.concatenate(
            [
                columns[128 * group : 128 * group + 64],
                columns[128 * group + 64 : 128 * group + 128],
            ],
            axis=1,
        ).astype(BF16)
        blank = jnp.zeros(both.shape, BF16)
        own = HEAD * (group % 2)
        target[group, own : own + HEAD, :] = both
        target[group, HEAD - own : 2 * HEAD - own, :] = blank


def fold(wide):
    count = wide.shape[0] // 2
    return jnp.concatenate([wide[:count], wide[count:]], axis=1)


INPUTS = (
    "resid", "grad", "ids", "starts", "adapters", "attn_gain", "moe_gain", "freq",
    "qkv_down", "q_up", "kv_up", "o_down", "o_up", "router",
    "q_hbm", "kv_hbm", "o_hbm", "in_hbm", "out_hbm", "in_down_hbm", "in_up_hbm", "out_down_hbm", "out_up_hbm",
)
OUTPUTS = ("block_out", "in_grad", "final", "early_out", "late_out")


def layer_kernel(planes, slots, names, *refs):
    r = dict(zip(names, refs))
    r = type("Refs", (), r)
    r.acc_out, r.acc_h2 = r.halves.at[0], r.halves.at[1]
    me, ep, z, x, c = place()
    blocks = 4 * planes
    pair = {"ctx": me, "ep": 1 - ep}
    up = {"ctx": jnp.minimum(me + 4, blocks - 1), "ep": ep}
    down = {"ctx": jnp.maximum(me - 4, 0), "ep": ep}
    across = {"ctx": block_of(z, 1 - x, c), "ep": ep}
    beside = {"ctx": block_of(z, x, 1 - c), "ep": ep}
    rows = r.resid.shape[0]
    block = 2 * rows
    mine = span(ep * rows, rows)
    theirs = span(rows - ep * rows, rows)
    experts = r.in_hbm.shape[0]
    quarter_rows = r.pack.shape[1]
    piece_rows = quarter_rows // planes
    kept = r.from_across.shape[0]

    load_q = pltpu.make_async_copy(r.q_hbm, r.q_w, r.load_sem.at[0])
    load_kv = pltpu.make_async_copy(r.kv_hbm, r.kv_w, r.load_sem.at[1])
    load_o = pltpu.make_async_copy(r.o_hbm, r.ow_all.at[ep], r.load_sem.at[2])
    load_kv.start()
    load_q.start()
    load_o.start()
    weights = (
        (r.in_hbm, r.w_in), (r.out_hbm, r.w_out), (r.in_down_hbm, r.w_in_down),
        (r.in_up_hbm, r.w_in_up), (r.out_down_hbm, r.w_out_down), (r.out_up_hbm, r.w_out_up),
    )

    def quarter_at(turn):
        return jnp.where(turn % 2 == 0, 1 - x, x) * 2 + jnp.where(turn < 2, 1 - c, c)

    def expert_at(turn):
        return 2 * quarter_at(turn // 2) + turn % 2

    def expert_loads(turn):
        e, slot = expert_at(turn), turn % slots
        return [
            pltpu.make_async_copy(source.at[e], held.at[slot], r.expert_sem.at[slot, number])
            for number, (source, held) in enumerate(weights)
        ]

    def begin(turn, carry):
        for copy in expert_loads(turn):
            copy.start()
        return carry

    lax.fori_loop(0, slots, begin, 0)

    signal(pair)

    def greet(step, carry):
        signal({"ctx": lax.rem(me + step, blocks), "ep": ep})
        return carry

    lax.fori_loop(1, blocks, greet, 0)
    pl.semaphore_wait(pltpu.get_barrier_semaphore(), blocks)

    def swap(number, src, dst):
        return remote(src, dst, r.pair_send.at[number], r.pair_recv.at[number], pair)

    send_x = swap(0, r.resid, r.x_all.at[mine])
    send_x.start()

    hot = jnp.zeros((r.ids.shape[0], rows), F32)
    hot = jnp.zeros((128, rows), F32)
    numbers = iota((128, rows), 0)
    for choice in range(r.ids.shape[0]):
        hot = hot + jnp.where(r.ids[choice : choice + 1, :] == numbers, 1.0, 0.0)
    r.hot_all[mine, :] = hot.T.astype(BF16)
    r.x_all[mine, :] = r.resid[...]
    r.g_all[mine, :] = r.grad[...]
    r.od_all[ep] = r.o_down[...]
    position = me * block + iota((block, 128), 0)
    own_start, adapter = doc_scan(position, r.starts, r.adapters)
    r.mask[...] = jnp.where((iota((block, 128), 1) % SPAN) // RANK == adapter, 1.0, 0.0)
    angles = (position - own_start).astype(F32) * r.freq[...]
    r.cosine[...] = jnp.cos(angles)
    r.sine[...] = jnp.sin(angles)
    row_pos = me * block + iota((8, 2 * block), 1) % block
    row_start, unused = doc_scan(row_pos, r.starts, r.adapters)
    start_row, pos_row = row_start[:1], row_pos[:1]

    def ring(number, half, way, target):
        part = r.kvall.at[number, :, mine if half == 0 else theirs, :]
        return remote(part, part, r.ring_send.at[way, number, half], r.ring_recv.at[number, half], target)

    def forward_own(p, half):
        number = block_of(p, x, c)

        @pl.when(z < planes - 1)
        def _():
            ring(number, half, 0, up).start()

        ring(number, half, 1, across).start()
        ring(number, half, 2, beside).start()

    def forward_across(p, half):
        number = block_of(p, 1 - x, c)
        ring(number, half, 1, across).wait_recv()
        ring(number, half, 2, beside).start()

    def arrive_beside(p):
        for column in (0, 1):
            for half in (0, 1):
                ring(block_of(p, column, 1 - c), half, 2, beside).wait_recv()

    def project(here):
        h1 = rms(r.x_all[here, :].astype(F32), r.attn_gain[...]).astype(BF16)
        r.h1[here, :] = h1
        mids = (dot(h1, r.qkv_down[...], NT) * r.mask[here, : 3 * SPAN]).astype(BF16)
        r.mids[here, :] = mids
        k_lin = dot(h1, r.kv_w[0]) + dot(mids[:, SPAN : 2 * SPAN], r.kv_up[0])
        r.kvall[me, 0, here, :] = rotate(k_lin, r.cosine[here, :], r.sine[here, :], 1.0).astype(BF16)
        r.kvall[me, 1, here, :] = (dot(h1, r.kv_w[1]) + dot(mids[:, 2 * SPAN :], r.kv_up[1])).astype(BF16)

    load_kv.wait()
    project(mine)
    forward_own(z, 0)
    send_x.wait_recv()
    load_o.wait()
    send_ow = swap(3, r.ow_all.at[ep], r.ow_all.at[ep])
    send_od = swap(4, r.od_all.at[ep], r.od_all.at[ep])
    send_hot = swap(1, r.hot_all.at[mine], r.hot_all.at[mine])
    send_g = swap(2, r.grad, r.g_all.at[mine])
    for copy in (send_ow, send_od, send_hot, send_g):
        copy.start()
    project(theirs)
    forward_own(z, 1)
    load_q.wait()
    q_lin = dot(r.h1[...], r.q_w[...]) + dot(r.mids[:, :SPAN], r.q_up[...])
    query = rotate(q_lin, r.cosine[...], r.sine[...], 1.0).astype(BF16).astype(F32)
    pad_query(query, r.qn)
    pad_query_t((query * SCALE).T, r.qt)
    r.m_s[...] = jnp.full(r.m_s.shape, LOW, F32)
    r.l_s[...] = jnp.zeros(r.l_s.shape, F32)
    r.acc[...] = jnp.zeros(r.acc.shape, F32)
    forward_across(z, 0)
    forward_across(z, 1)
    arrive_beside(z)

    def head_step(p, group, masked):
        tile = slice(128 * (group // 2), 128 * (group // 2) + 128)
        scores, peak = [], None
        sees = start_row <= (4 * p + 1) * block
        for b in range(4):
            s = dot(r.kvall[4 * p + b, 0, :, tile], r.qt[group])
            if masked[b]:
                key = (4 * p + b) * block + iota(s.shape, 0)
                s = jnp.where((key <= pos_row) & (key >= start_row), s, LOW)
            scores.append(s)
            highest = jnp.max(s, axis=0, keepdims=True)
            if not masked[b]:
                highest = jnp.where(sees, highest, LOW)
            peak = highest if peak is None else jnp.maximum(peak, highest)
        old = r.m_s[group]
        new = jnp.maximum(old, peak)
        r.m_s[group] = new
        blind = jnp.where(sees, new, -LOW)
        decay = jnp.exp(old - new)
        total = r.l_s[group] * decay
        grown = r.acc[group] * decay
        for b in range(4):
            w = jnp.exp(scores[b] - (new if masked[b] else blind))
            total = total + jnp.sum(w, axis=0, keepdims=True)
            added = dot(r.kvall[4 * p + b, 1, :, tile], w.astype(BF16), TN)
            grown = grown + added[HEAD * (group % 2) : HEAD * (group % 2) + HEAD]
        r.l_s[group] = total
        r.acc[group] = grown

    def send_att(group):
        part = r.att_all.at[ep, :, pl.ds(128 * group, 128)]
        return swap(5 + group, part, part)

    def settle(group):
        r.lse[group] = r.m_s[group] + jnp.log(r.l_s[group])
        done = r.acc[group] / r.l_s[group]
        attended = jnp.concatenate([done[:, :block], done[:, block:]], axis=0).T
        tile = slice(128 * group, 128 * group + 128)
        r.att[:, tile] = attended
        r.att_all[ep, :, tile] = attended.astype(BF16)
        send_att(group).start()

    def plane_forward(turn, carry):
        p = z - turn

        def heads(group):
            @pl.when(turn == 0)
            def _():
                head_step(p, group, (True,) * 4)

            @pl.when((turn > 0) & (p > 0))
            def _():
                head_step(p, group, (False,) * 4)

            @pl.when((turn > 0) & (p == 0))
            def _():
                head_step(p, group, (True, False, False, False))

            @pl.when(p == 0)
            def _():
                settle(group)

        heads(0)

        @pl.when(p > 0)
        def _():
            ring(block_of(p - 1, x, c), 0, 0, up).wait_recv()
            forward_own(p - 1, 0)

        heads(1)

        @pl.when(p > 0)
        def _():
            ring(block_of(p - 1, x, c), 1, 0, up).wait_recv()
            forward_own(p - 1, 1)

        heads(2)

        @pl.when(p > 0)
        def _():
            forward_across(p - 1, 0)

        heads(3)

        @pl.when(p > 0)
        def _():
            forward_across(p - 1, 1)
            arrive_beside(p - 1)

        return carry

    lax.fori_loop(0, z + 1, plane_forward, 0)

    def ring_drain(p, carry):
        for side in (0, 1):

            @pl.when(z < planes - 1)
            def _():
                ring(block_of(p, x, c), side, 0, up).wait_send()

            ring(block_of(p, x, c), side, 1, across).wait_send()
            ring(block_of(p, x, c), side, 2, beside).wait_send()
            ring(block_of(p, 1 - x, c), side, 2, beside).wait_send()
        return carry

    send_ow.wait_recv()
    send_od.wait_recv()

    def half_product(index, carry):
        which = jnp.where(index == 0, ep, 1 - ep)

        @pl.when(index == 1)
        def _():
            for group in range(4):
                send_att(group).wait_recv()

        r.halves[which] = dot(r.att_all[which], r.ow_all[which])
        r.half_mid[which] = dot(r.att_all[which], r.od_all[which], NT)
        return carry

    lax.fori_loop(0, 2, half_product, 0)
    mid_o = ((r.half_mid[0] + r.half_mid[1]) * r.mask[:, :SPAN]).astype(BF16)
    r.mid_o[...] = mid_o
    x2 = r.x_all[...].astype(F32) + (r.halves[0] + r.halves[1]) + dot(mid_o, r.o_up[...])
    r.x2[...] = x2
    h2 = rms(x2, r.moe_gain[...]).astype(BF16)
    r.h2[...] = h2
    send_hot.wait_recv()
    logits = dot(h2, r.router[...], NT)
    chosen = r.hot_all[:, : 2 * experts].astype(F32) > 0.5
    logits = jnp.where(chosen, logits, LOW)
    grown = jnp.where(chosen, jnp.exp(logits - jnp.max(logits, axis=1, keepdims=True)), 0.0)
    gates = grown / jnp.sum(grown, axis=1, keepdims=True)
    r.gates[...] = gates
    r.acc_out[...] = jnp.zeros(r.acc_out.shape, F32)
    r.acc_h2[...] = jnp.zeros(r.acc_h2.shape, F32)
    r.dgates[...] = jnp.zeros(r.dgates.shape, F32)
    r.pack[:, 288:, :] = jnp.zeros((4, quarter_rows - 288, r.pack.shape[2]), BF16)
    send_g.wait_recv()

    def to_core(column):
        return remote(
            r.pack.at[2 * column + 1 - c], r.core_recv.at[column],
            r.core_send_sem.at[column], r.core_recv_sem.at[column], beside,
        )

    to_column = remote(r.pack.at[2 * (1 - x) + c], r.x_recv, r.x_sem.at[0], r.x_sem.at[1], across)
    quarter = 2 * x + c

    def one(turn, carry):
        slot = turn % slots
        e = expert_at(turn)
        for copy in expert_loads(turn):
            copy.wait()
        h2, g = r.h2[...], r.g_all[...]
        mask = r.mask[...]
        gate = jnp.sum(
            jnp.where(iota((block, 2 * experts), 1) == e + ep * experts, r.gates[...], 0.0), axis=1, keepdims=True
        )
        mid_in = (dot(h2, r.w_in_down[slot], NT) * mask[:, : 2 * SPAN]).astype(BF16)
        gate_part = dot(h2, r.w_in[slot, :, :FF]) + dot(mid_in[:, :SPAN], r.w_in_up[slot, 0])
        up_part = dot(h2, r.w_in[slot, :, FF:]) + dot(mid_in[:, SPAN:], r.w_in_up[slot, 1])
        squash = 1.0 / (1.0 + jnp.exp(-gate_part))
        silu = gate_part * squash
        act = (silu * up_part).astype(BF16)
        mid_out = dot(act, r.w_out_down[slot], NT) * mask[:, :SPAN]
        lifted = (dot(g, r.w_out_up[slot], NT) * mask[:, :SPAN]).astype(BF16)
        d_act = dot(g, r.w_out[slot], NT) + dot(lifted, r.w_out_down[slot])
        d_gate = jnp.sum(act.astype(F32) * d_act, axis=1, keepdims=True)
        r.dgates[...] += jnp.where(iota(r.dgates.shape, 1) == e, d_gate, 0.0)
        d_act = d_act * gate
        d_up = (d_act * silu).astype(BF16)
        d_gp = (d_act * up_part * squash * (1.0 + gate_part * (1.0 - squash))).astype(BF16)
        d_mid_in = (
            jnp.concatenate([dot(d_gp, r.w_in_up[slot, 0], NT), dot(d_up, r.w_in_up[slot, 1], NT)], axis=1)
            * mask[:, : 2 * SPAN]
        ).astype(BF16)
        scaled_mid = (mid_out * gate).astype(BF16)
        r.acc_out[...] += dot((act.astype(F32) * gate).astype(BF16), r.w_out[slot]) + dot(
            scaled_mid, r.w_out_up[slot]
        )
        r.acc_h2[...] += (
            dot(d_gp, r.w_in[slot, :, :FF], NT)
            + dot(d_up, r.w_in[slot, :, FF:], NT)
            + dot(d_mid_in, r.w_in_down[slot])
        )
        q = quarter_at(turn // 2)
        first = 144 * (turn % 2)

        def at(offset, count):
            return pl.ds(pl.multiple_of(first + offset, 16), count)

        r.pack[q, at(0, 64), :] = dot(d_mid_in, h2, TN).astype(BF16)
        r.pack[q, at(64, 32), :FF] = dot(mid_in[:, :SPAN], d_gp, TN).astype(BF16)
        r.pack[q, at(64, 32), FF:] = dot(mid_in[:, SPAN:], d_up, TN).astype(BF16)
        r.pack[q, at(96, 16), :] = fold(
            dot((lifted.astype(F32) * gate).astype(BF16), act, TN)
        ).astype(BF16)
        r.pack[q, at(112, 32), :] = dot(scaled_mid, g, TN).astype(BF16)

        @pl.when(turn + slots < experts)
        def _():
            for copy in expert_loads(turn + slots):
                copy.start()

        @pl.when(turn == 1)
        def _():
            to_core(1 - x).start()

        @pl.when(turn == 3)
        def _():
            to_core(x).start()

        def add_core(column):
            to_core(column).wait_recv()
            number = 2 * column + c
            r.pack[number] = (r.pack[number].astype(F32) + r.core_recv[column].astype(F32)).astype(BF16)

        @pl.when(turn == 5)
        def _():
            add_core(1 - x)
            to_column.start()

        @pl.when(turn == 7)
        def _():
            add_core(x)

        return carry

    lax.fori_loop(0, experts, one, 0)

    r.dg_trade[ep] = r.dgates[...].T[:8]
    send_dg = swap(9, r.dg_trade.at[ep], r.dg_trade.at[ep])
    send_dg.start()
    r.trade[ep] = r.acc_h2[...].astype(BF16)
    send_h2 = swap(10, r.trade.at[ep], r.trade.at[ep])
    send_h2.start()
    r.out_trade[0] = r.acc_out[theirs, :].astype(BF16)
    send_out = swap(11, r.out_trade.at[0], r.out_trade.at[1])
    send_out.start()

    to_column.wait_recv()
    r.pack[quarter] = (r.pack[quarter].astype(F32) + r.x_recv[...].astype(F32)).astype(BF16)

    def plane_of(step):
        return lax.rem(z + step, planes)

    def give(step):
        other = plane_of(step)
        return remote(
            r.pack.at[quarter, span(other * piece_rows, piece_rows), :], r.z_recv.at[z],
            r.z_send_sem.at[0, other], r.z_recv_sem.at[0, z], {"ctx": block_of(other, x, c), "ep": ep},
        )

    def take(step):
        other = plane_of(step)
        return remote(
            r.pack.at[quarter, span(other * piece_rows, piece_rows), :], r.z_recv.at[other],
            r.z_send_sem.at[0, other], r.z_recv_sem.at[0, other], {"ctx": block_of(other, x, c), "ep": ep},
        )

    def spread(step):
        other = plane_of(step)
        part = r.final.at[quarter, span(z * piece_rows, piece_rows), :]
        return remote(
            part, part, r.z_send_sem.at[1, other], r.z_recv_sem.at[1, z], {"ctx": block_of(other, x, c), "ep": ep}
        )

    def gather(step):
        other = plane_of(step)
        part = r.final.at[quarter, span(other * piece_rows, piece_rows), :]
        return remote(
            part, part, r.z_send_sem.at[1, other], r.z_recv_sem.at[1, other], {"ctx": block_of(other, x, c), "ep": ep}
        )

    def each_plane(act):
        def step(number, carry):
            act(number)
            return carry

        lax.fori_loop(1, planes, step, 0)

    each_plane(lambda step: give(step).start())

    def stage_own():
        each_plane(lambda step: take(step).wait_recv())
        r.z_recv[z] = r.pack[quarter, span(z * piece_rows, piece_rows), :]

        def add(p, total):
            return total + r.z_recv[p].astype(F32)

        total = lax.fori_loop(0, planes, add, jnp.zeros(r.z_recv.shape[1:], F32))
        r.final[quarter, span(z * piece_rows, piece_rows), :] = total.astype(BF16)
        each_plane(lambda step: spread(step).start())

    def over_final(number, way, target):
        part = r.final.at[number]
        return remote(part, part, r.last_send.at[way, number], r.last_recv.at[number], target)

    def stage_column():
        each_plane(lambda step: gather(step).wait_recv())
        over_final(quarter, 0, across).start()
        over_final(quarter, 1, beside).start()

    def stage_core():
        over_final(2 * (1 - x) + c, 0, across).wait_recv()
        over_final(2 * (1 - x) + c, 1, beside).start()

    def stage_end():
        over_final(2 * x + 1 - c, 1, beside).wait_recv()
        over_final(2 * (1 - x) + 1 - c, 1, beside).wait_recv()
        each_plane(lambda step: give(step).wait_send())
        each_plane(lambda step: spread(step).wait_send())
        over_final(quarter, 0, across).wait_send()
        over_final(quarter, 1, beside).wait_send()
        over_final(2 * (1 - x) + c, 1, beside).wait_send()
        to_core(0).wait_send()
        to_core(1).wait_send()
        to_column.wait_send()

    def small_sum(number, source, landing, result):
        tiles = source.shape[0] // 16
        width = landing.shape[2]
        each = source.shape[1] // width
        owners = tiles * each

        def region(ref, owner):
            return ref.at[span(owner // each * 16, 16), span(owner % each * width, width)]

        def other(step):
            return lax.rem(me + step, blocks)

        def to_owner(step):
            owner = other(step)
            return remote(
                region(source, owner), landing.at[me], r.small_send.at[number, 0, owner],
                r.small_recv.at[number, 0, me], {"ctx": owner, "ep": ep},
            )

        def from_all(step):
            device = other(step)
            return remote(
                region(source, me % owners), landing.at[device], r.small_send.at[number, 0, device],
                r.small_recv.at[number, 0, device], {"ctx": device, "ep": ep},
            )

        def to_all(step):
            device = other(step)
            part = region(result, me % owners)
            return remote(
                part, part, r.small_send.at[number, 1, device], r.small_recv.at[number, 1, me],
                {"ctx": device, "ep": ep},
            )

        def from_owner(step):
            owner = other(step)
            part = region(result, owner)
            return remote(
                part, part, r.small_send.at[number, 1, owner], r.small_recv.at[number, 1, owner],
                {"ctx": owner, "ep": ep},
            )

        def loop(act, mine_too):
            def step(index, carry):
                if mine_too:
                    act(index)
                else:

                    @pl.when(other(index) < owners)
                    def _():
                        act(index)

                return carry

            lax.fori_loop(1, blocks, step, 0)

        def scatter():
            loop(lambda step: to_owner(step).start(), False)

        def total():
            @pl.when(me < owners)
            def _():
                loop(lambda step: from_all(step).wait_recv(), True)
                landing[me] = region(source, me % owners)[...]

                def add(p, sums):
                    return sums + landing[p].astype(F32)

                sums = lax.fori_loop(0, blocks, add, jnp.zeros(landing.shape[1:], F32))
                region(result, me % owners)[...] = sums.astype(BF16)
                loop(lambda step: to_all(step).start(), True)

        def finish():
            loop(lambda step: from_owner(step).wait_recv(), False)
            loop(lambda step: to_owner(step).wait_send(), False)

            @pl.when(me < owners)
            def _():
                loop(lambda step: to_all(step).wait_send(), True)

        return scatter, total, finish

    early_scatter, early_total, early_finish = small_sum(0, r.early, r.early_land, r.early_out)
    late_scatter, late_total, late_finish = small_sum(1, r.late, r.late_land, r.late_out)

    lax.fori_loop(0, z + 1, ring_drain, 0)

    send_dg.wait_recv()
    blank = jnp.zeros((112, block), F32)
    table = jnp.concatenate([r.dg_trade[0], r.dg_trade[1], blank], axis=0).T
    d_gates = table[:, : 2 * experts]
    gates = r.gates[...]
    d_logits = (gates * (d_gates - jnp.sum(gates * d_gates, axis=1, keepdims=True))).astype(BF16)
    from_router = dot(d_logits, r.router[...])
    send_h2.wait_recv()
    d_h2 = r.trade[0].astype(F32) + r.trade[1].astype(F32) + from_router
    d_x2 = r.g_all[...].astype(F32) + rms_back(r.x2[...], r.moe_gain[...], d_h2)
    d_attn = d_x2.astype(BF16)
    r.acc_h2[...] = d_x2
    d_mid_o = (dot(d_attn, r.o_up[...], NT) * r.mask[:, :SPAN]).astype(BF16)

    d_att = (dot(d_attn, r.ow_all[ep], NT) + dot(d_mid_o, r.od_all[ep])).astype(BF16).astype(F32)
    pad_query(d_att, r.dn)
    pad_query_t(d_att.T, r.dt)
    product = (d_att * r.att[...]).T
    for group in range(4):
        for side in (0, 1):
            first = 128 * group + 64 * side
            r.delta[group, :, side * block : side * block + block] = jnp.sum(
                product[first : first + 64], axis=0, keepdims=True
            )
    r.dqt[...] = jnp.zeros(r.dqt.shape, F32)
    r.early[:32, :] = dot(r.mid_o[...], d_attn, TN).astype(BF16)
    r.early[32:48, :] = fold(dot(d_mid_o, r.att_all[ep], TN)).astype(BF16)
    r.early[48:, :] = jnp.zeros((16, r.early.shape[1]), BF16)
    early_scatter()

    def block_step(number, masked):
        new_k, new_v = [], []
        for group in range(4):
            tile = slice(128 * (group // 2), 128 * (group // 2) + 128)
            keys = r.kvall[number, 0, :, tile]
            s = dot(keys, r.qt[group])
            base = r.lse[group]
            if masked:
                key = number * block + iota(s.shape, 0)
                w = jnp.where((key <= pos_row) & (key >= start_row), jnp.exp(s - base), 0.0)
            else:
                w = jnp.exp(s - jnp.where(start_row <= number * block, base, -LOW))
            d_w = dot(r.kvall[number, 1, :, tile], r.dt[group])
            d_s = (w * (d_w - r.delta[group])).astype(BF16)
            new_k.append(dot(d_s, r.qn[group]))
            new_v.append(dot(w.astype(BF16), r.dn[group]))
            r.dqt[group] += dot(keys, d_s, TN)[HEAD * (group % 2) : HEAD * (group % 2) + HEAD]
        for side in (0, 1):
            tile = slice(128 * side, 128 * side + 128)
            r.kvall[number, 0, :, tile] = ((new_k[2 * side] + new_k[2 * side + 1]) * SCALE).astype(BF16)
            r.kvall[number, 1, :, tile] = (new_v[2 * side] + new_v[2 * side + 1]).astype(BF16)

    def compute(number):
        edge = (number == 0) | (number == me)

        @pl.when(edge)
        def _():
            block_step(number, True)

        @pl.when((number < me) & jnp.logical_not(edge))
        def _():
            block_step(number, False)

        @pl.when(number > me)
        def _():
            r.kvall[number] = jnp.zeros(r.kvall.shape[1:], BF16)

    def to_beside(p, column):
        return remote(
            r.kvall.at[block_of(p, column, 1 - c)], r.from_beside.at[p % kept, column],
            r.beside_send.at[p, column], r.beside_recv.at[p, column], beside,
        )

    def over(p):
        return remote(
            r.kvall.at[block_of(p, 1 - x, c)], r.from_across.at[p % kept], r.across_send.at[p], r.across_recv.at[p], across
        )

    def lower(p):
        return remote(r.kvall.at[block_of(p, x, c)], r.from_up.at[p % kept], r.down_send.at[p], r.down_recv.at[p], down)

    def claim(p, number):
        if planes > kept:

            @pl.when(p >= kept)
            def _():
                pl.semaphore_wait(r.credit.at[number], 1)

    def release(p):
        if planes > kept:

            @pl.when(p + kept <= z)
            def _():
                pl.semaphore_signal(r.credit.at[0], inc=1, device_id=beside, device_id_type=MESH)
                pl.semaphore_signal(r.credit.at[1], inc=1, device_id=across, device_id_type=MESH)

            @pl.when((p + kept <= z) & (z < planes - 1))
            def _():
                pl.semaphore_signal(r.credit.at[2], inc=1, device_id=up, device_id_type=MESH)

    def finish(p):
        number = block_of(p, x, c)
        over(p).wait_recv()
        total = (
            r.kvall[number].astype(F32) + r.from_beside[p % kept, x].astype(F32) + r.from_across[p % kept].astype(F32)
        )
        r.kvall[number] = total.astype(BF16)

        @pl.when(z < planes - 1)
        def _():
            lower(p).wait_recv()
            r.kvall[number] = (total + r.from_up[p % kept].astype(F32)).astype(BF16)

        release(p)

        @pl.when(p < z)
        def _():
            claim(p, 2)
            lower(p).start()

    def plane_back(p, carry):
        @pl.when(p <= z)
        def _():
            compute(block_of(p, 1 - x, 1 - c))
            claim(p, 0)
            to_beside(p, 1 - x).start()
            compute(block_of(p, x, 1 - c))
            to_beside(p, x).start()

            @pl.when(p > 0)
            def _():
                finish(p - 1)

            compute(block_of(p, 1 - x, c))
            to_beside(p, 1 - x).wait_recv()
            number = block_of(p, 1 - x, c)
            r.kvall[number] = (r.kvall[number].astype(F32) + r.from_beside[p % kept, 1 - x].astype(F32)).astype(BF16)
            claim(p, 1)
            over(p).start()
            compute(block_of(p, x, c))
            to_beside(p, x).wait_recv()

        @pl.when(p == 0)
        def _():
            stage_own()

        @pl.when(p == 1)
        def _():
            early_total()

        @pl.when(p == 2)
        def _():
            stage_column()

        @pl.when(p == planes - 1)
        def _():
            stage_core()

        return carry

    lax.fori_loop(0, planes, plane_back, 0)
    finish(z)

    cosine, sine = r.cosine[...], r.sine[...]
    parts = []
    for group in range(4):
        both = r.dqt[group]
        parts += [both[:, :block], both[:, block:]]
    d_query = jnp.concatenate(parts, axis=0).T * SCALE
    d_q = rotate(d_query.astype(BF16).astype(F32), cosine, sine, -1.0).astype(BF16)
    d_k = rotate(r.kvall[me, 0].astype(F32), cosine, sine, -1.0).astype(BF16)
    d_value = r.kvall[me, 1]
    r.mid_trade[ep] = jnp.concatenate(
        [dot(d_q, r.q_up[...], NT), dot(d_k, r.kv_up[0], NT), dot(d_value, r.kv_up[1], NT)], axis=1
    ).astype(BF16)
    send_mid = swap(12, r.mid_trade.at[ep], r.mid_trade.at[ep])
    send_mid.start()
    full = dot(d_q, r.q_w[...], NT) + dot(d_k, r.kv_w[0], NT) + dot(d_value, r.kv_w[1], NT)
    first, second = full[:rows], full[rows:]
    r.norm_trade[0] = jnp.where(ep == 0, second, first).astype(BF16)
    send_norm = swap(13, r.norm_trade.at[0], r.norm_trade.at[1])
    send_norm.start()
    r.late[96:112, :] = fold(dot(r.mids[:, :SPAN], d_q, TN)).astype(BF16)
    r.late[112:, :] = fold(
        jnp.concatenate(
            [dot(r.mids[:, SPAN : 2 * SPAN], d_k, TN), dot(r.mids[:, 2 * SPAN :], d_value, TN)], axis=1
        )
    ).astype(BF16)
    send_mid.wait_recv()
    d_mids = (
        (r.mid_trade[0].astype(F32) + r.mid_trade[1].astype(F32)) * r.mask[:, : 3 * SPAN]
    ).astype(BF16)
    r.late[:96, :] = dot(d_mids, r.h1[...], TN).astype(BF16)
    late_scatter()
    send_out.wait_recv()
    r.block_out[...] = (r.x2[mine, :] + (r.acc_out[mine, :] + r.out_trade[1].astype(F32))).astype(BF16)
    from_mids = dot(d_mids, r.qkv_down[...])
    own = jnp.where(ep == 0, first + from_mids[:rows], second + from_mids[rows:])
    send_norm.wait_recv()
    own = own + r.norm_trade[1].astype(F32)
    r.in_grad[...] = (
        r.acc_h2[mine, :] + rms_back(r.x_all[mine, :].astype(F32), r.attn_gain[...], own)
    ).astype(BF16)
    late_total()
    early_finish()
    stage_end()

    for copy in (send_x, send_ow, send_od, send_hot, send_g, send_dg, send_h2, send_out, send_mid, send_norm):
        copy.wait_send()
    for group in range(4):
        send_att(group).wait_send()

    def drain(p, carry):
        for side in (0, 1):
            to_beside(p, side).wait_send()
        over(p).wait_send()

        @pl.when(p < z)
        def _():
            lower(p).wait_send()

        return carry

    lax.fori_loop(0, z + 1, drain, 0)
    late_finish()


def unpack_kernel(
    final, early, late, block_in, grad_in,
    ein_down, ein_up, eout_down, eout_up, block_out, in_grad, g_down, g_q, g_kv, g_od, g_ou,
):
    for number in range(2):
        part = final[0, 144 * number : 144 * number + 144, :].astype(F32)
        ein_down[number] = part[:64]
        ein_up[number, 0] = part[64:96, :FF]
        ein_up[number, 1] = part[64:96, FF:]
        eout_down[number, :16] = part[96:112, :FF]
        eout_down[number, 16:] = part[96:112, FF:]
        eout_up[number] = part[112:]

    @pl.when(pl.program_id(0) == 0)
    def _():
        block_out[...] = block_in[...]
        in_grad[...] = grad_in[...]
        g_down[...] = late[:96, :].astype(F32)
        g_q[:16, :] = late[96:112, :FF].astype(F32)
        g_q[16:, :] = late[96:112, FF:].astype(F32)
        both = late[112:, :].astype(F32)
        kv = FF // 2
        g_kv[0, :16, :] = both[:, :kv]
        g_kv[1, :16, :] = both[:, kv : 2 * kv]
        g_kv[0, 16:, :] = both[:, 2 * kv : 3 * kv]
        g_kv[1, 16:, :] = both[:, 3 * kv :]
        g_od[:16, :] = early[32:48, :FF].astype(F32)
        g_od[16:, :] = early[32:48, FF:].astype(F32)
        g_ou[...] = early[:32, :].astype(F32)


def per_device(
    resid_in, out_grad, attn_gain, q_weight, key_value_weight, o_weight, moe_gain, router, expert_in,
    expert_out, qkv_down, q_up, key_value_up_factor, o_down, o_up, expert_in_down, expert_in_up,
    expert_out_down, expert_out_up, expert_ids, doc_starts, doc_adapter,
):
    blocks = lax.axis_size("ctx")
    planes = blocks // 4
    rows, width = resid_in.shape
    block = 2 * rows
    heads = q_weight.shape[1]
    kv = key_value_weight.shape[2]
    experts = expert_in.shape[0]
    slots = 4 if planes <= 4 else 2
    kept = planes if planes <= 4 else 2
    piece_rows = -(-288 // (16 * planes)) * 16
    quarter_rows = piece_rows * planes
    early_width = max(128, 4 * width // blocks)
    late_width = max(128, 8 * width // blocks)
    freq = np.tile(np.power(10000.0, -2.0 * np.arange(HEAD // 2) / HEAD).astype(np.float32), 4)[None, :]

    def shape(dims, kind=BF16):
        return jax.ShapeDtypeStruct(dims, kind)

    def dma(*dims):
        return pltpu.SemaphoreType.DMA(dims)

    def low(*dims):
        return pltpu.VMEM(dims, BF16)

    def full(*dims):
        return pltpu.VMEM(dims, F32)

    operands = dict(
        resid=resid_in, grad=out_grad, ids=expert_ids.T, starts=doc_starts, adapters=doc_adapter,
        attn_gain=attn_gain[None, :], moe_gain=moe_gain[None, :], freq=jnp.asarray(freq), qkv_down=qkv_down.T,
        q_up=q_up, kv_up=key_value_up_factor, o_down=o_down.T, o_up=o_up, router=router.T, q_hbm=q_weight,
        kv_hbm=key_value_weight, o_hbm=o_weight, in_hbm=expert_in, out_hbm=expert_out,
        in_down_hbm=jnp.swapaxes(expert_in_down, 1, 2), in_up_hbm=expert_in_up,
        out_down_hbm=jnp.swapaxes(expert_out_down, 1, 2), out_up_hbm=expert_out_up,
    )
    results = dict(
        block_out=shape((rows, width)), in_grad=shape((rows, width)), final=shape((4, quarter_rows, width)),
        early_out=shape((64, width)), late_out=shape((128, width)),
    )
    scratch = dict(
        q_w=low(*q_weight.shape), kv_w=low(*key_value_weight.shape), ow_all=low(2, heads, width),
        od_all=low(2, SPAN, heads), w_in=low(slots, *expert_in.shape[1:]), w_out=low(slots, *expert_out.shape[1:]),
        w_in_down=low(slots, 2 * SPAN, width), w_in_up=low(slots, *expert_in_up.shape[1:]),
        w_out_down=low(slots, SPAN, FF), w_out_up=low(slots, *expert_out_up.shape[1:]),
        x_all=low(block, width), g_all=low(block, width), h1=low(block, width), h2=low(block, width),
        hot_all=low(block, 128), mask=full(block, 128), cosine=full(block, 128), sine=full(block, 128),
        mids=low(block, 3 * SPAN), kvall=low(blocks, 2, block, kv), qt=low(4, 128, 2 * block),
        qn=low(4, 2 * block, 128), dt=low(4, 128, 2 * block), dn=low(4, 2 * block, 128),
        m_s=full(4, 1, 2 * block), l_s=full(4, 1, 2 * block), lse=full(4, 1, 2 * block),
        delta=full(4, 1, 2 * block), acc=full(4, HEAD, 2 * block), dqt=full(4, HEAD, 2 * block),
        att=full(block, heads), att_all=low(2, block, heads), halves=full(2, block, width), half_mid=full(2, block, SPAN), mid_o=low(block, SPAN), x2=full(block, width),
        gates=full(block, 2 * experts), dgates=full(block, 128), trade=low(2, block, width), out_trade=low(2, rows, width),
        norm_trade=low(2, rows, width), mid_trade=low(2, block, 3 * SPAN), dg_trade=full(2, 8, block),
        pack=low(4, quarter_rows, width), core_recv=low(2, quarter_rows, width), x_recv=low(quarter_rows, width),
        z_recv=low(planes, piece_rows, width), early=low(64, width), late=low(128, width),
        early_land=low(blocks, 16, early_width), late_land=low(blocks, 16, late_width),
        from_beside=low(kept, 2, 2, block, kv), from_across=low(kept, 2, block, kv),
        from_up=low(kept, 2, block, kv), credit=pltpu.SemaphoreType.REGULAR((3,)),
        load_sem=dma(3), expert_sem=dma(slots, 6), pair_send=dma(14), pair_recv=dma(14),
        ring_send=dma(3, blocks, 2), ring_recv=dma(blocks, 2), core_send_sem=dma(2), core_recv_sem=dma(2),
        x_sem=dma(2), z_send_sem=dma(2, planes), z_recv_sem=dma(2, planes), last_send=dma(2, 4), last_recv=dma(4),
        small_send=dma(2, 2, blocks), small_recv=dma(2, 2, blocks), beside_send=dma(planes, 2),
        beside_recv=dma(planes, 2), across_send=dma(planes), across_recv=dma(planes), down_send=dma(planes),
        down_recv=dma(planes),
    )
    block_out, in_grad, final, early, late = pl.pallas_call(
        functools.partial(layer_kernel, planes, slots, INPUTS + OUTPUTS + tuple(scratch)),
        out_shape=[results[name] for name in OUTPUTS],
        in_specs=[
            SMEM if name in ("starts", "adapters") else HBM if name.endswith("hbm") else VMEM for name in INPUTS
        ],
        out_specs=[VMEM] * len(OUTPUTS),
        scratch_shapes=list(scratch.values()),
        compiler_params=pltpu.CompilerParams(
            collective_id=1, has_side_effects=True, vmem_limit_bytes=62 << 20
        ),
        name="layer",
    )(*[operands[name] for name in INPUTS])

    def whole(*dims):
        return pl.BlockSpec(dims, lambda step: (0,) * len(dims))

    def two(*dims):
        return pl.BlockSpec((2, *dims), lambda step: (step,) + (0,) * len(dims))

    small = [(96, width), (SPAN, heads), (2, SPAN, kv), (SPAN, heads), (SPAN, width)]
    ein_down, ein_up, eout_down, eout_up, block_out, in_grad, g_down, g_q, g_kv, g_od, g_ou = pl.pallas_call(
        unpack_kernel,
        grid=(4,),
        out_shape=[
            shape((experts, 2 * SPAN, width), F32), shape((experts, 2, SPAN, FF), F32),
            shape((experts, SPAN, FF), F32), shape((experts, SPAN, width), F32),
            shape((rows, width)), shape((rows, width)), *[shape(dims, F32) for dims in small],
        ],
        in_specs=[
            pl.BlockSpec((1, quarter_rows, width), lambda step: (step, 0, 0)), whole(64, width), whole(128, width),
            whole(rows, width), whole(rows, width),
        ],
        out_specs=[
            two(2 * SPAN, width), two(2, SPAN, FF), two(SPAN, FF), two(SPAN, width), whole(rows, width),
            whole(rows, width), *[whole(*dims) for dims in small],
        ],
        compiler_params=pltpu.CompilerParams(vmem_limit_bytes=40 << 20),
        name="unpack",
    )(final, early, late, block_out, in_grad)
    return (
        block_out, in_grad, g_down.T, g_q, g_kv, g_od.T, g_ou, jnp.swapaxes(ein_down, 1, 2), ein_up,
        jnp.swapaxes(eout_down, 1, 2), eout_up,
    )


def solution(mesh):
    placed = (
        P(("ctx", "ep"), None),
        P(("ctx", "ep"), None),
        P(),
        P(None, "ep"),
        P(None, None, "ep"),
        P("ep", None),
        P(),
        P(),
        P("ep", None, None),
        P("ep", None, None),
        P(),
        P(None, "ep"),
        P(None, None, "ep"),
        P("ep", None),
        P(),
        P("ep", None, None),
        P("ep", None, None, None),
        P("ep", None, None),
        P("ep", None, None),
        P(("ctx", "ep"), None),
        P(),
        P(),
    )
    return jax.shard_map(
        per_device,
        mesh=mesh,
        in_specs=placed,
        out_specs=(
            P(("ctx", "ep"), None),
            P(("ctx", "ep"), None),
            P(),
            P(None, "ep"),
            P(None, None, "ep"),
            P("ep", None),
            P(),
            P("ep", None, None),
            P("ep", None, None, None),
            P("ep", None, None),
            P("ep", None, None),
        ),
        check_vma=False,
    )
```

```python
import functools

import jax
import jax.numpy as jnp
import numpy as np
from jax import lax
from jax.experimental import pallas as pl
from jax.experimental.pallas import tpu as pltpu
from jax.sharding import PartitionSpec as P

MESH = pl.DeviceIdType.MESH
VMEM = pl.BlockSpec(memory_space=pltpu.VMEM)
SMEM = pl.BlockSpec(memory_space=pltpu.SMEM)
HBM = pl.BlockSpec(memory_space=pl.ANY)
F32 = jnp.float32
BF16 = jnp.bfloat16

HEAD = 64
FF = 512
RANK = 16
SPAN = 32
EPS = 1e-06
LOW = -1e30
SCALE = 0.125

NN = (((1,), (0,)), ((), ()))
NT = (((1,), (1,)), ((), ()))
TN = (((0,), (0,)), ((), ()))


def dot(left, right, dims=NN):
    return lax.dot_general(left, right, dims, preferred_element_type=F32)


def iota(shape, dim):
    return lax.broadcasted_iota(jnp.int32, shape, dim)


def rms(values, gain):
    return values * lax.rsqrt(jnp.mean(values * values, axis=-1, keepdims=True) + EPS) * gain


def rms_back(values, gain, upstream):
    factor = lax.rsqrt(jnp.mean(values * values, axis=-1, keepdims=True) + EPS)
    scaled = upstream * gain
    return factor * scaled - values * factor * factor * factor * jnp.mean(
        scaled * values, axis=-1, keepdims=True
    )


def rotate(values, cosine, sine, sign):
    width = values.shape[1]
    copies = width // 128
    cosine = jnp.concatenate([cosine] * copies, axis=1)
    sine = jnp.concatenate([sine] * copies, axis=1)
    first = iota(values.shape, 1) % HEAD < HEAD // 2
    ahead = pltpu.roll(values, width - HEAD // 2, 1)
    behind = pltpu.roll(values, HEAD // 2, 1)
    return values * cosine + sign * jnp.where(first, -ahead, behind) * sine


def doc_scan(positions, starts_ref, adapters_ref):
    own_start = jnp.zeros(positions.shape, jnp.int32)
    adapter = jnp.zeros(positions.shape, jnp.int32)
    for number in range(starts_ref.shape[0]):
        opened = starts_ref[number] <= positions
        own_start = jnp.where(opened, starts_ref[number], own_start)
        adapter = jnp.where(opened, adapters_ref[number], adapter)
    return own_start, adapter


def place():
    me = lax.axis_index("ctx")
    ep = lax.axis_index("ep")
    return me, ep, me // 4, (me // 2) % 2, me % 2


def block_of(z, x, c):
    return (z * 2 + x) * 2 + c


def signal(device):
    pl.semaphore_signal(
        pltpu.get_barrier_semaphore(), inc=1, device_id=device, device_id_type=MESH
    )


def remote(src, dst, send, recv, device):
    return pltpu.make_async_remote_copy(
        src_ref=src,
        dst_ref=dst,
        send_sem=send,
        recv_sem=recv,
        device_id=device,
        device_id_type=MESH,
    )


def span(start, count):
    return pl.ds(pl.multiple_of(start, count), count)


def pad_query(rows, target):
    count = rows.shape[0]
    upper = iota((count, 128), 1) >= HEAD
    for group in range(4):
        tile = rows[:, 128 * group : 128 * group + 128]
        turned = pltpu.roll(tile, HEAD, 1)
        keep = upper if group % 2 else jnp.logical_not(upper)
        low, high = (turned, tile) if group % 2 else (tile, turned)
        target[group, :count, :] = jnp.where(keep, low, 0.0).astype(BF16)
        target[group, count:, :] = jnp.where(keep, high, 0.0).astype(BF16)


def pad_query_t(columns, target):
    for group in range(4):
        both = jnp.concatenate(
            [
                columns[128 * group : 128 * group + 64],
                columns[128 * group + 64 : 128 * group + 128],
            ],
            axis=1,
        ).astype(BF16)
        blank = jnp.zeros(both.shape, BF16)
        own = HEAD * (group % 2)
        target[group, own : own + HEAD, :] = both
        target[group, HEAD - own : 2 * HEAD - own, :] = blank


def fold(wide):
    count = wide.shape[0] // 2
    return jnp.concatenate([wide[:count], wide[count:]], axis=1)


INPUTS = (
    "resid", "grad", "ids", "starts", "adapters", "attn_gain", "moe_gain", "freq",
    "qkv_down", "q_up", "kv_up", "o_down", "o_up", "router",
    "q_hbm", "kv_hbm", "o_hbm", "in_hbm", "out_hbm", "in_down_hbm", "in_up_hbm", "out_down_hbm", "out_up_hbm",
)
OUTPUTS = ("out",)


def layer_kernel(planes, slots, names, *refs):
    r = dict(zip(names, refs))
    r = type("Refs", (), r)
    r.acc_out, r.acc_h2 = r.halves.at[0], r.halves.at[1]
    grad_rows = r.pack.shape[2]
    base = r.in_hbm.shape[0] * grad_rows
    r.late_out = r.out.at[pl.ds(base, 128)]
    r.block_out = r.out.at[pl.ds(base + 128, 128)]
    r.in_grad = r.out.at[pl.ds(base + 256, 128)]
    r.early_out = r.out.at[pl.ds(base + 384, 64)]
    me, ep, z, x, c = place()
    blocks = 4 * planes
    pair = {"ctx": me, "ep": 1 - ep}
    up = {"ctx": jnp.minimum(me + 4, blocks - 1), "ep": ep}
    down = {"ctx": jnp.maximum(me - 4, 0), "ep": ep}
    across = {"ctx": block_of(z, 1 - x, c), "ep": ep}
    beside = {"ctx": block_of(z, x, 1 - c), "ep": ep}
    rows = r.resid.shape[0]
    block = 2 * rows
    mine = span(ep * rows, rows)
    theirs = span(rows - ep * rows, rows)
    experts = r.in_hbm.shape[0]
    groups = 3 if planes >= 12 else 1
    owners = 4 * groups
    piece = (grad_rows // groups, r.pack.shape[3] // 4)
    kept = r.from_across.shape[0]

    load_q = pltpu.make_async_copy(r.q_hbm, r.q_w, r.load_sem.at[0])
    load_kv = pltpu.make_async_copy(r.kv_hbm, r.kv_w, r.load_sem.at[1])
    load_o = pltpu.make_async_copy(r.o_hbm, r.ow_all.at[ep], r.load_sem.at[2])
    load_kv.start()
    load_q.start()
    load_o.start()
    load_in_down = pltpu.make_async_copy(r.in_down_hbm, r.in_down, r.load_sem.at[3])
    load_out_up = pltpu.make_async_copy(r.out_up_hbm, r.out_up, r.load_sem.at[4])
    load_in_down.start()
    load_out_up.start()
    weights = (
        (r.in_hbm, r.w_in), (r.out_hbm, r.w_out), (r.in_up_hbm, r.w_in_up), (r.out_down_hbm, r.w_out_down),
    )

    def quarter_at(turn):
        return jnp.where(turn % 2 == 0, 1 - x, x) * 2 + jnp.where(turn < 2, 1 - c, c)

    def expert_at(turn):
        return 2 * quarter_at(turn % 4) + turn // 4

    def expert_loads(turn):
        e, slot = expert_at(turn), turn % slots
        return [
            pltpu.make_async_copy(source.at[e], held.at[slot], r.expert_sem.at[slot, number])
            for number, (source, held) in enumerate(weights)
        ]

    def begin(turn, carry):
        for copy in expert_loads(turn):
            copy.start()
        return carry

    lax.fori_loop(0, slots, begin, 0)

    signal(pair)

    def greet(step, carry):
        signal({"ctx": lax.rem(me + step, blocks), "ep": ep})
        return carry

    lax.fori_loop(1, blocks, greet, 0)
    pl.semaphore_wait(pltpu.get_barrier_semaphore(), blocks)

    def swap(number, src, dst):
        return remote(src, dst, r.pair_send.at[number], r.pair_recv.at[number], pair)

    send_x = swap(0, r.resid, r.x_all.at[mine])
    send_x.start()

    hot = jnp.zeros((r.ids.shape[0], rows), F32)
    hot = jnp.zeros((128, rows), F32)
    numbers = iota((128, rows), 0)
    for choice in range(r.ids.shape[0]):
        hot = hot + jnp.where(r.ids[choice : choice + 1, :] == numbers, 1.0, 0.0)
    r.hot_all[mine, :] = hot.T.astype(BF16)
    r.x_all[mine, :] = r.resid[...]
    r.g_all[mine, :] = r.grad[...]
    r.od_all[ep] = r.o_down[...]
    position = me * block + iota((block, 128), 0)
    own_start, adapter = doc_scan(position, r.starts, r.adapters)
    r.mask[...] = jnp.where((iota((block, 128), 1) % SPAN) // RANK == adapter, 1.0, 0.0)
    angles = (position - own_start).astype(F32) * r.freq[...]
    r.cosine[...] = jnp.cos(angles)
    r.sine[...] = jnp.sin(angles)
    row_pos = me * block + iota((8, 2 * block), 1) % block
    row_start, unused = doc_scan(row_pos, r.starts, r.adapters)
    start_row, pos_row = row_start[:1], row_pos[:1]

    def ring(number, half, way, target):
        part = r.kvall.at[number, :, mine if half == 0 else theirs, :]
        return remote(part, part, r.ring_send.at[way, number, half], r.ring_recv.at[number, half], target)

    def forward_own(p, half):
        number = block_of(p, x, c)

        @pl.when(z < planes - 1)
        def _():
            ring(number, half, 0, up).start()

        ring(number, half, 1, across).start()
        ring(number, half, 2, beside).start()

    def forward_across(p, half):
        number = block_of(p, 1 - x, c)
        ring(number, half, 1, across).wait_recv()
        ring(number, half, 2, beside).start()

    def arrive_beside(p):
        for column in (0, 1):
            for half in (0, 1):
                ring(block_of(p, column, 1 - c), half, 2, beside).wait_recv()

    def project(here):
        h1 = rms(r.x_all[here, :].astype(F32), r.attn_gain[...]).astype(BF16)
        r.h1[here, :] = h1
        mids = (dot(h1, r.qkv_down[...], NT) * r.mask[here, : 3 * SPAN]).astype(BF16)
        r.mids[here, :] = mids
        k_lin = dot(h1, r.kv_w[0]) + dot(mids[:, SPAN : 2 * SPAN], r.kv_up[0])
        r.kvall[me, 0, here, :] = rotate(k_lin, r.cosine[here, :], r.sine[here, :], 1.0).astype(BF16)
        r.kvall[me, 1, here, :] = (dot(h1, r.kv_w[1]) + dot(mids[:, 2 * SPAN :], r.kv_up[1])).astype(BF16)

    load_kv.wait()
    project(mine)
    forward_own(z, 0)
    send_x.wait_recv()
    load_o.wait()
    send_ow = swap(3, r.ow_all.at[ep], r.ow_all.at[ep])
    send_od = swap(4, r.od_all.at[ep], r.od_all.at[ep])
    send_hot = swap(1, r.hot_all.at[mine], r.hot_all.at[mine])
    send_g = swap(2, r.grad, r.g_all.at[mine])
    for copy in (send_ow, send_od, send_hot, send_g):
        copy.start()
    project(theirs)
    forward_own(z, 1)
    load_q.wait()
    q_lin = dot(r.h1[...], r.q_w[...]) + dot(r.mids[:, :SPAN], r.q_up[...])
    query = rotate(q_lin, r.cosine[...], r.sine[...], 1.0).astype(BF16).astype(F32)
    pad_query(query, r.qn)
    pad_query_t((query * SCALE).T, r.qt)
    r.m_s[...] = jnp.full(r.m_s.shape, LOW, F32)
    r.l_s[...] = jnp.zeros(r.l_s.shape, F32)
    r.acc[...] = jnp.zeros(r.acc.shape, F32)
    forward_across(z, 0)
    forward_across(z, 1)
    arrive_beside(z)

    def head_step(p, group, masked):
        tile = slice(128 * (group // 2), 128 * (group // 2) + 128)
        scores, peak = [], None
        sees = start_row <= (4 * p + 1) * block
        for b in range(4):
            s = dot(r.kvall[4 * p + b, 0, :, tile], r.qt[group])
            if masked[b]:
                key = (4 * p + b) * block + iota(s.shape, 0)
                s = jnp.where((key <= pos_row) & (key >= start_row), s, LOW)
            scores.append(s)
            highest = jnp.max(s, axis=0, keepdims=True)
            if not masked[b]:
                highest = jnp.where(sees, highest, LOW)
            peak = highest if peak is None else jnp.maximum(peak, highest)
        old = r.m_s[group]
        new = jnp.maximum(old, peak)
        r.m_s[group] = new
        blind = jnp.where(sees, new, -LOW)
        decay = jnp.exp(old - new)
        total = r.l_s[group] * decay
        grown = r.acc[group] * decay
        for b in range(4):
            w = jnp.exp(scores[b] - (new if masked[b] else blind))
            total = total + jnp.sum(w, axis=0, keepdims=True)
            added = dot(r.kvall[4 * p + b, 1, :, tile], w.astype(BF16), TN)
            grown = grown + added[HEAD * (group % 2) : HEAD * (group % 2) + HEAD]
        r.l_s[group] = total
        r.acc[group] = grown

    def send_att(group):
        part = r.att_all.at[ep, :, pl.ds(128 * group, 128)]
        return swap(5 + group, part, part)

    def settle(group):
        r.lse[group] = r.m_s[group] + jnp.log(r.l_s[group])
        done = r.acc[group] / r.l_s[group]
        attended = jnp.concatenate([done[:, :block], done[:, block:]], axis=0).T
        tile = slice(128 * group, 128 * group + 128)
        r.att[:, tile] = attended
        r.att_all[ep, :, tile] = attended.astype(BF16)
        send_att(group).start()

    def plane_forward(turn, carry):
        p = z - turn

        def heads(group):
            @pl.when(turn == 0)
            def _():
                head_step(p, group, (True,) * 4)

            @pl.when((turn > 0) & (p > 0))
            def _():
                head_step(p, group, (False,) * 4)

            @pl.when((turn > 0) & (p == 0))
            def _():
                head_step(p, group, (True, False, False, False))

            @pl.when(p == 0)
            def _():
                settle(group)

        heads(0)

        @pl.when(p > 0)
        def _():
            ring(block_of(p - 1, x, c), 0, 0, up).wait_recv()
            forward_own(p - 1, 0)

        heads(1)

        @pl.when(p > 0)
        def _():
            ring(block_of(p - 1, x, c), 1, 0, up).wait_recv()
            forward_own(p - 1, 1)

        heads(2)

        @pl.when(p > 0)
        def _():
            forward_across(p - 1, 0)

        heads(3)

        @pl.when(p > 0)
        def _():
            forward_across(p - 1, 1)
            arrive_beside(p - 1)

        return carry

    lax.fori_loop(0, z + 1, plane_forward, 0)

    def ring_drain(p, carry):
        for side in (0, 1):

            @pl.when(z < planes - 1)
            def _():
                ring(block_of(p, x, c), side, 0, up).wait_send()

            ring(block_of(p, x, c), side, 1, across).wait_send()
            ring(block_of(p, x, c), side, 2, beside).wait_send()
            ring(block_of(p, 1 - x, c), side, 2, beside).wait_send()
        return carry

    send_ow.wait_recv()
    send_od.wait_recv()

    def half_product(index, carry):
        which = jnp.where(index == 0, ep, 1 - ep)

        @pl.when(index == 1)
        def _():
            for group in range(4):
                send_att(group).wait_recv()

        r.halves[which] = dot(r.att_all[which], r.ow_all[which])
        r.half_mid[which] = dot(r.att_all[which], r.od_all[which], NT)
        return carry

    lax.fori_loop(0, 2, half_product, 0)
    mid_o = ((r.half_mid[0] + r.half_mid[1]) * r.mask[:, :SPAN]).astype(BF16)
    r.mid_o[...] = mid_o
    x2 = r.x_all[...].astype(F32) + (r.halves[0] + r.halves[1]) + dot(mid_o, r.o_up[...])
    r.x2[...] = x2
    h2 = rms(x2, r.moe_gain[...]).astype(BF16)
    r.h2[...] = h2
    send_hot.wait_recv()
    logits = dot(h2, r.router[...], NT)
    chosen = r.hot_all[:, : 2 * experts].astype(F32) > 0.5
    logits = jnp.where(chosen, logits, LOW)
    grown = jnp.where(chosen, jnp.exp(logits - jnp.max(logits, axis=1, keepdims=True)), 0.0)
    gates = grown / jnp.sum(grown, axis=1, keepdims=True)
    r.gates[...] = gates
    r.acc_out[...] = jnp.zeros(r.acc_out.shape, F32)
    r.acc_h2[...] = jnp.zeros(r.acc_h2.shape, F32)
    r.dgates[...] = jnp.zeros(r.dgates.shape, F32)
    lanes = 2 * SPAN
    load_in_down.wait()
    load_out_up.wait()
    send_g.wait_recv()
    in_down = r.in_down[...].reshape(experts * lanes, -1)
    out_up = r.out_up[...].reshape(experts * SPAN, -1)
    all_mids = dot(h2, in_down, NT)
    all_lifted = dot(r.g_all[...], out_up, NT)
    for e in range(experts):
        r.mid_in[e] = (all_mids[:, lanes * e : lanes * e + lanes] * r.mask[:, :lanes]).astype(BF16)
        r.lifted[e] = (all_lifted[:, SPAN * e : SPAN * e + SPAN] * r.mask[:, :SPAN]).astype(BF16)

    quarter = 2 * x + c

    def to_core(half, column):
        return remote(
            r.pack.at[half, 2 * column + 1 - c], r.core_land.at[half, column],
            r.core_send.at[half, column], r.core_recv.at[half, column], beside,
        )

    def to_column(half):
        return remote(
            r.pack.at[half, 2 * (1 - x) + c], r.x_land.at[half], r.x_send.at[half], r.x_recv.at[half], across
        )

    def add_core(half, column):
        to_core(half, column).wait_recv()
        number = 2 * column + c
        r.pack[half, number] = (
            r.pack[half, number].astype(F32) + r.core_land[half, column].astype(F32)
        ).astype(BF16)

    def final_rows(half, number):
        return (2 * number + half) * grad_rows

    def piece_of(owner):
        return (
            pl.multiple_of(owner // 4 * piece[0], piece[0]),
            pl.multiple_of(owner % 4 * piece[1], piece[1]),
        )

    def piece_in_pack(half, owner):
        row, lane = piece_of(owner)
        return r.pack.at[half, quarter, pl.ds(row, piece[0]), pl.ds(lane, piece[1])]

    def piece_in_final(half, owner):
        row, lane = piece_of(owner)
        start = pl.multiple_of(final_rows(half, quarter) + row, 16)
        return r.out.at[pl.ds(start, piece[0]), pl.ds(lane, piece[1])]

    def plane_of(step):
        return lax.rem(z + step, planes)

    def give(half, step):
        other = plane_of(step)
        return remote(
            piece_in_pack(half, other), r.z_land.at[half, z], r.z_send.at[half, 0, other],
            r.z_recv.at[half, 0, z], {"ctx": block_of(other, x, c), "ep": ep},
        )

    def take(half, step):
        other = plane_of(step)
        return remote(
            piece_in_pack(half, 0), r.z_land.at[half, other], r.z_send.at[half, 0, other],
            r.z_recv.at[half, 0, other], {"ctx": block_of(other, x, c), "ep": ep},
        )

    def spread(half, step):
        other = plane_of(step)
        part = piece_in_final(half, z % owners)
        return remote(
            part, part, r.z_send.at[half, 1, other], r.z_recv.at[half, 1, z],
            {"ctx": block_of(other, x, c), "ep": ep},
        )

    def gather(half, step):
        other = plane_of(step)
        part = piece_in_final(half, other)
        return remote(
            part, part, r.z_send.at[half, 1, other], r.z_recv.at[half, 1, other],
            {"ctx": block_of(other, x, c), "ep": ep},
        )

    def each_plane(act, among_owners):
        def step(number, carry):
            if among_owners and owners < planes:

                @pl.when(plane_of(number) < owners)
                def _():
                    act(number)

            else:
                act(number)
            return carry

        lax.fori_loop(1, planes, step, 0)

    def if_owner(act):
        if owners < planes:
            pl.when(z < owners)(act)
        else:
            act()

    def over_final(half, number, way, target):
        part = r.out.at[pl.ds(pl.multiple_of(final_rows(half, number), 16), grad_rows)]
        return remote(part, part, r.last_send.at[half, way, number], r.last_recv.at[half, number], target)

    def stage_pieces(half):
        to_column(half).wait_recv()
        r.pack[half, quarter] = (
            r.pack[half, quarter].astype(F32) + r.x_land[half].astype(F32)
        ).astype(BF16)
        each_plane(lambda step: give(half, step).start(), True)

    def stage_own(half):
        def act():
            each_plane(lambda step: take(half, step).wait_recv(), False)
            r.z_land[half, z] = piece_in_pack(half, z % owners)[...]

            def add(p, total):
                return total + r.z_land[half, p].astype(F32)

            total = lax.fori_loop(0, planes, add, jnp.zeros(piece, F32))
            piece_in_final(half, z % owners)[...] = total.astype(BF16)
            each_plane(lambda step: spread(half, step).start(), False)

        if_owner(act)

    def stage_column(half):
        each_plane(lambda step: gather(half, step).wait_recv(), True)
        over_final(half, quarter, 0, across).start()
        over_final(half, quarter, 1, beside).start()

    def stage_core(half):
        over_final(half, 2 * (1 - x) + c, 0, across).wait_recv()
        over_final(half, 2 * (1 - x) + c, 1, beside).start()

    def stage_end(half):
        over_final(half, 2 * x + 1 - c, 1, beside).wait_recv()
        over_final(half, 2 * (1 - x) + 1 - c, 1, beside).wait_recv()
        each_plane(lambda step: give(half, step).wait_send(), True)
        if_owner(lambda: each_plane(lambda step: spread(half, step).wait_send(), False))
        over_final(half, quarter, 0, across).wait_send()
        over_final(half, quarter, 1, beside).wait_send()
        over_final(half, 2 * (1 - x) + c, 1, beside).wait_send()
        to_core(half, 0).wait_send()
        to_core(half, 1).wait_send()
        to_column(half).wait_send()

    def one(turn, carry):
        slot = turn % slots
        e = expert_at(turn)
        half, q = turn // 4, quarter_at(turn % 4)
        for copy in expert_loads(turn):
            copy.wait()
        h2, g = r.h2[...], r.g_all[...]
        gate = jnp.sum(
            jnp.where(iota((block, 2 * experts), 1) == e + ep * experts, r.gates[...], 0.0), axis=1, keepdims=True
        )
        mid_in, lifted = r.mid_in[e], r.lifted[e]
        gate_part = dot(h2, r.w_in[slot, :, :FF]) + dot(mid_in[:, :SPAN], r.w_in_up[slot, 0])
        up_part = dot(h2, r.w_in[slot, :, FF:]) + dot(mid_in[:, SPAN:], r.w_in_up[slot, 1])
        d_act = dot(g, r.w_out[slot], NT) + dot(lifted, r.w_out_down[slot])
        squash = 1.0 / (1.0 + jnp.exp(-gate_part))
        silu = gate_part * squash
        act = (silu * up_part).astype(BF16)
        mid_out = dot(act, r.w_out_down[slot], NT) * r.mask[:, :SPAN]
        d_gate = jnp.sum(act.astype(F32) * d_act, axis=1, keepdims=True)
        r.dgates[...] += jnp.where(iota(r.dgates.shape, 1) == e, d_gate, 0.0)
        d_act = d_act * gate
        d_up = (d_act * silu).astype(BF16)
        d_gp = (d_act * up_part * squash * (1.0 + gate_part * (1.0 - squash))).astype(BF16)
        d_mid_in = (
            jnp.concatenate([dot(d_gp, r.w_in_up[slot, 0], NT), dot(d_up, r.w_in_up[slot, 1], NT)], axis=1)
            * r.mask[:, :lanes]
        ).astype(BF16)
        scaled_mid = (mid_out * gate).astype(BF16)
        r.d_mid_in[e] = d_mid_in
        r.mid_out[e] = scaled_mid
        r.acc_out[...] += dot((act.astype(F32) * gate).astype(BF16), r.w_out[slot])
        r.acc_h2[...] += dot(d_gp, r.w_in[slot, :, :FF], NT) + dot(d_up, r.w_in[slot, :, FF:], NT)
        r.pack[half, q, :64, :] = dot(d_mid_in, h2, TN).astype(BF16)
        r.pack[half, q, 64:96, :FF] = dot(mid_in[:, :SPAN], d_gp, TN).astype(BF16)
        r.pack[half, q, 64:96, FF:] = dot(mid_in[:, SPAN:], d_up, TN).astype(BF16)
        r.pack[half, q, 96:112, :] = fold(
            dot((lifted.astype(F32) * gate).astype(BF16), act, TN)
        ).astype(BF16)
        r.pack[half, q, 112:, :] = dot(scaled_mid, g, TN).astype(BF16)

        @pl.when(turn + slots < experts)
        def _():
            for copy in expert_loads(turn + slots):
                copy.start()

        @pl.when(turn % 4 == 0)
        def _():
            to_core(half, 1 - x).start()

        @pl.when(turn % 4 == 1)
        def _():
            to_core(half, x).start()

        @pl.when(turn % 4 == 2)
        def _():
            add_core(half, 1 - x)
            to_column(half).start()

        @pl.when(turn % 4 == 3)
        def _():
            add_core(half, x)

        @pl.when(turn == 5)
        def _():
            stage_pieces(0)

        return carry

    lax.fori_loop(0, experts, one, 0)
    every = range(experts)
    r.acc_h2[...] += dot(jnp.concatenate([r.d_mid_in[e] for e in every], axis=1), r.in_down[...].reshape(experts * lanes, -1))

    r.dg_trade[ep] = r.dgates[...].T[:8]
    send_dg = swap(9, r.dg_trade.at[ep], r.dg_trade.at[ep])
    send_dg.start()
    r.trade[ep] = r.acc_h2[...].astype(BF16)
    send_h2 = swap(10, r.trade.at[ep], r.trade.at[ep])
    send_h2.start()
    r.acc_out[...] += dot(jnp.concatenate([r.mid_out[e] for e in every], axis=1), r.out_up[...].reshape(experts * SPAN, -1))
    r.out_trade[0] = r.acc_out[theirs, :].astype(BF16)
    send_out = swap(11, r.out_trade.at[0], r.out_trade.at[1])
    send_out.start()
    stage_own(0)
    stage_pieces(1)

    def small_sum(number, source, landing, result):
        tiles = source.shape[0] // 16
        width = landing.shape[2]
        each = source.shape[1] // width
        holders = tiles * each

        def region(ref, owner):
            return ref.at[span(owner // each * 16, 16), span(owner % each * width, width)]

        def other(step):
            return lax.rem(me + step, blocks)

        def to_owner(step):
            owner = other(step)
            return remote(
                region(source, owner), landing.at[me], r.small_send.at[number, 0, owner],
                r.small_recv.at[number, 0, me], {"ctx": owner, "ep": ep},
            )

        def from_all(step):
            device = other(step)
            return remote(
                region(source, me % holders), landing.at[device], r.small_send.at[number, 0, device],
                r.small_recv.at[number, 0, device], {"ctx": device, "ep": ep},
            )

        def to_all(step):
            device = other(step)
            part = region(result, me % holders)
            return remote(
                part, part, r.small_send.at[number, 1, device], r.small_recv.at[number, 1, me],
                {"ctx": device, "ep": ep},
            )

        def from_owner(step):
            owner = other(step)
            part = region(result, owner)
            return remote(
                part, part, r.small_send.at[number, 1, owner], r.small_recv.at[number, 1, owner],
                {"ctx": owner, "ep": ep},
            )

        def loop(act, mine_too):
            def step(index, carry):
                if mine_too:
                    act(index)
                else:

                    @pl.when(other(index) < holders)
                    def _():
                        act(index)

                return carry

            lax.fori_loop(1, blocks, step, 0)

        def scatter():
            loop(lambda step: to_owner(step).start(), False)

        def total():
            @pl.when(me < holders)
            def _():
                loop(lambda step: from_all(step).wait_recv(), True)
                landing[me] = region(source, me % holders)[...]

                def add(p, sums):
                    return sums + landing[p].astype(F32)

                sums = lax.fori_loop(0, blocks, add, jnp.zeros(landing.shape[1:], F32))
                region(result, me % holders)[...] = sums.astype(BF16)
                loop(lambda step: to_all(step).start(), True)

        def finish():
            loop(lambda step: from_owner(step).wait_recv(), False)
            loop(lambda step: to_owner(step).wait_send(), False)

            @pl.when(me < holders)
            def _():
                loop(lambda step: to_all(step).wait_send(), True)

        return scatter, total, finish

    early_scatter, early_total, early_finish = small_sum(0, r.early, r.early_land, r.early_out)
    late_scatter, late_total, late_finish = small_sum(1, r.late, r.late_land, r.late_out)

    lax.fori_loop(0, z + 1, ring_drain, 0)

    send_dg.wait_recv()
    blank = jnp.zeros((112, block), F32)
    table = jnp.concatenate([r.dg_trade[0], r.dg_trade[1], blank], axis=0).T
    d_gates = table[:, : 2 * experts]
    gates = r.gates[...]
    d_logits = (gates * (d_gates - jnp.sum(gates * d_gates, axis=1, keepdims=True))).astype(BF16)
    from_router = dot(d_logits, r.router[...])
    stage_column(0)
    send_h2.wait_recv()
    d_h2 = r.trade[0].astype(F32) + r.trade[1].astype(F32) + from_router
    d_x2 = r.g_all[...].astype(F32) + rms_back(r.x2[...], r.moe_gain[...], d_h2)
    d_attn = d_x2.astype(BF16)
    r.acc_h2[...] = d_x2
    d_mid_o = (dot(d_attn, r.o_up[...], NT) * r.mask[:, :SPAN]).astype(BF16)

    d_att = (dot(d_attn, r.ow_all[ep], NT) + dot(d_mid_o, r.od_all[ep])).astype(BF16).astype(F32)
    pad_query(d_att, r.dn)
    pad_query_t(d_att.T, r.dt)
    product = (d_att * r.att[...]).T
    for group in range(4):
        for side in (0, 1):
            first = 128 * group + 64 * side
            r.delta[group, :, side * block : side * block + block] = jnp.sum(
                product[first : first + 64], axis=0, keepdims=True
            )
    r.dqt[...] = jnp.zeros(r.dqt.shape, F32)
    r.early[:32, :] = dot(r.mid_o[...], d_attn, TN).astype(BF16)
    r.early[32:48, :] = fold(dot(d_mid_o, r.att_all[ep], TN)).astype(BF16)
    r.early[48:, :] = jnp.zeros((16, r.early.shape[1]), BF16)
    early_scatter()
    stage_own(1)

    def block_step(number, masked):
        new_k, new_v = [], []
        for group in range(4):
            tile = slice(128 * (group // 2), 128 * (group // 2) + 128)
            keys = r.kvall[number, 0, :, tile]
            s = dot(keys, r.qt[group])
            base = r.lse[group]
            if masked:
                key = number * block + iota(s.shape, 0)
                w = jnp.where((key <= pos_row) & (key >= start_row), jnp.exp(s - base), 0.0)
            else:
                w = jnp.exp(s - jnp.where(start_row <= number * block, base, -LOW))
            d_w = dot(r.kvall[number, 1, :, tile], r.dt[group])
            d_s = (w * (d_w - r.delta[group])).astype(BF16)
            new_k.append(dot(d_s, r.qn[group]))
            new_v.append(dot(w.astype(BF16), r.dn[group]))
            r.dqt[group] += dot(keys, d_s, TN)[HEAD * (group % 2) : HEAD * (group % 2) + HEAD]
        for side in (0, 1):
            tile = slice(128 * side, 128 * side + 128)
            r.kvall[number, 0, :, tile] = ((new_k[2 * side] + new_k[2 * side + 1]) * SCALE).astype(BF16)
            r.kvall[number, 1, :, tile] = (new_v[2 * side] + new_v[2 * side + 1]).astype(BF16)

    def compute(number):
        edge = (number == 0) | (number == me)

        @pl.when(edge)
        def _():
            block_step(number, True)

        @pl.when((number < me) & jnp.logical_not(edge))
        def _():
            block_step(number, False)

        @pl.when(number > me)
        def _():
            r.kvall[number] = jnp.zeros(r.kvall.shape[1:], BF16)

    def to_beside(p, column):
        return remote(
            r.kvall.at[block_of(p, column, 1 - c)], r.from_beside.at[p % kept, column],
            r.beside_send.at[p, column], r.beside_recv.at[p, column], beside,
        )

    def over(p):
        return remote(
            r.kvall.at[block_of(p, 1 - x, c)], r.from_across.at[p % kept], r.across_send.at[p], r.across_recv.at[p], across
        )

    def lower(p):
        return remote(r.kvall.at[block_of(p, x, c)], r.from_up.at[p % kept], r.down_send.at[p], r.down_recv.at[p], down)

    def claim(p, number):
        if planes > kept:

            @pl.when(p >= kept)
            def _():
                pl.semaphore_wait(r.credit.at[number], 1)

    def release(p):
        if planes > kept:

            @pl.when(p + kept <= z)
            def _():
                pl.semaphore_signal(r.credit.at[0], inc=1, device_id=beside, device_id_type=MESH)
                pl.semaphore_signal(r.credit.at[1], inc=1, device_id=across, device_id_type=MESH)

            @pl.when((p + kept <= z) & (z < planes - 1))
            def _():
                pl.semaphore_signal(r.credit.at[2], inc=1, device_id=up, device_id_type=MESH)

    def finish(p):
        number = block_of(p, x, c)
        over(p).wait_recv()
        total = (
            r.kvall[number].astype(F32) + r.from_beside[p % kept, x].astype(F32) + r.from_across[p % kept].astype(F32)
        )
        r.kvall[number] = total.astype(BF16)

        @pl.when(z < planes - 1)
        def _():
            lower(p).wait_recv()
            r.kvall[number] = (total + r.from_up[p % kept].astype(F32)).astype(BF16)

        release(p)

        @pl.when(p < z)
        def _():
            claim(p, 2)
            lower(p).start()

    def plane_back(p, carry):
        @pl.when(p <= z)
        def _():
            compute(block_of(p, 1 - x, 1 - c))
            claim(p, 0)
            to_beside(p, 1 - x).start()
            compute(block_of(p, 1 - x, c))
            to_beside(p, 1 - x).wait_recv()
            number = block_of(p, 1 - x, c)
            r.kvall[number] = (r.kvall[number].astype(F32) + r.from_beside[p % kept, 1 - x].astype(F32)).astype(BF16)
            claim(p, 1)
            over(p).start()
            compute(block_of(p, x, 1 - c))
            to_beside(p, x).start()

            @pl.when(p > 0)
            def _():
                finish(p - 1)

            compute(block_of(p, x, c))
            to_beside(p, x).wait_recv()

        @pl.when(p == 0)
        def _():
            stage_column(1)
            stage_core(0)

        @pl.when(p == 1)
        def _():
            early_total()

        @pl.when(p == 2)
        def _():
            stage_core(1)

        return carry

    lax.fori_loop(0, planes, plane_back, 0)
    finish(z)

    cosine, sine = r.cosine[...], r.sine[...]
    parts = []
    for group in range(4):
        both = r.dqt[group]
        parts += [both[:, :block], both[:, block:]]
    d_query = jnp.concatenate(parts, axis=0).T * SCALE
    d_q = rotate(d_query.astype(BF16).astype(F32), cosine, sine, -1.0).astype(BF16)
    d_k = rotate(r.kvall[me, 0].astype(F32), cosine, sine, -1.0).astype(BF16)
    d_value = r.kvall[me, 1]
    r.mid_trade[ep] = jnp.concatenate(
        [dot(d_q, r.q_up[...], NT), dot(d_k, r.kv_up[0], NT), dot(d_value, r.kv_up[1], NT)], axis=1
    ).astype(BF16)
    send_mid = swap(12, r.mid_trade.at[ep], r.mid_trade.at[ep])
    send_mid.start()
    full = dot(d_q, r.q_w[...], NT) + dot(d_k, r.kv_w[0], NT) + dot(d_value, r.kv_w[1], NT)
    first, second = full[:rows], full[rows:]
    r.norm_trade[0] = jnp.where(ep == 0, second, first).astype(BF16)
    send_norm = swap(13, r.norm_trade.at[0], r.norm_trade.at[1])
    send_norm.start()
    r.late[96:112, :] = fold(dot(r.mids[:, :SPAN], d_q, TN)).astype(BF16)
    r.late[112:, :] = fold(
        jnp.concatenate(
            [dot(r.mids[:, SPAN : 2 * SPAN], d_k, TN), dot(r.mids[:, 2 * SPAN :], d_value, TN)], axis=1
        )
    ).astype(BF16)
    send_mid.wait_recv()
    d_mids = (
        (r.mid_trade[0].astype(F32) + r.mid_trade[1].astype(F32)) * r.mask[:, : 3 * SPAN]
    ).astype(BF16)
    r.late[:96, :] = dot(d_mids, r.h1[...], TN).astype(BF16)
    late_scatter()
    send_out.wait_recv()
    r.block_out[...] = (r.x2[mine, :] + (r.acc_out[mine, :] + r.out_trade[1].astype(F32))).astype(BF16)
    from_mids = dot(d_mids, r.qkv_down[...])
    own = jnp.where(ep == 0, first + from_mids[:rows], second + from_mids[rows:])
    send_norm.wait_recv()
    own = own + r.norm_trade[1].astype(F32)
    r.in_grad[...] = (
        r.acc_h2[mine, :] + rms_back(r.x_all[mine, :].astype(F32), r.attn_gain[...], own)
    ).astype(BF16)
    late_total()
    early_finish()
    stage_end(0)
    stage_end(1)

    for copy in (send_x, send_ow, send_od, send_hot, send_g, send_dg, send_h2, send_out, send_mid, send_norm):
        copy.wait_send()
    for group in range(4):
        send_att(group).wait_send()

    def drain(p, carry):
        for side in (0, 1):
            to_beside(p, side).wait_send()
        over(p).wait_send()

        @pl.when(p < z)
        def _():
            lower(p).wait_send()

        return carry

    lax.fori_loop(0, z + 1, drain, 0)
    late_finish()


RESULTS = (
    "ein_down", "ein_up", "eout_down", "eout_up", "block_out", "in_grad", "g_down", "g_q", "g_kv", "g_od", "g_ou",
)


def unpack_kernel(packed, *refs):
    count = len(RESULTS)
    outs = dict(zip(RESULTS, refs[:count]))
    held = dict(zip(RESULTS, refs[count : 2 * count]))
    rows, sem_in, sem_out = refs[2 * count :]
    experts = outs["ein_down"].shape[0]
    grad_rows = 144
    base = experts * grad_rows

    def fetch(start, size, number):
        return pltpu.make_async_copy(
            packed.at[pl.ds(start, size)], rows.at[pl.ds(start, size)], sem_in.at[number]
        )

    fetches = [fetch(grad_rows * e, grad_rows, e) for e in range(experts)]
    fetches.append(fetch(base, rows.shape[0] - base, experts))
    for copy in fetches:
        copy.start()
    stores = []

    def store(name, number):
        copy = pltpu.make_async_copy(
            held[name] if number is None else held[name].at[number],
            outs[name] if number is None else outs[name].at[number],
            sem_out.at[len(stores)],
        )
        copy.start()
        stores.append(copy)

    for e in range(experts):
        fetches[e].wait()
        part = rows[grad_rows * e : grad_rows * e + grad_rows, :].astype(F32)
        held["ein_down"][e] = part[:64]
        held["ein_up"][e, 0] = part[64:96, :FF]
        held["ein_up"][e, 1] = part[64:96, FF:]
        held["eout_down"][e, :16] = part[96:112, :FF]
        held["eout_down"][e, 16:] = part[96:112, FF:]
        held["eout_up"][e] = part[112:]
        for name in RESULTS[:4]:
            store(name, e)
    fetches[experts].wait()
    late = rows[base : base + 128, :].astype(F32)
    early = rows[base + 384 : base + 448, :].astype(F32)
    held["block_out"][...] = rows[base + 128 : base + 256, :]
    held["in_grad"][...] = rows[base + 256 : base + 384, :]
    held["g_down"][...] = late[:96]
    held["g_q"][:16, :] = late[96:112, :FF]
    held["g_q"][16:, :] = late[96:112, FF:]
    kv = FF // 2
    for side in (0, 1):
        for half in (0, 1):
            first = kv * (2 * half + side)
            held["g_kv"][side, 16 * half : 16 * half + 16, :] = late[112:, first : first + kv]
    held["g_od"][:16, :] = early[32:48, :FF]
    held["g_od"][16:, :] = early[32:48, FF:]
    held["g_ou"][...] = early[:32]
    for name in RESULTS[4:]:
        store(name, None)
    for copy in stores:
        copy.wait()


def per_device(
    resid_in, out_grad, attn_gain, q_weight, key_value_weight, o_weight, moe_gain, router, expert_in,
    expert_out, qkv_down, q_up, key_value_up_factor, o_down, o_up, expert_in_down, expert_in_up,
    expert_out_down, expert_out_up, expert_ids, doc_starts, doc_adapter,
):
    blocks = lax.axis_size("ctx")
    planes = blocks // 4
    rows, width = resid_in.shape
    block = 2 * rows
    heads = q_weight.shape[1]
    kv = key_value_weight.shape[2]
    experts = expert_in.shape[0]
    slots = 4 if planes <= 4 else 2
    kept = planes if planes <= 4 else 2
    grad_rows = 2 * SPAN + SPAN + SPAN // 2 + SPAN
    base = experts * grad_rows
    groups = 3 if planes >= 12 else 1
    piece = (grad_rows // groups, width // 4)
    early_width = max(128, 4 * width // blocks)
    late_width = max(128, 8 * width // blocks)
    freq = np.tile(np.power(10000.0, -2.0 * np.arange(HEAD // 2) / HEAD).astype(np.float32), 4)[None, :]

    def shape(dims, kind=BF16):
        return jax.ShapeDtypeStruct(dims, kind)

    def dma(*dims):
        return pltpu.SemaphoreType.DMA(dims)

    def low(*dims):
        return pltpu.VMEM(dims, BF16)

    def full(*dims):
        return pltpu.VMEM(dims, F32)

    operands = dict(
        resid=resid_in, grad=out_grad, ids=expert_ids.T, starts=doc_starts, adapters=doc_adapter,
        attn_gain=attn_gain[None, :], moe_gain=moe_gain[None, :], freq=jnp.asarray(freq), qkv_down=qkv_down.T,
        q_up=q_up, kv_up=key_value_up_factor, o_down=o_down.T, o_up=o_up, router=router.T, q_hbm=q_weight,
        kv_hbm=key_value_weight, o_hbm=o_weight, in_hbm=expert_in, out_hbm=expert_out,
        in_down_hbm=jnp.swapaxes(expert_in_down, 1, 2), in_up_hbm=expert_in_up,
        out_down_hbm=jnp.swapaxes(expert_out_down, 1, 2), out_up_hbm=expert_out_up,
    )
    results = dict(out=shape((base + 448, width)))
    scratch = dict(
        q_w=low(*q_weight.shape), kv_w=low(*key_value_weight.shape), ow_all=low(2, heads, width),
        od_all=low(2, SPAN, heads), w_in=low(slots, *expert_in.shape[1:]), w_out=low(slots, *expert_out.shape[1:]),
        in_down=low(experts, 2 * SPAN, width), w_in_up=low(slots, *expert_in_up.shape[1:]),
        w_out_down=low(slots, SPAN, FF), out_up=low(experts, SPAN, width),
        mid_in=low(experts, block, 2 * SPAN), lifted=low(experts, block, SPAN),
        d_mid_in=low(experts, block, 2 * SPAN), mid_out=low(experts, block, SPAN),
        x_all=low(block, width), g_all=low(block, width), h1=low(block, width), h2=low(block, width),
        hot_all=low(block, 128), mask=full(block, 128), cosine=full(block, 128), sine=full(block, 128),
        mids=low(block, 3 * SPAN), kvall=low(blocks, 2, block, kv), qt=low(4, 128, 2 * block),
        qn=low(4, 2 * block, 128), dt=low(4, 128, 2 * block), dn=low(4, 2 * block, 128),
        m_s=full(4, 1, 2 * block), l_s=full(4, 1, 2 * block), lse=full(4, 1, 2 * block),
        delta=full(4, 1, 2 * block), acc=full(4, HEAD, 2 * block), dqt=full(4, HEAD, 2 * block),
        att=full(block, heads), att_all=low(2, block, heads), halves=full(2, block, width), half_mid=full(2, block, SPAN), mid_o=low(block, SPAN), x2=full(block, width),
        gates=full(block, 2 * experts), dgates=full(block, 128), trade=low(2, block, width), out_trade=low(2, rows, width),
        norm_trade=low(2, rows, width), mid_trade=low(2, block, 3 * SPAN), dg_trade=full(2, 8, block),
        pack=low(2, 4, grad_rows, width), core_land=low(2, 2, grad_rows, width), x_land=low(2, grad_rows, width),
        z_land=low(2, planes, *piece), early=low(64, width), late=low(128, width),
        early_land=low(blocks, 16, early_width), late_land=low(blocks, 16, late_width),
        from_beside=low(kept, 2, 2, block, kv), from_across=low(kept, 2, block, kv),
        from_up=low(kept, 2, block, kv), credit=pltpu.SemaphoreType.REGULAR((3,)),
        load_sem=dma(5), expert_sem=dma(slots, 4), pair_send=dma(14), pair_recv=dma(14),
        ring_send=dma(3, blocks, 2), ring_recv=dma(blocks, 2), core_send=dma(2, 2), core_recv=dma(2, 2),
        x_send=dma(2), x_recv=dma(2), z_send=dma(2, 2, planes), z_recv=dma(2, 2, planes), last_send=dma(2, 2, 4),
        last_recv=dma(2, 4),
        small_send=dma(2, 2, blocks), small_recv=dma(2, 2, blocks), beside_send=dma(planes, 2),
        beside_recv=dma(planes, 2), across_send=dma(planes), across_recv=dma(planes), down_send=dma(planes),
        down_recv=dma(planes),
    )
    (out,) = pl.pallas_call(
        functools.partial(layer_kernel, planes, slots, INPUTS + OUTPUTS + tuple(scratch)),
        out_shape=[results[name] for name in OUTPUTS],
        in_specs=[
            SMEM if name in ("starts", "adapters") else HBM if name.endswith("hbm") else VMEM for name in INPUTS
        ],
        out_specs=[VMEM] * len(OUTPUTS),
        scratch_shapes=list(scratch.values()),
        compiler_params=pltpu.CompilerParams(
            collective_id=1, has_side_effects=True, vmem_limit_bytes=62 << 20
        ),
        name="layer",
    )(*[operands[name] for name in INPUTS])

    unpacked = dict(
        ein_down=shape((experts, 2 * SPAN, width), F32), ein_up=shape((experts, 2, SPAN, FF), F32),
        eout_down=shape((experts, SPAN, FF), F32), eout_up=shape((experts, SPAN, width), F32),
        block_out=shape((rows, width)), in_grad=shape((rows, width)), g_down=shape((3 * SPAN, width), F32),
        g_q=shape((SPAN, heads), F32), g_kv=shape((2, SPAN, kv), F32), g_od=shape((SPAN, heads), F32),
        g_ou=shape((SPAN, width), F32),
    )
    ein_down, ein_up, eout_down, eout_up, block_out, in_grad, g_down, g_q, g_kv, g_od, g_ou = pl.pallas_call(
        unpack_kernel,
        out_shape=[unpacked[name] for name in RESULTS],
        in_specs=[HBM],
        out_specs=[HBM] * len(RESULTS),
        scratch_shapes=[
            *[pltpu.VMEM(unpacked[name].shape, unpacked[name].dtype) for name in RESULTS],
            pltpu.VMEM(out.shape, BF16), dma(experts + 1), dma(4 * experts + 7),
        ],
        compiler_params=pltpu.CompilerParams(vmem_limit_bytes=62 << 20),
        name="unpack",
    )(out)
    return (
        block_out, in_grad, g_down.T, g_q, g_kv, g_od.T, g_ou, jnp.swapaxes(ein_down, 1, 2), ein_up,
        jnp.swapaxes(eout_down, 1, 2), eout_up,
    )


def solution(mesh):
    placed = (
        P(("ctx", "ep"), None),
        P(("ctx", "ep"), None),
        P(),
        P(None, "ep"),
        P(None, None, "ep"),
        P("ep", None),
        P(),
        P(),
        P("ep", None, None),
        P("ep", None, None),
        P(),
        P(None, "ep"),
        P(None, None, "ep"),
        P("ep", None),
        P(),
        P("ep", None, None),
        P("ep", None, None, None),
        P("ep", None, None),
        P("ep", None, None),
        P(("ctx", "ep"), None),
        P(),
        P(),
    )
    return jax.shard_map(
        per_device,
        mesh=mesh,
        in_specs=placed,
        out_specs=(
            P(("ctx", "ep"), None),
            P(("ctx", "ep"), None),
            P(),
            P(None, "ep"),
            P(None, None, "ep"),
            P("ep", None),
            P(),
            P("ep", None, None),
            P("ep", None, None, None),
            P("ep", None, None),
            P("ep", None, None),
        ),
        check_vma=False,
    )
```

```python
import functools

import jax
import jax.numpy as jnp
import numpy as np
from jax import lax
from jax.experimental import pallas as pl
from jax.experimental.pallas import tpu as pltpu
from jax.sharding import PartitionSpec as P

MESH = pl.DeviceIdType.MESH
VMEM = pl.BlockSpec(memory_space=pltpu.VMEM)
SMEM = pl.BlockSpec(memory_space=pltpu.SMEM)
HBM = pl.BlockSpec(memory_space=pl.ANY)
F32 = jnp.float32
BF16 = jnp.bfloat16

HEAD = 64
FF = 512
RANK = 16
SPAN = 32
EPS = 1e-06
LOW = -1e30
SCALE = 0.125

NN = (((1,), (0,)), ((), ()))
NT = (((1,), (1,)), ((), ()))
TN = (((0,), (0,)), ((), ()))


def dot(left, right, dims=NN):
    return lax.dot_general(left, right, dims, preferred_element_type=F32)


def iota(shape, dim):
    return lax.broadcasted_iota(jnp.int32, shape, dim)


def rms(values, gain):
    return values * lax.rsqrt(jnp.mean(values * values, axis=-1, keepdims=True) + EPS) * gain


def rms_back(values, gain, upstream):
    factor = lax.rsqrt(jnp.mean(values * values, axis=-1, keepdims=True) + EPS)
    scaled = upstream * gain
    return factor * scaled - values * factor * factor * factor * jnp.mean(
        scaled * values, axis=-1, keepdims=True
    )


def rotate(values, cosine, sine, sign):
    width = values.shape[1]
    copies = width // 128
    cosine = jnp.concatenate([cosine] * copies, axis=1)
    sine = jnp.concatenate([sine] * copies, axis=1)
    first = iota(values.shape, 1) % HEAD < HEAD // 2
    ahead = pltpu.roll(values, width - HEAD // 2, 1)
    behind = pltpu.roll(values, HEAD // 2, 1)
    return values * cosine + sign * jnp.where(first, -ahead, behind) * sine


def doc_scan(positions, starts_ref, adapters_ref):
    own_start = jnp.zeros(positions.shape, jnp.int32)
    adapter = jnp.zeros(positions.shape, jnp.int32)
    for number in range(starts_ref.shape[0]):
        opened = starts_ref[number] <= positions
        own_start = jnp.where(opened, starts_ref[number], own_start)
        adapter = jnp.where(opened, adapters_ref[number], adapter)
    return own_start, adapter


def place():
    me = lax.axis_index("ctx")
    ep = lax.axis_index("ep")
    return me, ep, me // 4, (me // 2) % 2, me % 2


def block_of(z, x, c):
    return (z * 2 + x) * 2 + c


def signal(device):
    pl.semaphore_signal(
        pltpu.get_barrier_semaphore(), inc=1, device_id=device, device_id_type=MESH
    )


def remote(src, dst, send, recv, device):
    return pltpu.make_async_remote_copy(
        src_ref=src,
        dst_ref=dst,
        send_sem=send,
        recv_sem=recv,
        device_id=device,
        device_id_type=MESH,
    )


def span(start, count):
    return pl.ds(pl.multiple_of(start, count), count)


def stack_rows(piece, upper):
    turned = pltpu.roll(piece, HEAD, 1)
    keep = iota(piece.shape, 1) >= HEAD if upper else iota(piece.shape, 1) < HEAD
    first, second = (turned, piece) if upper else (piece, turned)
    blank = jnp.zeros(piece.shape, piece.dtype)
    return jnp.concatenate([jnp.where(keep, first, blank), jnp.where(keep, second, blank)], axis=0).astype(BF16)


def stack_columns(piece):
    turned = piece.T
    return jnp.concatenate([turned[:HEAD], turned[HEAD:]], axis=1)


def unstack(columns):
    count = columns.shape[1] // 2
    return jnp.concatenate([columns[:, :count], columns[:, count:]], axis=0).T


def fold(wide):
    count = wide.shape[0] // 2
    return jnp.concatenate([wide[:count], wide[count:]], axis=1)


INPUTS = (
    "resid", "grad", "ids", "starts", "adapters", "attn_gain", "moe_gain", "freq",
    "qkv_down", "q_up", "kv_up", "o_down", "o_up", "router",
    "q_hbm", "kv_hbm", "o_hbm", "in_hbm", "out_hbm", "in_down_hbm", "in_up_hbm", "out_down_hbm", "out_up_hbm",
)
OUTPUTS = ("out",)


def layer_kernel(planes, slots, names, *refs):
    r = dict(zip(names, refs))
    r = type("Refs", (), r)
    r.acc_out, r.acc_h2 = r.halves.at[0], r.halves.at[1]
    grad_rows = r.pack.shape[2]
    base = r.in_hbm.shape[0] * grad_rows
    r.late_out = r.out.at[pl.ds(base, 128)]
    r.block_out = r.out.at[pl.ds(base + 128, 128)]
    r.in_grad = r.out.at[pl.ds(base + 256, 128)]
    r.early_out = r.out.at[pl.ds(base + 384, 64)]
    me, ep, z, x, c = place()
    blocks = 4 * planes
    pair = {"ctx": me, "ep": 1 - ep}
    head = 2 * x + c
    up = {"ctx": jnp.minimum(me + 4, blocks - 1), "ep": ep}
    down = {"ctx": jnp.maximum(me - 4, 0), "ep": ep}
    across = {"ctx": block_of(z, 1 - x, c), "ep": ep}
    beside = {"ctx": block_of(z, x, 1 - c), "ep": ep}
    rows = r.resid.shape[0]
    block = 2 * rows
    mine = span(ep * rows, rows)
    theirs = span(rows - ep * rows, rows)
    experts = r.in_hbm.shape[0]
    groups = 3 if planes >= 12 else 1
    owners = 4 * groups
    piece = (grad_rows // groups, r.pack.shape[3] // 4)
    kept = r.from_up.shape[0]

    load_q = pltpu.make_async_copy(r.q_hbm, r.q_w, r.load_sem.at[0])
    load_kv = pltpu.make_async_copy(r.kv_hbm, r.kv_w, r.load_sem.at[1])
    load_o = pltpu.make_async_copy(r.o_hbm, r.ow_all.at[ep], r.load_sem.at[2])
    load_kv.start()
    load_q.start()
    load_o.start()
    load_in_down = pltpu.make_async_copy(r.in_down_hbm, r.in_down, r.load_sem.at[3])
    load_out_up = pltpu.make_async_copy(r.out_up_hbm, r.out_up, r.load_sem.at[4])
    load_in_down.start()
    load_out_up.start()
    weights = (
        (r.in_hbm, r.w_in), (r.out_hbm, r.w_out), (r.in_up_hbm, r.w_in_up), (r.out_down_hbm, r.w_out_down),
    )

    def quarter_at(turn):
        return jnp.where(turn % 2 == 0, 1 - x, x) * 2 + jnp.where(turn < 2, 1 - c, c)

    def expert_at(turn):
        return 2 * quarter_at(turn % 4) + turn // 4

    def expert_loads(turn):
        e, slot = expert_at(turn), turn % slots
        return [
            pltpu.make_async_copy(source.at[e], held.at[slot], r.expert_sem.at[slot, number])
            for number, (source, held) in enumerate(weights)
        ]

    def begin(turn, carry):
        for copy in expert_loads(turn):
            copy.start()
        return carry

    lax.fori_loop(0, slots, begin, 0)

    def greet(step, carry):
        signal({"ctx": lax.rem(me + step, blocks), "ep": ep})
        return carry

    for b in range(4):
        signal({"ctx": 4 * z + b, "ep": 1 - ep})
    lax.fori_loop(1, blocks, greet, 0)
    pl.semaphore_wait(pltpu.get_barrier_semaphore(), blocks + 3)

    def swap(number, src, dst):
        return remote(src, dst, r.pair_send.at[number], r.pair_recv.at[number], pair)

    send_x = swap(0, r.resid, r.x_all.at[mine])
    send_x.start()

    hot = jnp.zeros((r.ids.shape[0], rows), F32)
    hot = jnp.zeros((128, rows), F32)
    numbers = iota((128, rows), 0)
    for choice in range(r.ids.shape[0]):
        hot = hot + jnp.where(r.ids[choice : choice + 1, :] == numbers, 1.0, 0.0)
    r.hot_all[mine, :] = hot.T.astype(BF16)
    r.x_all[mine, :] = r.resid[...]
    r.g_all[mine, :] = r.grad[...]
    r.od_all[ep] = r.o_down[...]
    position = me * block + iota((block, 128), 0)
    own_start, adapter = doc_scan(position, r.starts, r.adapters)
    r.mask[...] = jnp.where((iota((block, 128), 1) % SPAN) // RANK == adapter, 1.0, 0.0)
    angles = (position - own_start).astype(F32) * r.freq[...]
    r.cosine[...] = jnp.cos(angles)
    r.sine[...] = jnp.sin(angles)
    pos_rows = [((4 * z + b) * block + iota((8, 2 * block), 1) % block)[:1] for b in range(4)]
    start_rows = [
        doc_scan((4 * z + b) * block + iota((8, 2 * block), 1) % block, r.starts, r.adapters)[0][:1] for b in range(4)
    ]

    halves = (mine, theirs)

    def other_head(step):
        return lax.rem(head + step, 4)

    def device_of(number):
        return {"ctx": 4 * z + number, "ep": ep}

    def kv_to(step, half):
        number = other_head(step)
        return remote(
            r.kv_out.at[number, halves[half], :], r.kvall.at[z, head, halves[half], :],
            r.kv_send.at[number, half], r.kv_recv.at[head, half], device_of(number),
        )

    def kv_from(step, half):
        number = other_head(step)
        return remote(
            r.kv_out.at[number, halves[half], :], r.kvall.at[z, number, halves[half], :],
            r.kv_send.at[number, half], r.kv_recv.at[number, half], device_of(number),
        )

    def piece_to(source, landing, sends, recvs, step):
        number = other_head(step)
        return remote(source.at[number], landing.at[head], sends.at[number], recvs.at[head], device_of(number))

    def piece_from(source, landing, sends, recvs, step):
        number = other_head(step)
        return remote(source.at[number], landing.at[number], sends.at[number], recvs.at[number], device_of(number))

    query_pieces = (r.q_out, r.q_in, r.q_send, r.q_recv)
    grad_pieces = (r.d_out, r.d_in, r.d_send, r.d_recv)

    def climb(p, half):
        part = r.kvall.at[p, :, halves[half], :]
        return remote(part, part, r.up_send.at[p, half], r.up_recv.at[p, half], up)

    def climb_on(p, half):
        @pl.when(z < planes - 1)
        def _():
            climb(p, half).start()

    def collect(half):
        for step in (1, 2, 3):
            kv_from(step, half).wait_recv()
        climb_on(z, half)

    def project(here):
        h1 = rms(r.x_all[here, :].astype(F32), r.attn_gain[...]).astype(BF16)
        r.h1[here, :] = h1
        mids = (dot(h1, r.qkv_down[...], NT) * r.mask[here, : 3 * SPAN]).astype(BF16)
        r.mids[here, :] = mids
        k_lin = dot(h1, r.kv_w[0]) + dot(mids[:, SPAN : 2 * SPAN], r.kv_up[0])
        keys = rotate(k_lin, r.cosine[here, :], r.sine[here, :], 1.0)
        values = dot(h1, r.kv_w[1]) + dot(mids[:, 2 * SPAN :], r.kv_up[1])
        for number in range(4):
            lanes = slice(HEAD * number, HEAD * number + HEAD)
            r.kv_out[number, here, :] = jnp.concatenate([keys[:, lanes], values[:, lanes]], axis=1).astype(BF16)
        r.kvall[z, head, here, :] = r.kv_out[head, here, :]

    load_kv.wait()
    project(mine)
    for step in (1, 2, 3):
        kv_to(step, 0).start()
    send_x.wait_recv()
    load_o.wait()

    def ow_quarter(side, number):
        return r.ow_all.at[side, pl.ds(pl.multiple_of(128 * number, 128), 128), :]

    def hand_on(number, way, target):
        part = ow_quarter(1 - ep, number)
        return remote(part, part, r.ow_send.at[number, way], r.ow_recv.at[number], target)

    sibling = 2 * (1 - x) + c

    def hand_first():
        send_ow.wait_recv()
        hand_on(head, 0, across).start()
        hand_on(head, 1, beside).start()

    def hand_second():
        hand_on(sibling, 0, across).wait_recv()
        hand_on(sibling, 1, beside).start()

    def hand_last():
        hand_on(2 * x + 1 - c, 1, beside).wait_recv()
        hand_on(2 * (1 - x) + 1 - c, 1, beside).wait_recv()

    send_ow = swap(3, ow_quarter(ep, head), ow_quarter(ep, head))
    send_od = swap(4, r.od_all.at[ep], r.od_all.at[ep])
    send_hot = swap(1, r.hot_all.at[mine], r.hot_all.at[mine])
    send_g = swap(2, r.grad, r.g_all.at[mine])
    for copy in (send_ow, send_od, send_hot):
        copy.start()
    project(theirs)
    for step in (1, 2, 3):
        kv_to(step, 1).start()
    load_q.wait()
    q_lin = dot(r.h1[...], r.q_w[...]) + dot(r.mids[:, :SPAN], r.q_up[...])
    query = rotate(q_lin, r.cosine[...], r.sine[...], 1.0).astype(BF16)
    for number in range(4):
        r.q_out[number] = query[:, 128 * number : 128 * number + 128]
    for step in (1, 2, 3):
        piece_to(*query_pieces, step).start()
    collect(0)
    send_g.start()
    hand_first()
    r.q_in[head] = r.q_out[head]
    r.m_s[...] = jnp.full(r.m_s.shape, LOW, F32)
    r.l_s[...] = jnp.zeros(r.l_s.shape, F32)
    r.acc[...] = jnp.zeros(r.acc.shape, F32)
    r.qt[:, HEAD:, :] = jnp.zeros((4, HEAD, 2 * block), BF16)
    r.dt[:, :HEAD, :] = jnp.zeros((4, HEAD, 2 * block), BF16)
    collect(1)
    for step in (1, 2, 3):
        piece_from(*query_pieces, step).wait_recv()
    for b in range(4):
        scaled = r.q_in[b].astype(F32) * SCALE
        r.qt[b, :HEAD, :] = stack_columns(scaled).astype(BF16)
        r.qn[b] = stack_rows(scaled, False)

    def attend_step(p, b, kinds):
        scores, peak = [], None
        pos_row, start_row = pos_rows[b], start_rows[b]
        sees = start_row <= (4 * p + 1) * block
        for kb, masked in kinds:
            s = dot(r.kvall[p, kb], r.qt[b])
            if masked:
                key = (4 * p + kb) * block + iota(s.shape, 0)
                s = jnp.where((key <= pos_row) & (key >= start_row), s, LOW)
            scores.append(s)
            highest = jnp.max(s, axis=0, keepdims=True)
            if not masked:
                highest = jnp.where(sees, highest, LOW)
            peak = highest if peak is None else jnp.maximum(peak, highest)
        old = r.m_s[b]
        new = jnp.maximum(old, peak)
        r.m_s[b] = new
        blind = jnp.where(sees, new, -LOW)
        decay = jnp.exp(old - new)
        total = r.l_s[b] * decay
        grown = r.acc[b] * decay
        for (kb, masked), s in zip(kinds, scores):
            w = jnp.exp(s - (new if masked else blind))
            total = total + jnp.sum(w, axis=0, keepdims=True)
            grown = grown + dot(r.kvall[p, kb], w.astype(BF16), TN)[HEAD:]
        r.l_s[b] = total
        r.acc[b] = grown

    def att_to(b, side):
        return remote(
            r.o_out.at[b], r.att_all.at[ep, :, pl.ds(pl.multiple_of(128 * head, 128), 128)],
            r.att_send.at[b, side], r.att_recv.at[ep, head], {"ctx": 4 * z + b, "ep": side},
        )

    def att_from(side, number):
        return remote(
            r.o_out.at[0], r.att_all.at[side, :, pl.ds(128 * number, 128)],
            r.att_send.at[0, 0], r.att_recv.at[side, number], {"ctx": 4 * z + number, "ep": side},
        )

    def settle(b):
        r.lse[b] = r.m_s[b] + jnp.log(r.l_s[b])
        done = r.acc[b] / r.l_s[b]
        r.acc[b] = done
        r.o_out[b] = unstack(done).astype(BF16)

        @pl.when(b == head)
        def _():
            r.att_all[ep, :, pl.ds(pl.multiple_of(128 * head, 128), 128)] = r.o_out[b]

        @pl.when(b != head)
        def _():
            att_to(b, ep).start()

        att_to(b, 1 - ep).start()

    def plane_forward(turn, carry):
        p = z - turn

        def steps(b):
            @pl.when(turn == 0)
            def _():
                attend_step(p, b, [(kb, kb in (0, b)) for kb in range(b + 1)])

            @pl.when((turn > 0) & (p > 0))
            def _():
                attend_step(p, b, [(kb, False) for kb in range(4)])

            @pl.when((turn > 0) & (p == 0))
            def _():
                attend_step(p, b, [(kb, kb == 0) for kb in range(4)])

            @pl.when(p == 0)
            def _():
                settle(b)

        def climbing(half):
            @pl.when(p > 0)
            def _():
                climb(p - 1, half).wait_recv()
                climb_on(p - 1, half)

        steps(3)
        climbing(0)
        steps(2)
        steps(1)
        climbing(1)

        @pl.when(turn == 0)
        def _():
            hand_second()

        steps(0)
        return carry

    lax.fori_loop(0, z + 1, plane_forward, 0)

    def drain_forward():
        for step in (1, 2, 3):
            kv_to(step, 0).wait_send()
            kv_to(step, 1).wait_send()
            piece_to(*query_pieces, step).wait_send()

        @pl.when(z < planes - 1)
        def _():
            def left(p, carry):
                climb(p, 0).wait_send()
                climb(p, 1).wait_send()
                return carry

            lax.fori_loop(0, z + 1, left, 0)

    hand_last()
    send_od.wait_recv()

    def half_product(index, carry):
        which = jnp.where(index == 0, ep, 1 - ep)

        for number in range(4):

            @pl.when((index == 1) | (number != head))
            def _():
                att_from(which, number).wait_recv()

        r.halves[which] = dot(r.att_all[which], r.ow_all[which])
        r.half_mid[which] = dot(r.att_all[which], r.od_all[which], NT)
        return carry

    lax.fori_loop(0, 2, half_product, 0)
    mid_o = ((r.half_mid[0] + r.half_mid[1]) * r.mask[:, :SPAN]).astype(BF16)
    r.mid_o[...] = mid_o
    x2 = r.x_all[...].astype(F32) + (r.halves[0] + r.halves[1]) + dot(mid_o, r.o_up[...])
    r.x2[...] = x2
    h2 = rms(x2, r.moe_gain[...]).astype(BF16)
    r.h2[...] = h2
    send_hot.wait_recv()
    logits = dot(h2, r.router[...], NT)
    chosen = r.hot_all[:, : 2 * experts].astype(F32) > 0.5
    logits = jnp.where(chosen, logits, LOW)
    grown = jnp.where(chosen, jnp.exp(logits - jnp.max(logits, axis=1, keepdims=True)), 0.0)
    gates = grown / jnp.sum(grown, axis=1, keepdims=True)
    r.gates[...] = gates
    r.acc_out[...] = jnp.zeros(r.acc_out.shape, F32)
    r.acc_h2[...] = jnp.zeros(r.acc_h2.shape, F32)
    r.dgates[...] = jnp.zeros(r.dgates.shape, F32)
    lanes = 2 * SPAN
    load_in_down.wait()
    load_out_up.wait()
    send_g.wait_recv()
    in_down = r.in_down[...].reshape(experts * lanes, -1)
    out_up = r.out_up[...].reshape(experts * SPAN, -1)
    all_mids = dot(h2, in_down, NT)
    all_lifted = dot(r.g_all[...], out_up, NT)
    for e in range(experts):
        r.mid_in[e] = (all_mids[:, lanes * e : lanes * e + lanes] * r.mask[:, :lanes]).astype(BF16)
        r.lifted[e] = (all_lifted[:, SPAN * e : SPAN * e + SPAN] * r.mask[:, :SPAN]).astype(BF16)

    quarter = 2 * x + c

    def to_core(half, column):
        return remote(
            r.pack.at[half, 2 * column + 1 - c], r.core_land.at[half, column],
            r.core_send.at[half, column], r.core_recv.at[half, column], beside,
        )

    def to_column(half):
        return remote(
            r.pack.at[half, 2 * (1 - x) + c], r.x_land.at[half], r.x_send.at[half], r.x_recv.at[half], across
        )

    def add_core(half, column):
        to_core(half, column).wait_recv()
        number = 2 * column + c
        r.pack[half, number] = (
            r.pack[half, number].astype(F32) + r.core_land[half, column].astype(F32)
        ).astype(BF16)

    def final_rows(half, number):
        return (2 * number + half) * grad_rows

    def piece_of(owner):
        return (
            pl.multiple_of(owner // 4 * piece[0], piece[0]),
            pl.multiple_of(owner % 4 * piece[1], piece[1]),
        )

    def piece_in_pack(half, owner):
        row, lane = piece_of(owner)
        return r.pack.at[half, quarter, pl.ds(row, piece[0]), pl.ds(lane, piece[1])]

    def piece_in_final(half, owner):
        row, lane = piece_of(owner)
        start = pl.multiple_of(final_rows(half, quarter) + row, 16)
        return r.out.at[pl.ds(start, piece[0]), pl.ds(lane, piece[1])]

    def plane_of(step):
        return lax.rem(z + step, planes)

    def give(half, step):
        other = plane_of(step)
        return remote(
            piece_in_pack(half, other), r.z_land.at[half, z], r.z_send.at[half, 0, other],
            r.z_recv.at[half, 0, z], {"ctx": block_of(other, x, c), "ep": ep},
        )

    def take(half, step):
        other = plane_of(step)
        return remote(
            piece_in_pack(half, 0), r.z_land.at[half, other], r.z_send.at[half, 0, other],
            r.z_recv.at[half, 0, other], {"ctx": block_of(other, x, c), "ep": ep},
        )

    def spread(half, step):
        other = plane_of(step)
        part = piece_in_final(half, z % owners)
        return remote(
            part, part, r.z_send.at[half, 1, other], r.z_recv.at[half, 1, z],
            {"ctx": block_of(other, x, c), "ep": ep},
        )

    def gather(half, step):
        other = plane_of(step)
        part = piece_in_final(half, other)
        return remote(
            part, part, r.z_send.at[half, 1, other], r.z_recv.at[half, 1, other],
            {"ctx": block_of(other, x, c), "ep": ep},
        )

    def each_plane(act, among_owners):
        def step(number, carry):
            if among_owners and owners < planes:

                @pl.when(plane_of(number) < owners)
                def _():
                    act(number)

            else:
                act(number)
            return carry

        lax.fori_loop(1, planes, step, 0)

    def if_owner(act):
        if owners < planes:
            pl.when(z < owners)(act)
        else:
            act()

    def over_final(half, number, way, target):
        part = r.out.at[pl.ds(pl.multiple_of(final_rows(half, number), 16), grad_rows)]
        return remote(part, part, r.last_send.at[half, way, number], r.last_recv.at[half, number], target)

    def stage_pieces(half):
        to_column(half).wait_recv()
        r.pack[half, quarter] = (
            r.pack[half, quarter].astype(F32) + r.x_land[half].astype(F32)
        ).astype(BF16)
        each_plane(lambda step: give(half, step).start(), True)

    def stage_own(half):
        def act():
            each_plane(lambda step: take(half, step).wait_recv(), False)
            r.z_land[half, z] = piece_in_pack(half, z % owners)[...]

            def add(p, total):
                return total + r.z_land[half, p].astype(F32)

            total = lax.fori_loop(0, planes, add, jnp.zeros(piece, F32))
            piece_in_final(half, z % owners)[...] = total.astype(BF16)
            each_plane(lambda step: spread(half, step).start(), False)

        if_owner(act)

    def stage_column(half):
        each_plane(lambda step: gather(half, step).wait_recv(), True)
        over_final(half, quarter, 0, across).start()
        over_final(half, quarter, 1, beside).start()

    def stage_core(half):
        over_final(half, 2 * (1 - x) + c, 0, across).wait_recv()
        over_final(half, 2 * (1 - x) + c, 1, beside).start()

    def stage_end(half):
        over_final(half, 2 * x + 1 - c, 1, beside).wait_recv()
        over_final(half, 2 * (1 - x) + 1 - c, 1, beside).wait_recv()
        each_plane(lambda step: give(half, step).wait_send(), True)
        if_owner(lambda: each_plane(lambda step: spread(half, step).wait_send(), False))
        over_final(half, quarter, 0, across).wait_send()
        over_final(half, quarter, 1, beside).wait_send()
        over_final(half, 2 * (1 - x) + c, 1, beside).wait_send()
        to_core(half, 0).wait_send()
        to_core(half, 1).wait_send()
        to_column(half).wait_send()

    def one(turn, carry):
        slot = turn % slots
        e = expert_at(turn)
        half, q = turn // 4, quarter_at(turn % 4)
        for copy in expert_loads(turn):
            copy.wait()
        h2, g = r.h2[...], r.g_all[...]
        gate = jnp.sum(
            jnp.where(iota((block, 2 * experts), 1) == e + ep * experts, r.gates[...], 0.0), axis=1, keepdims=True
        )
        mid_in, lifted = r.mid_in[e], r.lifted[e]
        gate_part = dot(h2, r.w_in[slot, :, :FF]) + dot(mid_in[:, :SPAN], r.w_in_up[slot, 0])
        up_part = dot(h2, r.w_in[slot, :, FF:]) + dot(mid_in[:, SPAN:], r.w_in_up[slot, 1])
        d_act = dot(g, r.w_out[slot], NT) + dot(lifted, r.w_out_down[slot])
        squash = 1.0 / (1.0 + jnp.exp(-gate_part))
        silu = gate_part * squash
        act = (silu * up_part).astype(BF16)
        mid_out = dot(act, r.w_out_down[slot], NT) * r.mask[:, :SPAN]
        d_gate = jnp.sum(act.astype(F32) * d_act, axis=1, keepdims=True)
        r.dgates[...] += jnp.where(iota(r.dgates.shape, 1) == e, d_gate, 0.0)
        d_act = d_act * gate
        d_up = (d_act * silu).astype(BF16)
        d_gp = (d_act * up_part * squash * (1.0 + gate_part * (1.0 - squash))).astype(BF16)
        d_mid_in = (
            jnp.concatenate([dot(d_gp, r.w_in_up[slot, 0], NT), dot(d_up, r.w_in_up[slot, 1], NT)], axis=1)
            * r.mask[:, :lanes]
        ).astype(BF16)
        scaled_mid = (mid_out * gate).astype(BF16)
        r.d_mid_in[e] = d_mid_in
        r.mid_out[e] = scaled_mid
        r.acc_out[...] += dot((act.astype(F32) * gate).astype(BF16), r.w_out[slot])
        r.acc_h2[...] += dot(d_gp, r.w_in[slot, :, :FF], NT) + dot(d_up, r.w_in[slot, :, FF:], NT)
        r.pack[half, q, :64, :] = dot(d_mid_in, h2, TN).astype(BF16)
        r.pack[half, q, 64:96, :FF] = dot(mid_in[:, :SPAN], d_gp, TN).astype(BF16)
        r.pack[half, q, 64:96, FF:] = dot(mid_in[:, SPAN:], d_up, TN).astype(BF16)
        r.pack[half, q, 96:112, :] = fold(
            dot((lifted.astype(F32) * gate).astype(BF16), act, TN)
        ).astype(BF16)
        r.pack[half, q, 112:, :] = dot(scaled_mid, g, TN).astype(BF16)

        @pl.when(turn + slots < experts)
        def _():
            for copy in expert_loads(turn + slots):
                copy.start()

        @pl.when(turn % 4 == 0)
        def _():
            to_core(half, 1 - x).start()

        @pl.when(turn % 4 == 1)
        def _():
            to_core(half, x).start()

        @pl.when(turn % 4 == 2)
        def _():
            add_core(half, 1 - x)
            to_column(half).start()

        @pl.when(turn % 4 == 3)
        def _():
            add_core(half, x)

        @pl.when(turn == 5)
        def _():
            stage_pieces(0)

        return carry

    lax.fori_loop(0, experts, one, 0)
    every = range(experts)
    r.acc_h2[...] += dot(jnp.concatenate([r.d_mid_in[e] for e in every], axis=1), r.in_down[...].reshape(experts * lanes, -1))

    r.dg_trade[ep] = r.dgates[...].T[:8]
    send_dg = swap(9, r.dg_trade.at[ep], r.dg_trade.at[ep])
    send_dg.start()
    r.trade[ep] = r.acc_h2[...].astype(BF16)
    send_h2 = swap(10, r.trade.at[ep], r.trade.at[ep])
    send_h2.start()
    r.acc_out[...] += dot(jnp.concatenate([r.mid_out[e] for e in every], axis=1), r.out_up[...].reshape(experts * SPAN, -1))
    r.out_trade[0] = r.acc_out[theirs, :].astype(BF16)
    send_out = swap(11, r.out_trade.at[0], r.out_trade.at[1])
    send_out.start()
    stage_own(0)
    stage_pieces(1)

    def small_sum(number, source, landing, result):
        tiles = source.shape[0] // 16
        width = landing.shape[2]
        each = source.shape[1] // width
        holders = tiles * each

        def region(ref, owner):
            return ref.at[span(owner // each * 16, 16), span(owner % each * width, width)]

        def other(step):
            return lax.rem(me + step, blocks)

        def to_owner(step):
            owner = other(step)
            return remote(
                region(source, owner), landing.at[me], r.small_send.at[number, 0, owner],
                r.small_recv.at[number, 0, me], {"ctx": owner, "ep": ep},
            )

        def from_all(step):
            device = other(step)
            return remote(
                region(source, me % holders), landing.at[device], r.small_send.at[number, 0, device],
                r.small_recv.at[number, 0, device], {"ctx": device, "ep": ep},
            )

        def to_all(step):
            device = other(step)
            part = region(result, me % holders)
            return remote(
                part, part, r.small_send.at[number, 1, device], r.small_recv.at[number, 1, me],
                {"ctx": device, "ep": ep},
            )

        def from_owner(step):
            owner = other(step)
            part = region(result, owner)
            return remote(
                part, part, r.small_send.at[number, 1, owner], r.small_recv.at[number, 1, owner],
                {"ctx": owner, "ep": ep},
            )

        def loop(act, mine_too):
            def step(index, carry):
                if mine_too:
                    act(index)
                else:

                    @pl.when(other(index) < holders)
                    def _():
                        act(index)

                return carry

            lax.fori_loop(1, blocks, step, 0)

        def scatter():
            loop(lambda step: to_owner(step).start(), False)

        def total():
            @pl.when(me < holders)
            def _():
                loop(lambda step: from_all(step).wait_recv(), True)
                landing[me] = region(source, me % holders)[...]

                def add(p, sums):
                    return sums + landing[p].astype(F32)

                sums = lax.fori_loop(0, blocks, add, jnp.zeros(landing.shape[1:], F32))
                region(result, me % holders)[...] = sums.astype(BF16)
                loop(lambda step: to_all(step).start(), True)

        def finish():
            loop(lambda step: from_owner(step).wait_recv(), False)
            loop(lambda step: to_owner(step).wait_send(), False)

            @pl.when(me < holders)
            def _():
                loop(lambda step: to_all(step).wait_send(), True)

        return scatter, total, finish

    early_scatter, early_total, early_finish = small_sum(0, r.early, r.early_land, r.early_out)
    late_scatter, late_total, late_finish = small_sum(1, r.late, r.late_land, r.late_out)

    drain_forward()

    send_dg.wait_recv()
    blank = jnp.zeros((112, block), F32)
    table = jnp.concatenate([r.dg_trade[0], r.dg_trade[1], blank], axis=0).T
    d_gates = table[:, : 2 * experts]
    gates = r.gates[...]
    d_logits = (gates * (d_gates - jnp.sum(gates * d_gates, axis=1, keepdims=True))).astype(BF16)
    from_router = dot(d_logits, r.router[...])
    stage_column(0)
    send_h2.wait_recv()
    d_h2 = r.trade[0].astype(F32) + r.trade[1].astype(F32) + from_router
    d_x2 = r.g_all[...].astype(F32) + rms_back(r.x2[...], r.moe_gain[...], d_h2)
    d_attn = d_x2.astype(BF16)
    r.acc_h2[...] = d_x2
    d_mid_o = (dot(d_attn, r.o_up[...], NT) * r.mask[:, :SPAN]).astype(BF16)

    d_att = (dot(d_attn, r.ow_all[ep], NT) + dot(d_mid_o, r.od_all[ep])).astype(BF16)
    for number in range(4):
        r.d_out[number] = d_att[:, 128 * number : 128 * number + 128]
    for step in (1, 2, 3):
        piece_to(*grad_pieces, step).start()
    r.dqt[...] = jnp.zeros(r.dqt.shape, F32)
    r.early[:32, :] = dot(r.mid_o[...], d_attn, TN).astype(BF16)
    r.early[32:48, :] = fold(dot(d_mid_o, r.att_all[ep], TN)).astype(BF16)
    r.early[48:, :] = jnp.zeros((16, r.early.shape[1]), BF16)
    early_scatter()
    stage_own(1)

    r.d_in[head] = r.d_out[head]
    for step in (1, 2, 3):
        piece_from(*grad_pieces, step).wait_recv()
    for b in range(4):
        received = r.d_in[b].astype(F32)
        turned = stack_columns(received)
        r.dt[b, HEAD:, :] = turned.astype(BF16)
        r.delta[b] = jnp.sum(turned * r.acc[b], axis=0, keepdims=True)
        r.dn[b] = stack_rows(received, True)

    def back_step(p, kb, kinds):
        kv = r.kvall[p, kb]
        grown = None
        for b, masked in kinds:
            pos_row, start_row = pos_rows[b], start_rows[b]
            s = dot(kv, r.qt[b])
            base = r.lse[b]
            if masked:
                key = (4 * p + kb) * block + iota(s.shape, 0)
                w = jnp.where((key <= pos_row) & (key >= start_row), jnp.exp(s - base), 0.0)
            else:
                w = jnp.exp(s - jnp.where(start_row <= (4 * p + 1) * block, base, -LOW))
            d_w = dot(kv, r.dt[b])
            d_s = (w * (d_w - r.delta[b])).astype(BF16)
            added = dot(d_s, r.qn[b]) + dot(w.astype(BF16), r.dn[b])
            grown = added if grown is None else grown + added
            r.dqt[b] += dot(kv, d_s, TN)[:HEAD]
        r.kvall[p, kb] = grown.astype(BF16)

    def lower(p):
        return remote(r.kvall.at[p], r.from_up.at[p % kept], r.down_send.at[p], r.down_recv.at[p], down)

    def finish(p):
        @pl.when(z < planes - 1)
        def _():
            lower(p).wait_recv()
            r.kvall[p] = (r.kvall[p].astype(F32) + r.from_up[p % kept].astype(F32)).astype(BF16)
            if planes > kept:

                @pl.when(p + kept <= z)
                def _():
                    pl.semaphore_signal(r.credit, inc=1, device_id=up, device_id_type=MESH)

        @pl.when(p < z)
        def _():
            if planes > kept:

                @pl.when(p >= kept)
                def _():
                    pl.semaphore_wait(r.credit, 1)

            lower(p).start()

    def back_to(source, landing, sends, recvs, b):
        return remote(source.at[b], landing.at[head], sends.at[b], recvs.at[head], device_of(b))

    def back_from(landing, sends, recvs, number):
        return remote(landing.at[number], landing.at[number], sends.at[number], recvs.at[number], device_of(number))

    def give_back(source, landing, sends, recvs, b):
        @pl.when(b == head)
        def _():
            landing[b] = source[b]

        @pl.when(b != head)
        def _():
            back_to(source, landing, sends, recvs, b).start()

    dq_pieces = (r.dq_out, r.dq_in, r.dq_send, r.dq_recv)
    dkv_pieces = (r.kvall.at[z], r.dkv_in, r.dkv_send, r.dkv_recv)

    def plane_back(p, carry):
        @pl.when(p < z)
        def _():
            @pl.when(p == 0)
            def _():
                back_step(p, 0, [(b, True) for b in range(4)])

            def middle(kb, inner):
                back_step(p, kb, [(b, False) for b in range(4)])
                return inner

            lax.fori_loop(jnp.where(p == 0, 1, 0), 2, middle, 0)

            @pl.when((p > 0) & (z < planes - 1))
            def _():
                finish(p - 1)

            lax.fori_loop(2, 4, middle, 0)

            @pl.when(z == planes - 1)
            def _():
                finish(p)

        @pl.when(p == z)
        def _():
            for kb in range(4):
                back_step(p, kb, [(b, b == kb or kb == 0) for b in range(kb, 4)])
                r.dq_out[kb] = (unstack(r.dqt[kb]) * SCALE).astype(BF16)
                give_back(*dq_pieces, kb)

                @pl.when(z == planes - 1)
                def _():
                    give_back(*dkv_pieces, kb)

                if kb == 1:

                    @pl.when((p > 0) & (z < planes - 1))
                    def _():
                        finish(p - 1)

        @pl.when(p == 0)
        def _():
            stage_column(1)
            stage_core(0)

        @pl.when(p == 1)
        def _():
            early_total()

        @pl.when(p == 2)
        def _():
            stage_core(1)

        return carry

    lax.fori_loop(0, planes, plane_back, 0)

    @pl.when(z < planes - 1)
    def _():
        finish(z)
        for b in range(4):
            give_back(*dkv_pieces, b)

    cosine, sine = r.cosine[...], r.sine[...]
    for number in range(4):

        @pl.when(number != head)
        def _():
            back_from(*dq_pieces[1:], number).wait_recv()
            back_from(*dkv_pieces[1:], number).wait_recv()

    d_query = jnp.concatenate([r.dq_in[number] for number in range(4)], axis=1)
    d_q = rotate(d_query.astype(F32), cosine, sine, -1.0).astype(BF16)
    d_key = jnp.concatenate([r.dkv_in[number, :, :HEAD] for number in range(4)], axis=1)
    d_k = rotate(d_key.astype(F32), cosine, sine, -1.0).astype(BF16)
    d_value = jnp.concatenate([r.dkv_in[number, :, HEAD:] for number in range(4)], axis=1)
    r.mid_trade[ep] = jnp.concatenate(
        [dot(d_q, r.q_up[...], NT), dot(d_k, r.kv_up[0], NT), dot(d_value, r.kv_up[1], NT)], axis=1
    ).astype(BF16)
    send_mid = swap(12, r.mid_trade.at[ep], r.mid_trade.at[ep])
    send_mid.start()
    full = dot(d_q, r.q_w[...], NT) + dot(d_k, r.kv_w[0], NT) + dot(d_value, r.kv_w[1], NT)
    first, second = full[:rows], full[rows:]
    r.norm_trade[0] = jnp.where(ep == 0, second, first).astype(BF16)
    send_norm = swap(13, r.norm_trade.at[0], r.norm_trade.at[1])
    send_norm.start()
    r.late[96:112, :] = fold(dot(r.mids[:, :SPAN], d_q, TN)).astype(BF16)
    r.late[112:, :] = fold(
        jnp.concatenate(
            [dot(r.mids[:, SPAN : 2 * SPAN], d_k, TN), dot(r.mids[:, 2 * SPAN :], d_value, TN)], axis=1
        )
    ).astype(BF16)
    send_mid.wait_recv()
    d_mids = (
        (r.mid_trade[0].astype(F32) + r.mid_trade[1].astype(F32)) * r.mask[:, : 3 * SPAN]
    ).astype(BF16)
    r.late[:96, :] = dot(d_mids, r.h1[...], TN).astype(BF16)
    late_scatter()
    send_out.wait_recv()
    r.block_out[...] = (r.x2[mine, :] + (r.acc_out[mine, :] + r.out_trade[1].astype(F32))).astype(BF16)
    from_mids = dot(d_mids, r.qkv_down[...])
    own = jnp.where(ep == 0, first + from_mids[:rows], second + from_mids[rows:])
    send_norm.wait_recv()
    own = own + r.norm_trade[1].astype(F32)
    r.in_grad[...] = (
        r.acc_h2[mine, :] + rms_back(r.x_all[mine, :].astype(F32), r.attn_gain[...], own)
    ).astype(BF16)
    late_total()
    early_finish()
    stage_end(0)
    stage_end(1)

    for copy in (send_x, send_ow, send_od, send_hot, send_g, send_dg, send_h2, send_out, send_mid, send_norm):
        copy.wait_send()
    for b in range(4):
        att_to(b, 1 - ep).wait_send()

        @pl.when(b != head)
        def _():
            att_to(b, ep).wait_send()
            back_to(*dq_pieces, b).wait_send()
            back_to(*dkv_pieces, b).wait_send()

    for step in (1, 2, 3):
        piece_to(*grad_pieces, step).wait_send()
    hand_on(head, 0, across).wait_send()
    hand_on(head, 1, beside).wait_send()
    hand_on(sibling, 1, beside).wait_send()

    def drain(p, carry):
        lower(p).wait_send()
        return carry

    lax.fori_loop(0, z, drain, 0)
    late_finish()


RESULTS = (
    "ein_down", "ein_up", "eout_down", "eout_up", "block_out", "in_grad", "g_down", "g_q", "g_kv", "g_od", "g_ou",
)


def unpack_kernel(packed, *refs):
    count = len(RESULTS)
    outs = dict(zip(RESULTS, refs[:count]))
    held = dict(zip(RESULTS, refs[count : 2 * count]))
    rows, sem_in, sem_out = refs[2 * count :]
    experts = outs["ein_down"].shape[0]
    grad_rows = 144
    base = experts * grad_rows

    def fetch(start, size, number):
        return pltpu.make_async_copy(
            packed.at[pl.ds(start, size)], rows.at[pl.ds(start, size)], sem_in.at[number]
        )

    fetches = [fetch(grad_rows * e, grad_rows, e) for e in range(experts)]
    fetches.append(fetch(base, rows.shape[0] - base, experts))
    for copy in fetches:
        copy.start()
    stores = []

    def store(name, number):
        copy = pltpu.make_async_copy(
            held[name] if number is None else held[name].at[number],
            outs[name] if number is None else outs[name].at[number],
            sem_out.at[len(stores)],
        )
        copy.start()
        stores.append(copy)

    for e in range(experts):
        fetches[e].wait()
        part = rows[grad_rows * e : grad_rows * e + grad_rows, :].astype(F32)
        held["ein_down"][e] = part[:64]
        held["ein_up"][e, 0] = part[64:96, :FF]
        held["ein_up"][e, 1] = part[64:96, FF:]
        held["eout_down"][e, :16] = part[96:112, :FF]
        held["eout_down"][e, 16:] = part[96:112, FF:]
        held["eout_up"][e] = part[112:]
        for name in RESULTS[:4]:
            store(name, e)
    fetches[experts].wait()
    late = rows[base : base + 128, :].astype(F32)
    early = rows[base + 384 : base + 448, :].astype(F32)
    held["block_out"][...] = rows[base + 128 : base + 256, :]
    held["in_grad"][...] = rows[base + 256 : base + 384, :]
    held["g_down"][...] = late[:96]
    held["g_q"][:16, :] = late[96:112, :FF]
    held["g_q"][16:, :] = late[96:112, FF:]
    kv = FF // 2
    for side in (0, 1):
        for half in (0, 1):
            first = kv * (2 * half + side)
            held["g_kv"][side, 16 * half : 16 * half + 16, :] = late[112:, first : first + kv]
    held["g_od"][:16, :] = early[32:48, :FF]
    held["g_od"][16:, :] = early[32:48, FF:]
    held["g_ou"][...] = early[:32]
    for name in RESULTS[4:]:
        store(name, None)
    for copy in stores:
        copy.wait()


def per_device(
    resid_in, out_grad, attn_gain, q_weight, key_value_weight, o_weight, moe_gain, router, expert_in,
    expert_out, qkv_down, q_up, key_value_up_factor, o_down, o_up, expert_in_down, expert_in_up,
    expert_out_down, expert_out_up, expert_ids, doc_starts, doc_adapter,
):
    blocks = lax.axis_size("ctx")
    planes = blocks // 4
    rows, width = resid_in.shape
    block = 2 * rows
    heads = q_weight.shape[1]
    kv = key_value_weight.shape[2]
    experts = expert_in.shape[0]
    slots = 6 if planes <= 4 else 4
    kept = planes if planes <= 4 else 2
    grad_rows = 2 * SPAN + SPAN + SPAN // 2 + SPAN
    base = experts * grad_rows
    groups = 3 if planes >= 12 else 1
    piece = (grad_rows // groups, width // 4)
    early_width = max(128, 4 * width // blocks)
    late_width = max(128, 8 * width // blocks)
    freq = np.tile(np.power(10000.0, -2.0 * np.arange(HEAD // 2) / HEAD).astype(np.float32), 4)[None, :]

    def shape(dims, kind=BF16):
        return jax.ShapeDtypeStruct(dims, kind)

    def dma(*dims):
        return pltpu.SemaphoreType.DMA(dims)

    def low(*dims):
        return pltpu.VMEM(dims, BF16)

    def full(*dims):
        return pltpu.VMEM(dims, F32)

    operands = dict(
        resid=resid_in, grad=out_grad, ids=expert_ids.T, starts=doc_starts, adapters=doc_adapter,
        attn_gain=attn_gain[None, :], moe_gain=moe_gain[None, :], freq=jnp.asarray(freq), qkv_down=qkv_down.T,
        q_up=q_up, kv_up=key_value_up_factor, o_down=o_down.T, o_up=o_up, router=router.T, q_hbm=q_weight,
        kv_hbm=key_value_weight, o_hbm=o_weight, in_hbm=expert_in, out_hbm=expert_out,
        in_down_hbm=jnp.swapaxes(expert_in_down, 1, 2), in_up_hbm=expert_in_up,
        out_down_hbm=jnp.swapaxes(expert_out_down, 1, 2), out_up_hbm=expert_out_up,
    )
    results = dict(out=shape((base + 448, width)))
    scratch = dict(
        q_w=low(*q_weight.shape), kv_w=low(*key_value_weight.shape), ow_all=low(2, heads, width),
        od_all=low(2, SPAN, heads), w_in=low(slots, *expert_in.shape[1:]), w_out=low(slots, *expert_out.shape[1:]),
        in_down=low(experts, 2 * SPAN, width), w_in_up=low(slots, *expert_in_up.shape[1:]),
        w_out_down=low(slots, SPAN, FF), out_up=low(experts, SPAN, width),
        mid_in=low(experts, block, 2 * SPAN), lifted=low(experts, block, SPAN),
        d_mid_in=low(experts, block, 2 * SPAN), mid_out=low(experts, block, SPAN),
        x_all=low(block, width), g_all=low(block, width), h1=low(block, width), h2=low(block, width),
        hot_all=low(block, 128), mask=full(block, 128), cosine=full(block, 128), sine=full(block, 128),
        mids=low(block, 3 * SPAN), kvall=low(planes, 4, block, 128), kv_out=low(4, block, 128), q_out=low(4, block, 128),
        q_in=low(4, block, 128), d_out=low(4, block, 128), d_in=low(4, block, 128), o_out=low(4, block, 128),
        dq_out=low(4, block, 128), dq_in=low(4, block, 128), dkv_in=low(4, block, 128), qt=low(4, 128, 2 * block),
        qn=low(4, 2 * block, 128), dt=low(4, 128, 2 * block), dn=low(4, 2 * block, 128),
        m_s=full(4, 1, 2 * block), l_s=full(4, 1, 2 * block), lse=full(4, 1, 2 * block),
        delta=full(4, 1, 2 * block), acc=full(4, HEAD, 2 * block), dqt=full(4, HEAD, 2 * block),
        att_all=low(2, block, heads), halves=full(2, block, width), half_mid=full(2, block, SPAN), mid_o=low(block, SPAN), x2=full(block, width),
        gates=full(block, 2 * experts), dgates=full(block, 128), trade=low(2, block, width), out_trade=low(2, rows, width),
        norm_trade=low(2, rows, width), mid_trade=low(2, block, 3 * SPAN), dg_trade=full(2, 8, block),
        pack=low(2, 4, grad_rows, width), core_land=low(2, 2, grad_rows, width), x_land=low(2, grad_rows, width),
        z_land=low(2, planes, *piece), early=low(64, width), late=low(128, width),
        early_land=low(blocks, 16, early_width), late_land=low(blocks, 16, late_width),
        from_up=low(kept, 4, block, 128), credit=pltpu.SemaphoreType.REGULAR,
        load_sem=dma(5), expert_sem=dma(slots, 4), pair_send=dma(14), pair_recv=dma(14),
        kv_send=dma(4, 2), kv_recv=dma(4, 2), q_send=dma(4), q_recv=dma(4), d_send=dma(4), d_recv=dma(4),
        dq_send=dma(4), dq_recv=dma(4), dkv_send=dma(4), dkv_recv=dma(4), up_send=dma(planes, 2),
        up_recv=dma(planes, 2), ow_send=dma(4, 2), ow_recv=dma(4), att_send=dma(4, 2), att_recv=dma(2, 4), core_send=dma(2, 2), core_recv=dma(2, 2),
        x_send=dma(2), x_recv=dma(2), z_send=dma(2, 2, planes), z_recv=dma(2, 2, planes), last_send=dma(2, 2, 4),
        last_recv=dma(2, 4),
        small_send=dma(2, 2, blocks), small_recv=dma(2, 2, blocks), down_send=dma(planes),
        down_recv=dma(planes),
    )
    (out,) = pl.pallas_call(
        functools.partial(layer_kernel, planes, slots, INPUTS + OUTPUTS + tuple(scratch)),
        out_shape=[results[name] for name in OUTPUTS],
        in_specs=[
            SMEM if name in ("starts", "adapters") else HBM if name.endswith("hbm") else VMEM for name in INPUTS
        ],
        out_specs=[VMEM] * len(OUTPUTS),
        scratch_shapes=list(scratch.values()),
        compiler_params=pltpu.CompilerParams(
            collective_id=1, has_side_effects=True, vmem_limit_bytes=62 << 20
        ),
        name="layer",
    )(*[operands[name] for name in INPUTS])

    unpacked = dict(
        ein_down=shape((experts, 2 * SPAN, width), F32), ein_up=shape((experts, 2, SPAN, FF), F32),
        eout_down=shape((experts, SPAN, FF), F32), eout_up=shape((experts, SPAN, width), F32),
        block_out=shape((rows, width)), in_grad=shape((rows, width)), g_down=shape((3 * SPAN, width), F32),
        g_q=shape((SPAN, heads), F32), g_kv=shape((2, SPAN, kv), F32), g_od=shape((SPAN, heads), F32),
        g_ou=shape((SPAN, width), F32),
    )
    ein_down, ein_up, eout_down, eout_up, block_out, in_grad, g_down, g_q, g_kv, g_od, g_ou = pl.pallas_call(
        unpack_kernel,
        out_shape=[unpacked[name] for name in RESULTS],
        in_specs=[HBM],
        out_specs=[HBM] * len(RESULTS),
        scratch_shapes=[
            *[pltpu.VMEM(unpacked[name].shape, unpacked[name].dtype) for name in RESULTS],
            pltpu.VMEM(out.shape, BF16), dma(experts + 1), dma(4 * experts + 7),
        ],
        compiler_params=pltpu.CompilerParams(vmem_limit_bytes=62 << 20),
        name="unpack",
    )(out)
    return (
        block_out, in_grad, g_down.T, g_q, g_kv, g_od.T, g_ou, jnp.swapaxes(ein_down, 1, 2), ein_up,
        jnp.swapaxes(eout_down, 1, 2), eout_up,
    )


def solution(mesh):
    placed = (
        P(("ctx", "ep"), None),
        P(("ctx", "ep"), None),
        P(),
        P(None, "ep"),
        P(None, None, "ep"),
        P("ep", None),
        P(),
        P(),
        P("ep", None, None),
        P("ep", None, None),
        P(),
        P(None, "ep"),
        P(None, None, "ep"),
        P("ep", None),
        P(),
        P("ep", None, None),
        P("ep", None, None, None),
        P("ep", None, None),
        P("ep", None, None),
        P(("ctx", "ep"), None),
        P(),
        P(),
    )
    return jax.shard_map(
        per_device,
        mesh=mesh,
        in_specs=placed,
        out_specs=(
            P(("ctx", "ep"), None),
            P(("ctx", "ep"), None),
            P(),
            P(None, "ep"),
            P(None, None, "ep"),
            P("ep", None),
            P(),
            P("ep", None, None),
            P("ep", None, None, None),
            P("ep", None, None),
            P("ep", None, None),
        ),
        check_vma=False,
    )
```

```python
import functools

import jax
import jax.numpy as jnp
import numpy as np
from jax import lax
from jax.experimental import pallas as pl
from jax.experimental.pallas import tpu as pltpu
from jax.sharding import PartitionSpec as P

MESH = pl.DeviceIdType.MESH
VMEM = pl.BlockSpec(memory_space=pltpu.VMEM)
SMEM = pl.BlockSpec(memory_space=pltpu.SMEM)
HBM = pl.BlockSpec(memory_space=pl.ANY)
F32 = jnp.float32
BF16 = jnp.bfloat16

HEAD = 64
FF = 512
RANK = 16
SPAN = 32
EPS = 1e-06
LOW = -1e30
SCALE = 0.125

NN = (((1,), (0,)), ((), ()))
NT = (((1,), (1,)), ((), ()))
TN = (((0,), (0,)), ((), ()))


def dot(left, right, dims=NN):
    return lax.dot_general(left, right, dims, preferred_element_type=F32)


def iota(shape, dim):
    return lax.broadcasted_iota(jnp.int32, shape, dim)


def rms(values, gain):
    return values * lax.rsqrt(jnp.mean(values * values, axis=-1, keepdims=True) + EPS) * gain


def rms_back(values, gain, upstream):
    factor = lax.rsqrt(jnp.mean(values * values, axis=-1, keepdims=True) + EPS)
    scaled = upstream * gain
    return factor * scaled - values * factor * factor * factor * jnp.mean(
        scaled * values, axis=-1, keepdims=True
    )


def rotate(values, cosine, sine, sign):
    width = values.shape[1]
    copies = width // 128
    cosine = jnp.concatenate([cosine] * copies, axis=1)
    sine = jnp.concatenate([sine] * copies, axis=1)
    first = iota(values.shape, 1) % HEAD < HEAD // 2
    ahead = pltpu.roll(values, width - HEAD // 2, 1)
    behind = pltpu.roll(values, HEAD // 2, 1)
    return values * cosine + sign * jnp.where(first, -ahead, behind) * sine


def doc_scan(positions, starts_ref, adapters_ref):
    own_start = jnp.zeros(positions.shape, jnp.int32)
    adapter = jnp.zeros(positions.shape, jnp.int32)
    for number in range(starts_ref.shape[0]):
        opened = starts_ref[number] <= positions
        own_start = jnp.where(opened, starts_ref[number], own_start)
        adapter = jnp.where(opened, adapters_ref[number], adapter)
    return own_start, adapter


def place():
    me = lax.axis_index("ctx")
    ep = lax.axis_index("ep")
    return me, ep, me // 4, (me // 2) % 2, me % 2


def block_of(z, x, c):
    return (z * 2 + x) * 2 + c


def signal(device):
    pl.semaphore_signal(
        pltpu.get_barrier_semaphore(), inc=1, device_id=device, device_id_type=MESH
    )


def remote(src, dst, send, recv, device):
    return pltpu.make_async_remote_copy(
        src_ref=src,
        dst_ref=dst,
        send_sem=send,
        recv_sem=recv,
        device_id=device,
        device_id_type=MESH,
    )


def span(start, count):
    return pl.ds(pl.multiple_of(start, count), count)


def stack_rows(piece, upper):
    turned = pltpu.roll(piece, HEAD, 1)
    keep = iota(piece.shape, 1) >= HEAD if upper else iota(piece.shape, 1) < HEAD
    first, second = (turned, piece) if upper else (piece, turned)
    blank = jnp.zeros(piece.shape, piece.dtype)
    return jnp.concatenate([jnp.where(keep, first, blank), jnp.where(keep, second, blank)], axis=0).astype(BF16)


def stack_columns(piece):
    turned = piece.T
    return jnp.concatenate([turned[:HEAD], turned[HEAD:]], axis=1)


def unstack(columns):
    count = columns.shape[1] // 2
    return jnp.concatenate([columns[:, :count], columns[:, count:]], axis=0).T


def fold(wide):
    count = wide.shape[0] // 2
    return jnp.concatenate([wide[:count], wide[count:]], axis=1)


INPUTS = (
    "resid", "grad", "ids", "starts", "adapters", "attn_gain", "moe_gain", "freq",
    "qkv_down", "q_up", "kv_up", "o_down", "o_up", "router",
    "q_hbm", "kv_hbm", "o_hbm", "in_hbm", "out_hbm", "in_down_hbm", "in_up_hbm", "out_down_hbm", "out_up_hbm",
)
OUTPUTS = ("out",)


def layer_kernel(planes, slots, names, *refs):
    r = dict(zip(names, refs))
    r = type("Refs", (), r)
    r.acc_out, r.acc_h2 = r.halves.at[0], r.halves.at[1]
    grad_rows = r.pack.shape[2]
    base = r.in_hbm.shape[0] * grad_rows
    r.late_out = r.packed.at[pl.ds(base, 128)]
    r.block_out = r.packed.at[pl.ds(base + 128, 128)]
    r.in_grad = r.packed.at[pl.ds(base + 256, 128)]
    r.early_out = r.packed.at[pl.ds(base + 384, 64)]
    me, ep, z, x, c = place()
    blocks = 4 * planes
    pair = {"ctx": me, "ep": 1 - ep}
    head = 2 * x + c
    up = {"ctx": jnp.minimum(me + 4, blocks - 1), "ep": ep}
    down = {"ctx": jnp.maximum(me - 4, 0), "ep": ep}
    across = {"ctx": block_of(z, 1 - x, c), "ep": ep}
    beside = {"ctx": block_of(z, x, 1 - c), "ep": ep}
    rows = r.resid.shape[0]
    block = 2 * rows
    mine = span(ep * rows, rows)
    theirs = span(rows - ep * rows, rows)
    experts = r.in_hbm.shape[0]
    groups = 3 if planes >= 12 else 1
    owners = 4 * groups
    piece = (grad_rows // groups, r.pack.shape[3] // 4)
    kept = r.from_up.shape[0]

    load_q = pltpu.make_async_copy(r.q_hbm, r.q_w, r.load_sem.at[0])
    load_kv = pltpu.make_async_copy(r.kv_hbm, r.kv_w, r.load_sem.at[1])
    load_o = pltpu.make_async_copy(r.o_hbm, r.ow_all.at[ep], r.load_sem.at[2])
    load_kv.start()
    load_q.start()
    load_o.start()
    load_in_down = pltpu.make_async_copy(r.in_down_hbm, r.in_down, r.load_sem.at[3])
    load_out_up = pltpu.make_async_copy(r.out_up_hbm, r.out_up, r.load_sem.at[4])
    load_in_down.start()
    load_out_up.start()
    weights = (
        (r.in_hbm, r.w_in), (r.out_hbm, r.w_out), (r.in_up_hbm, r.w_in_up), (r.out_down_hbm, r.w_out_down),
    )

    def quarter_at(turn):
        return jnp.where(turn % 2 == 0, 1 - x, x) * 2 + jnp.where(turn < 2, 1 - c, c)

    def expert_at(turn):
        return 2 * quarter_at(turn % 4) + turn // 4

    def expert_loads(turn):
        e, slot = expert_at(turn), turn % slots
        return [
            pltpu.make_async_copy(source.at[e], held.at[slot], r.expert_sem.at[slot, number])
            for number, (source, held) in enumerate(weights)
        ]

    def begin(turn, carry):
        for copy in expert_loads(turn):
            copy.start()
        return carry

    lax.fori_loop(0, slots, begin, 0)

    def greet(step, carry):
        signal({"ctx": lax.rem(me + step, blocks), "ep": ep})
        signal({"ctx": lax.rem(me + step, blocks), "ep": 1 - ep})
        return carry

    signal(pair)
    lax.fori_loop(1, blocks, greet, 0)
    pl.semaphore_wait(pltpu.get_barrier_semaphore(), 2 * blocks - 1)

    def wait_sent(like, sem):
        remote(like, like, sem, sem, pair).wait_send()

    def wait_received(like, sem):
        remote(like, like, sem, sem, pair).wait_recv()

    def swap(number, src, dst):
        return remote(src, dst, r.pair_send.at[number], r.pair_recv.at[number], pair)

    small = rows // 2
    chunks = (
        (mine, rows),
        (span(rows - ep * rows, small), small),
        (span(rows - ep * rows + small, small), small),
    )
    send_x = []
    for number in (0, 1):
        part = pl.ds(small * number, small)
        copy = swap(number, r.resid.at[part], r.x_all.at[span(ep * rows + small * number, small)])
        copy.start()
        send_x.append(copy)

    hot = jnp.zeros((r.ids.shape[0], rows), F32)
    hot = jnp.zeros((128, rows), F32)
    numbers = iota((128, rows), 0)
    for choice in range(r.ids.shape[0]):
        hot = hot + jnp.where(r.ids[choice : choice + 1, :] == numbers, 1.0, 0.0)
    r.hot_all[mine, :] = hot.T.astype(BF16)
    r.x_all[mine, :] = r.resid[...]
    r.g_all[mine, :] = r.grad[...]
    r.od_all[ep] = r.o_down[...]
    position = me * block + iota((block, 128), 0)
    own_start, adapter = doc_scan(position, r.starts, r.adapters)
    r.mask[...] = jnp.where((iota((block, 128), 1) % SPAN) // RANK == adapter, 1.0, 0.0)
    angles = (position - own_start).astype(F32) * r.freq[...]
    r.cosine[...] = jnp.cos(angles)
    r.sine[...] = jnp.sin(angles)
    pos_rows = [((4 * z + b) * block + iota((8, 2 * block), 1) % block)[:1] for b in range(4)]
    start_rows = [
        doc_scan((4 * z + b) * block + iota((8, 2 * block), 1) % block, r.starts, r.adapters)[0][:1] for b in range(4)
    ]

    def other_head(step):
        return lax.rem(head + step, 4)

    def device_of(number):
        return {"ctx": 4 * z + number, "ep": ep}

    def kv_to(step, chunk):
        number = other_head(step)
        here = chunks[chunk][0]
        return remote(
            r.kv_out.at[number, here, :], r.kvall.at[z, head, here, :],
            r.kv_send.at[chunk], r.kv_recv.at[chunk], device_of(number),
        )

    def three(chunk):
        return r.kv_out.at[pl.ds(0, 3), chunks[chunk][0], :]

    def piece_to(source, landing, send, recv, step):
        number = other_head(step)
        return remote(source.at[number], landing.at[head], send, recv, device_of(number))

    three_pieces = r.q_out.at[pl.ds(0, 3)]

    query_pieces = (r.q_out, r.q_in, r.piece_send.at[0], r.piece_recv.at[0])
    grad_pieces = (r.d_out, r.d_in, r.piece_send.at[1], r.piece_recv.at[1])

    def climb(p, half):
        part = r.kvall.at[p, :, chunks[half][0], :]
        return remote(part, part, r.up_send.at[p, half], r.up_recv.at[p, half], up)

    def climb_on(p, half):
        @pl.when(z < planes - 1)
        def _():
            climb(p, half).start()

    def collect(half):
        wait_received(three(half), r.kv_recv.at[half])
        climb_on(z, half)

    def project(here):
        h1 = rms(r.x_all[here, :].astype(F32), r.attn_gain[...]).astype(BF16)
        r.h1[here, :] = h1
        mids = (dot(h1, r.qkv_down[...], NT) * r.mask[here, : 3 * SPAN]).astype(BF16)
        r.mids[here, :] = mids
        k_lin = dot(h1, r.kv_w[0]) + dot(mids[:, SPAN : 2 * SPAN], r.kv_up[0])
        keys = rotate(k_lin, r.cosine[here, :], r.sine[here, :], 1.0)
        values = dot(h1, r.kv_w[1]) + dot(mids[:, 2 * SPAN :], r.kv_up[1])
        for number in range(4):
            lanes = slice(HEAD * number, HEAD * number + HEAD)
            r.kv_out[number, here, :] = jnp.concatenate([keys[:, lanes], values[:, lanes]], axis=1).astype(BF16)
        r.kvall[z, head, here, :] = r.kv_out[head, here, :]

    load_kv.wait()
    project(mine)
    for step in (1, 2, 3):
        kv_to(step, 0).start()
    send_x[0].wait_recv()
    project(chunks[1][0])
    for step in (1, 2, 3):
        kv_to(step, 1).start()
    collect(0)
    send_x[1].wait_recv()
    load_o.wait()

    def ow_quarter(side, number):
        return r.ow_all.at[side, pl.ds(pl.multiple_of(128 * number, 128), 128), :]

    def hand_on(number, way, target):
        part = ow_quarter(1 - ep, number)
        return remote(part, part, r.ow_send.at[number, way], r.ow_recv.at[number], target)

    sibling = 2 * (1 - x) + c

    def hand_first():
        send_ow.wait_recv()
        hand_on(head, 0, across).start()
        hand_on(head, 1, beside).start()

    def hand_second():
        hand_on(sibling, 0, across).wait_recv()
        hand_on(sibling, 1, beside).start()

    def hand_last():
        hand_on(2 * x + 1 - c, 1, beside).wait_recv()
        hand_on(2 * (1 - x) + 1 - c, 1, beside).wait_recv()

    send_ow = swap(12, ow_quarter(ep, head), ow_quarter(ep, head))
    send_od = swap(4, r.od_all.at[ep], r.od_all.at[ep])
    send_hot = swap(14, r.hot_all.at[mine], r.hot_all.at[mine])
    send_g = swap(2, r.grad, r.g_all.at[mine])
    for copy in (send_ow, send_od, send_hot):
        copy.start()
    project(chunks[2][0])
    for step in (1, 2, 3):
        kv_to(step, 2).start()
    load_q.wait()
    q_lin = dot(r.h1[...], r.q_w[...]) + dot(r.mids[:, :SPAN], r.q_up[...])
    query = rotate(q_lin, r.cosine[...], r.sine[...], 1.0).astype(BF16)
    for number in range(4):
        r.q_out[number] = query[:, 128 * number : 128 * number + 128]
    for step in (1, 2, 3):
        piece_to(*query_pieces, step).start()
    collect(1)
    send_g.start()
    hand_first()
    r.q_in[head] = r.q_out[head]
    r.m_s[...] = jnp.full(r.m_s.shape, LOW, F32)
    r.l_s[...] = jnp.zeros(r.l_s.shape, F32)
    r.acc[...] = jnp.zeros(r.acc.shape, F32)
    r.qt[:, HEAD:, :] = jnp.zeros((4, HEAD, 2 * block), BF16)
    r.dt[:, :HEAD, :] = jnp.zeros((4, HEAD, 2 * block), BF16)
    collect(2)
    wait_received(three_pieces, r.piece_recv.at[0])
    for b in range(4):
        scaled = r.q_in[b].astype(F32) * SCALE
        r.qt[b, :HEAD, :] = stack_columns(scaled).astype(BF16)
        r.qn[b] = stack_rows(scaled, False)

    def attend_step(p, b, keys, kinds):
        pos_row, start_row = pos_rows[b], start_rows[b]
        sees = start_row <= (4 * p + 1) * block
        everything = dot(keys, r.qt[b])
        scores, peak = [], None
        for first, count, position, masked in kinds:
            s = everything[first : first + count]
            if masked:
                key = position + iota(s.shape, 0)
                s = jnp.where((key <= pos_row) & (key >= start_row), s, LOW)
            scores.append(s)
            highest = jnp.max(s, axis=0, keepdims=True)
            if not masked:
                highest = jnp.where(sees, highest, LOW)
            peak = highest if peak is None else jnp.maximum(peak, highest)
        old = r.m_s[b]
        new = jnp.maximum(old, peak)
        r.m_s[b] = new
        blind = jnp.where(sees, new, -LOW)
        decay = jnp.exp(old - new)
        total = r.l_s[b] * decay
        weights = []
        for (first, count, position, masked), s in zip(kinds, scores):
            w = jnp.exp(s - (new if masked else blind))
            total = total + jnp.sum(w, axis=0, keepdims=True)
            weights.append(w.astype(BF16))
        weights = jnp.concatenate(weights, axis=0) if len(weights) > 1 else weights[0]
        r.l_s[b] = total
        r.acc[b] = r.acc[b] * decay + dot(keys, weights, TN)[HEAD:]

    def att_to(b, side):
        return remote(
            r.o_out.at[b], r.att_all.at[ep, :, pl.ds(pl.multiple_of(128 * head, 128), 128)],
            r.att_send.at[jnp.where(side == ep, 0, 1)], r.att_recv.at[ep], {"ctx": 4 * z + b, "ep": side},
        )

    def settle(b):
        r.lse[b] = r.m_s[b] + jnp.log(r.l_s[b])
        done = r.acc[b] / r.l_s[b]
        r.acc[b] = done
        r.o_out[b] = unstack(done).astype(BF16)

        @pl.when(b == head)
        def _():
            r.att_all[ep, :, pl.ds(pl.multiple_of(128 * head, 128), 128)] = r.o_out[b]

        @pl.when(b != head)
        def _():
            att_to(b, ep).start()

        att_to(b, 1 - ep).start()

    def take_chunk(p, chunk):
        @pl.when((p >= 0) & ((p > 0) | (chunk == 0) | (z < planes - 1)))
        def _():
            climb(p, chunk).wait_recv()
            climb_on(p, chunk)

    def whole_plane(p, b, masked):
        count = len(masked) * block
        attend_step(
            p, b, r.kvall[p, : len(masked)].reshape(count, 128),
            [(kb * block, block, (4 * p + kb) * block, masked[kb]) for kb in range(len(masked))],
        )

    def half_plane(b, here, first):
        attend_step(
            0, b, r.kvall[0, :, here, :].reshape(4 * rows, 128),
            [(kb * rows, rows, kb * block + first, kb == 0) for kb in range(4)],
        )

    def plane_forward(turn, carry):
        p = z - turn
        for b in (3, 2, 1, 0):

            @pl.when(turn == 0)
            def _():
                whole_plane(p, b, [kb in (0, b) for kb in range(b + 1)])

            @pl.when((turn > 0) & (p > 0))
            def _():
                whole_plane(p, b, [False] * 4)

            @pl.when((turn > 0) & (p == 0))
            def _():
                half_plane(b, mine, ep * rows)

            if b > 0:
                take_chunk(p - 1, 3 - b)

        @pl.when(turn == 0)
        def _():
            hand_second()

        return carry

    lax.fori_loop(0, z + 1, plane_forward, 0)

    @pl.when((z == planes - 1) & (z > 0))
    def _():
        climb(0, 1).wait_recv()
        climb(0, 2).wait_recv()

    for b in (3, 2, 1, 0):

        @pl.when(z > 0)
        def _():
            half_plane(b, theirs, rows - ep * rows)

        settle(b)

    def drain_forward():
        for chunk in range(3):
            wait_sent(three(chunk), r.kv_send.at[chunk])
        wait_sent(three_pieces, r.piece_send.at[0])

        @pl.when(z < planes - 1)
        def _():
            def left(p, carry):
                for chunk in range(3):
                    climb(p, chunk).wait_send()
                return carry

            lax.fori_loop(0, z + 1, left, 0)

    hand_last()
    send_od.wait_recv()

    def half_product(index, carry):
        which = jnp.where(index == 0, ep, 1 - ep)

        @pl.when(index == 0)
        def _():
            wait_received(r.o_out.at[pl.ds(0, 3)], r.att_recv.at[ep])

        @pl.when(index == 1)
        def _():
            wait_received(r.o_out, r.att_recv.at[1 - ep])

        r.halves[which] = dot(r.att_all[which], r.ow_all[which])
        r.half_mid[which] = dot(r.att_all[which], r.od_all[which], NT)
        return carry

    lax.fori_loop(0, 2, half_product, 0)
    mid_o = ((r.half_mid[0] + r.half_mid[1]) * r.mask[:, :SPAN]).astype(BF16)
    r.mid_o[...] = mid_o
    x2 = r.x_all[...].astype(F32) + (r.halves[0] + r.halves[1]) + dot(mid_o, r.o_up[...])
    r.x2[...] = x2
    h2 = rms(x2, r.moe_gain[...]).astype(BF16)
    r.h2[...] = h2
    send_hot.wait_recv()
    logits = dot(h2, r.router[...], NT)
    chosen = r.hot_all[:, : 2 * experts].astype(F32) > 0.5
    logits = jnp.where(chosen, logits, LOW)
    grown = jnp.where(chosen, jnp.exp(logits - jnp.max(logits, axis=1, keepdims=True)), 0.0)
    gates = grown / jnp.sum(grown, axis=1, keepdims=True)
    r.gates[...] = gates
    r.acc_out[...] = jnp.zeros(r.acc_out.shape, F32)
    r.acc_h2[...] = jnp.zeros(r.acc_h2.shape, F32)
    r.dgates[...] = jnp.zeros(r.dgates.shape, F32)
    lanes = 2 * SPAN
    load_in_down.wait()
    load_out_up.wait()
    send_g.wait_recv()
    in_down = r.in_down[...].reshape(experts * lanes, -1)
    out_up = r.out_up[...].reshape(experts * SPAN, -1)
    all_mids = dot(h2, in_down, NT)
    all_lifted = dot(r.g_all[...], out_up, NT)
    for e in range(experts):
        r.mid_in[e] = (all_mids[:, lanes * e : lanes * e + lanes] * r.mask[:, :lanes]).astype(BF16)
        r.lifted[e] = (all_lifted[:, SPAN * e : SPAN * e + SPAN] * r.mask[:, :SPAN]).astype(BF16)

    quarter = 2 * x + c

    def to_core(half, column):
        return remote(
            r.pack.at[half, 2 * column + 1 - c], r.core_land.at[half, column],
            r.core_send.at[half, column], r.core_recv.at[half, column], beside,
        )

    def to_column(half):
        return remote(
            r.pack.at[half, 2 * (1 - x) + c], r.x_land.at[half], r.x_send.at[half], r.x_recv.at[half], across
        )

    def add_core(half, column):
        to_core(half, column).wait_recv()
        number = 2 * column + c
        r.pack[half, number] = (
            r.pack[half, number].astype(F32) + r.core_land[half, column].astype(F32)
        ).astype(BF16)

    def final_rows(half, number):
        return (2 * number + half) * grad_rows

    def piece_of(owner):
        return (
            pl.multiple_of(owner // 4 * piece[0], piece[0]),
            pl.multiple_of(owner % 4 * piece[1], piece[1]),
        )

    def piece_in_pack(half, owner):
        row, lane = piece_of(owner)
        return r.pack.at[half, quarter, pl.ds(row, piece[0]), pl.ds(lane, piece[1])]

    def piece_in_final(half, owner):
        row, lane = piece_of(owner)
        start = pl.multiple_of(final_rows(half, quarter) + row, 16)
        return r.packed.at[pl.ds(start, piece[0]), pl.ds(lane, piece[1])]

    def plane_of(step):
        return lax.rem(z + step, planes)

    def give(half, step):
        other = plane_of(step)
        return remote(
            piece_in_pack(half, other), r.z_land.at[half, z], r.z_send.at[half, 0],
            r.z_recv.at[half, 0], {"ctx": block_of(other, x, c), "ep": ep},
        )

    def spread(half, step):
        other = plane_of(step)
        part = piece_in_final(half, z % owners)
        return remote(
            part, part, r.z_send.at[half, 1], r.z_recv.at[half, 1],
            {"ctx": block_of(other, x, c), "ep": ep},
        )

    def pieces(count):
        return r.z_land.at[0, pl.ds(0, count)]

    def for_pieces(wait, sem):
        if owners < planes:

            @pl.when(z < owners)
            def _():
                wait(pieces(owners - 1), sem)

            @pl.when(z >= owners)
            def _():
                wait(pieces(owners), sem)

        else:
            wait(pieces(owners - 1), sem)

    def each_plane(act, among_owners):
        def step(number, carry):
            if among_owners and owners < planes:

                @pl.when(plane_of(number) < owners)
                def _():
                    act(number)

            else:
                act(number)
            return carry

        lax.fori_loop(1, planes, step, 0)

    def if_owner(act):
        if owners < planes:
            pl.when(z < owners)(act)
        else:
            act()

    def over_final(half, number, way, target):
        part = r.packed.at[pl.ds(pl.multiple_of(final_rows(half, number), 16), grad_rows)]
        return remote(part, part, r.last_send.at[half, way, number], r.last_recv.at[half, number], target)

    def stage_pieces(half):
        to_column(half).wait_recv()
        r.pack[half, quarter] = (
            r.pack[half, quarter].astype(F32) + r.x_land[half].astype(F32)
        ).astype(BF16)
        each_plane(lambda step: give(half, step).start(), True)

    def stage_own(half):
        def act():
            wait_received(pieces(planes - 1), r.z_recv.at[half, 0])
            r.z_land[half, z] = piece_in_pack(half, z % owners)[...]

            def add(p, total):
                return total + r.z_land[half, p].astype(F32)

            total = lax.fori_loop(0, planes, add, jnp.zeros(piece, F32))
            piece_in_final(half, z % owners)[...] = total.astype(BF16)
            each_plane(lambda step: spread(half, step).start(), False)

        if_owner(act)

    def stage_column(half):
        for_pieces(wait_received, r.z_recv.at[half, 1])
        over_final(half, quarter, 0, across).start()
        over_final(half, quarter, 1, beside).start()

    def stage_core(half):
        over_final(half, 2 * (1 - x) + c, 0, across).wait_recv()
        over_final(half, 2 * (1 - x) + c, 1, beside).start()

    def stage_end(half):
        over_final(half, 2 * x + 1 - c, 1, beside).wait_recv()
        over_final(half, 2 * (1 - x) + 1 - c, 1, beside).wait_recv()

    def stage_drain(half):
        for_pieces(wait_sent, r.z_send.at[half, 0])
        if_owner(lambda: wait_sent(pieces(planes - 1), r.z_send.at[half, 1]))
        over_final(half, quarter, 0, across).wait_send()
        over_final(half, quarter, 1, beside).wait_send()
        over_final(half, 2 * (1 - x) + c, 1, beside).wait_send()
        to_core(half, 0).wait_send()
        to_core(half, 1).wait_send()
        to_column(half).wait_send()

    def one(turn, carry):
        slot = turn % slots
        e = expert_at(turn)
        half, q = turn // 4, quarter_at(turn % 4)
        for copy in expert_loads(turn):
            copy.wait()
        h2, g = r.h2[...], r.g_all[...]
        gate = jnp.sum(
            jnp.where(iota((block, 2 * experts), 1) == e + ep * experts, r.gates[...], 0.0), axis=1, keepdims=True
        )
        mid_in, lifted = r.mid_in[e], r.lifted[e]
        gate_part = dot(h2, r.w_in[slot, :, :FF]) + dot(mid_in[:, :SPAN], r.w_in_up[slot, 0])
        up_part = dot(h2, r.w_in[slot, :, FF:]) + dot(mid_in[:, SPAN:], r.w_in_up[slot, 1])
        d_act = dot(g, r.w_out[slot], NT) + dot(lifted, r.w_out_down[slot])
        squash = 1.0 / (1.0 + jnp.exp(-gate_part))
        silu = gate_part * squash
        act = (silu * up_part).astype(BF16)
        mid_out = dot(act, r.w_out_down[slot], NT) * r.mask[:, :SPAN]
        d_gate = jnp.sum(act.astype(F32) * d_act, axis=1, keepdims=True)
        r.dgates[...] += jnp.where(iota(r.dgates.shape, 1) == e, d_gate, 0.0)
        d_act = d_act * gate
        d_up = (d_act * silu).astype(BF16)
        d_gp = (d_act * up_part * squash * (1.0 + gate_part * (1.0 - squash))).astype(BF16)
        d_mid_in = (
            jnp.concatenate([dot(d_gp, r.w_in_up[slot, 0], NT), dot(d_up, r.w_in_up[slot, 1], NT)], axis=1)
            * r.mask[:, :lanes]
        ).astype(BF16)
        scaled_mid = (mid_out * gate).astype(BF16)
        r.d_mid_in[e] = d_mid_in
        r.mid_out[e] = scaled_mid
        r.acc_out[...] += dot((act.astype(F32) * gate).astype(BF16), r.w_out[slot])

        @pl.when(turn < experts - 2)
        def _():
            r.acc_h2[...] += dot(d_gp, r.w_in[slot, :, :FF], NT) + dot(d_up, r.w_in[slot, :, FF:], NT)

        @pl.when(turn >= experts - 2)
        def _():
            r.d_joint[turn - (experts - 2), :, :FF] = d_gp
            r.d_joint[turn - (experts - 2), :, FF:] = d_up

        r.pack[half, q, :64, :] = dot(d_mid_in, h2, TN).astype(BF16)
        r.pack[half, q, 64:96, :FF] = dot(mid_in[:, :SPAN], d_gp, TN).astype(BF16)
        r.pack[half, q, 64:96, FF:] = dot(mid_in[:, SPAN:], d_up, TN).astype(BF16)
        r.pack[half, q, 96:112, :] = fold(
            dot((lifted.astype(F32) * gate).astype(BF16), act, TN)
        ).astype(BF16)
        r.pack[half, q, 112:, :] = dot(scaled_mid, g, TN).astype(BF16)

        @pl.when(turn + slots < experts)
        def _():
            for copy in expert_loads(turn + slots):
                copy.start()

        @pl.when(turn % 4 == 0)
        def _():
            to_core(half, 1 - x).start()

        @pl.when(turn % 4 == 1)
        def _():
            to_core(half, x).start()

        @pl.when(turn % 4 == 2)
        def _():
            add_core(half, 1 - x)
            to_column(half).start()

        @pl.when(turn % 4 == 3)
        def _():
            add_core(half, x)

        @pl.when(turn == 5)
        def _():
            stage_pieces(0)

        return carry

    lax.fori_loop(0, experts, one, 0)
    every = range(experts)
    r.dg_trade[ep] = r.dgates[...].T[:8]
    send_dg = swap(9, r.dg_trade.at[ep], r.dg_trade.at[ep])
    send_dg.start()
    all_d_mids = jnp.concatenate([r.d_mid_in[e] for e in every], axis=1)
    tile = 256
    send_h2 = []
    for number in range(r.acc_h2.shape[1] // tile):
        columns = slice(tile * number, tile * number + tile)
        ends = r.acc_h2[:, columns] + dot(all_d_mids, r.in_down[:, :, columns].reshape(experts * lanes, tile))
        for index in (0, 1):
            ends = ends + dot(r.d_joint[index], r.w_in[(experts - 2 + index) % slots, columns, :], NT)
        r.trade[ep, :, columns] = ends.astype(BF16)
        part = r.trade.at[ep, :, columns]
        copy = swap((10, 3, 15, 16)[number], part, part)
        copy.start()
        send_h2.append(copy)
    r.acc_out[...] += dot(jnp.concatenate([r.mid_out[e] for e in every], axis=1), r.out_up[...].reshape(experts * SPAN, -1))
    r.out_trade[0] = r.acc_out[theirs, :].astype(BF16)
    send_out = swap(11, r.out_trade.at[0], r.out_trade.at[1])
    send_out.start()
    stage_own(0)
    stage_pieces(1)

    def small_sum(number, source, landing, result, shared):
        tiles = source.shape[0] // 16
        width = landing.shape[2]
        each = source.shape[1] // width
        holders = tiles * each
        shared = shared * each
        private = me >= shared
        mine_too = (me < holders) & (private | (me % 2 == ep))
        send_one, send_two = r.small_send.at[number, 0], r.small_send.at[number, 1]
        recv_one, recv_two = r.small_recv.at[number, 0], r.small_recv.at[number, 1]
        own_index = me + blocks * ep

        def region(ref, owner):
            return ref.at[span(owner // each * 16, 16), span(owner % each * width, width)]

        def several(count):
            return landing.at[pl.ds(0, count)]

        def scatter():
            def step(index, carry):
                owner = lax.rem(me + index, blocks)
                side = jnp.where(owner < shared, owner % 2, ep)

                @pl.when((owner < holders) & ((index > 0) | (side != ep)))
                def _():
                    remote(
                        region(source, owner), landing.at[own_index], send_one, recv_one, {"ctx": owner, "ep": side}
                    ).start()

                return carry

            lax.fori_loop(0, blocks, step, 0)

        def add(first, count):
            def step(p, sums):
                return sums + landing[p].astype(F32)

            return lax.fori_loop(first, first + count, step, jnp.zeros(landing.shape[1:], F32))

        def tell(side):
            part = region(result, me % holders)

            def step(index, carry):
                device = lax.rem(me + index, blocks)

                @pl.when((index > 0) | (side != ep))
                def _():
                    remote(part, part, send_two, recv_two, {"ctx": device, "ep": side}).start()

                return carry

            lax.fori_loop(0, blocks, step, 0)

        def total():
            @pl.when(mine_too)
            def _():
                landing[own_index] = region(source, me % holders)[...]

            @pl.when(mine_too & private)
            def _():
                wait_received(several(blocks - 1), recv_one)
                region(result, me % holders)[...] = add(blocks * ep, blocks).astype(BF16)
                tell(ep)

            if shared:

                @pl.when(mine_too & jnp.logical_not(private))
                def _():
                    wait_received(several(2 * blocks - 1), recv_one)
                    region(result, me % holders)[...] = add(0, 2 * blocks).astype(BF16)
                    tell(ep)
                    tell(1 - ep)

        def finish():
            @pl.when(mine_too)
            def _():
                wait_received(several(holders - 1), recv_two)
                wait_sent(several(holders - 1), send_one)

            @pl.when(jnp.logical_not(mine_too))
            def _():
                wait_received(several(holders), recv_two)
                wait_sent(several(holders), send_one)

            @pl.when(mine_too & private)
            def _():
                wait_sent(several(blocks - 1), send_two)

            if shared:

                @pl.when(mine_too & jnp.logical_not(private))
                def _():
                    wait_sent(several(2 * blocks - 1), send_two)

        return scatter, total, finish

    early_scatter, early_total, early_finish = small_sum(0, r.early, r.early_land, r.early_out, 0)
    late_scatter, late_total, late_finish = small_sum(1, r.late, r.late_land, r.late_out, 6)
    drain_forward()

    send_dg.wait_recv()
    blank = jnp.zeros((112, block), F32)
    table = jnp.concatenate([r.dg_trade[0], r.dg_trade[1], blank], axis=0).T
    d_gates = table[:, : 2 * experts]
    gates = r.gates[...]
    d_logits = (gates * (d_gates - jnp.sum(gates * d_gates, axis=1, keepdims=True))).astype(BF16)
    from_router = dot(d_logits, r.router[...])
    stage_column(0)
    for copy in send_h2:
        copy.wait_recv()
    d_h2 = r.trade[0].astype(F32) + r.trade[1].astype(F32) + from_router
    d_x2 = r.g_all[...].astype(F32) + rms_back(r.x2[...], r.moe_gain[...], d_h2)
    d_attn = d_x2.astype(BF16)
    r.acc_h2[...] = d_x2
    d_mid_o = (dot(d_attn, r.o_up[...], NT) * r.mask[:, :SPAN]).astype(BF16)

    d_att = (dot(d_attn, r.ow_all[ep], NT) + dot(d_mid_o, r.od_all[ep])).astype(BF16)
    for number in range(4):
        r.d_out[number] = d_att[:, 128 * number : 128 * number + 128]
    for step in (1, 2, 3):
        piece_to(*grad_pieces, step).start()
    r.dqt[...] = jnp.zeros(r.dqt.shape, F32)
    r.early[:32, :] = dot(r.mid_o[...], d_attn, TN).astype(BF16)
    r.early[32:48, :] = fold(dot(d_mid_o, r.att_all[ep], TN)).astype(BF16)
    r.early[48:, :] = jnp.zeros((16, r.early.shape[1]), BF16)
    early_scatter()
    stage_own(1)

    r.d_in[head] = r.d_out[head]
    wait_received(three_pieces, r.piece_recv.at[1])
    for b in range(4):
        received = r.d_in[b].astype(F32)
        turned = stack_columns(received)
        r.dt[b, HEAD:, :] = turned.astype(BF16)
        r.delta[b] = jnp.sum(turned * r.acc[b], axis=0, keepdims=True)
        r.dn[b] = stack_rows(received, True)

    def back_step(p, kb, kinds):
        kv = r.kvall[p, kb]
        grown = None
        for b, masked in kinds:
            pos_row, start_row = pos_rows[b], start_rows[b]
            s = dot(kv, r.qt[b])
            base = r.lse[b]
            if masked:
                key = (4 * p + kb) * block + iota(s.shape, 0)
                w = jnp.where((key <= pos_row) & (key >= start_row), jnp.exp(s - base), 0.0)
            else:
                w = jnp.exp(s - jnp.where(start_row <= (4 * p + 1) * block, base, -LOW))
            d_w = dot(kv, r.dt[b])
            d_s = (w * (d_w - r.delta[b])).astype(BF16)
            added = dot(d_s, r.qn[b]) + dot(w.astype(BF16), r.dn[b])
            grown = added if grown is None else grown + added
            r.dqt[b] += dot(kv, d_s, TN)[:HEAD]
        r.kvall[p, kb] = grown.astype(BF16)

    def lower(p):
        return remote(r.kvall.at[p], r.from_up.at[p % kept], r.down_send.at[p], r.down_recv.at[p], down)

    def finish(p):
        @pl.when(z < planes - 1)
        def _():
            lower(p).wait_recv()
            r.kvall[p] = (r.kvall[p].astype(F32) + r.from_up[p % kept].astype(F32)).astype(BF16)
            if planes > kept:

                @pl.when(p + kept <= z)
                def _():
                    pl.semaphore_signal(r.credit, inc=1, device_id=up, device_id_type=MESH)

        @pl.when(p < z)
        def _():
            if planes > kept:

                @pl.when(p >= kept)
                def _():
                    pl.semaphore_wait(r.credit, 1)

            lower(p).start()

    def back_to(source, landing, send, recv, b):
        return remote(source.at[b], landing.at[head], send, recv, device_of(b))

    def give_back(source, landing, send, recv, b):
        @pl.when(b == head)
        def _():
            landing[b] = source[b]

        @pl.when(b != head)
        def _():
            back_to(source, landing, send, recv, b).start()

    dq_pieces = (r.dq_out, r.dq_in, r.piece_send.at[2], r.piece_recv.at[2])
    dkv_pieces = (r.kvall.at[z], r.dkv_in, r.piece_send.at[3], r.piece_recv.at[3])

    def plane_back(p, carry):
        @pl.when(p < z)
        def _():
            @pl.when(p == 0)
            def _():
                back_step(p, 0, [(b, True) for b in range(4)])

            def middle(kb, inner):
                back_step(p, kb, [(b, False) for b in range(4)])
                return inner

            lax.fori_loop(jnp.where(p == 0, 1, 0), 2, middle, 0)

            @pl.when((p > 0) & (z < planes - 1))
            def _():
                finish(p - 1)

            lax.fori_loop(2, 4, middle, 0)

            @pl.when(z == planes - 1)
            def _():
                finish(p)

        @pl.when(p == z)
        def _():
            for kb in range(4):
                back_step(p, kb, [(b, b == kb or kb == 0) for b in range(kb, 4)])
                r.dq_out[kb] = (unstack(r.dqt[kb]) * SCALE).astype(BF16)
                give_back(*dq_pieces, kb)

                @pl.when(z == planes - 1)
                def _():
                    give_back(*dkv_pieces, kb)

                if kb == 1:

                    @pl.when((p > 0) & (z < planes - 1))
                    def _():
                        finish(p - 1)

        @pl.when(p == 0)
        def _():
            stage_core(0)

        @pl.when(p == 1)
        def _():
            stage_column(1)

        @pl.when(p == 2)
        def _():
            early_total()

        return carry

    lax.fori_loop(0, planes, plane_back, 0)

    @pl.when(z < planes - 1)
    def _():
        finish(z)
        for b in range(4):
            give_back(*dkv_pieces, b)

    cosine, sine = r.cosine[...], r.sine[...]
    wait_received(three_pieces, r.piece_recv.at[2])
    wait_received(three_pieces, r.piece_recv.at[3])
    d_query = jnp.concatenate([r.dq_in[number] for number in range(4)], axis=1)
    d_q = rotate(d_query.astype(F32), cosine, sine, -1.0).astype(BF16)
    d_key = jnp.concatenate([r.dkv_in[number, :, :HEAD] for number in range(4)], axis=1)
    d_k = rotate(d_key.astype(F32), cosine, sine, -1.0).astype(BF16)
    d_value = jnp.concatenate([r.dkv_in[number, :, HEAD:] for number in range(4)], axis=1)
    d_mids = jnp.concatenate(
        [dot(d_q, r.q_up[...], NT), dot(d_k, r.kv_up[0], NT), dot(d_value, r.kv_up[1], NT)], axis=1
    )
    d_mids = (d_mids * r.mask[:, : 3 * SPAN]).astype(BF16)
    r.late[:96, :] = dot(d_mids, r.h1[...], TN).astype(BF16)
    r.late[96:112, :] = fold(dot(r.mids[:, :SPAN], d_q, TN)).astype(BF16)
    r.late[112:, :] = fold(
        jnp.concatenate(
            [dot(r.mids[:, SPAN : 2 * SPAN], d_k, TN), dot(r.mids[:, 2 * SPAN :], d_value, TN)], axis=1
        )
    ).astype(BF16)
    late_scatter()
    full = (
        dot(d_q, r.q_w[...], NT) + dot(d_k, r.kv_w[0], NT) + dot(d_value, r.kv_w[1], NT) + dot(d_mids, r.qkv_down[...])
    )
    first, second = full[:rows], full[rows:]
    r.norm_trade[0] = jnp.where(ep == 0, second, first).astype(BF16)
    send_norm = swap(13, r.norm_trade.at[0], r.norm_trade.at[1])
    send_norm.start()
    stage_core(1)
    stage_end(0)
    early_finish()
    send_out.wait_recv()
    r.block_out[...] = (r.x2[mine, :] + (r.acc_out[mine, :] + r.out_trade[1].astype(F32))).astype(BF16)
    own = jnp.where(ep == 0, first, second)
    late_total()
    stage_end(1)

    def store(number, start, count):
        return pltpu.make_async_copy(
            r.packed.at[pl.ds(start, count)], r.out.at[pl.ds(start, count)], r.load_sem.at[number]
        )

    stores = [store(0, 0, base), store(1, base + 128, 128), store(2, base + 384, 64)]
    for copy in stores:
        copy.start()
    send_norm.wait_recv()
    own = own + r.norm_trade[1].astype(F32)
    r.in_grad[...] = (
        r.acc_h2[mine, :] + rms_back(r.x_all[mine, :].astype(F32), r.attn_gain[...], own)
    ).astype(BF16)
    stores.append(store(3, base + 256, 128))
    stores[-1].start()
    stage_drain(0)
    stage_drain(1)

    for copy in (*send_x, send_ow, send_od, send_hot, send_g, send_dg, *send_h2, send_out, send_norm):
        copy.wait_send()
    wait_sent(r.o_out.at[pl.ds(0, 3)], r.att_send.at[0])
    wait_sent(r.o_out, r.att_send.at[1])
    for number in (1, 2, 3):
        wait_sent(three_pieces, r.piece_send.at[number])
    hand_on(head, 0, across).wait_send()
    hand_on(head, 1, beside).wait_send()
    hand_on(sibling, 1, beside).wait_send()

    def drain(p, carry):
        lower(p).wait_send()
        return carry

    lax.fori_loop(0, z, drain, 0)
    late_finish()
    stores.append(store(4, base, 128))
    stores[-1].start()
    for copy in stores:
        copy.wait()


RESULTS = (
    "ein_down", "ein_up", "eout_down", "eout_up", "block_out", "in_grad", "g_down", "g_q", "g_kv", "g_od", "g_ou",
)


def unpack_kernel(packed, *refs):
    count = len(RESULTS)
    outs = dict(zip(RESULTS, refs[:count]))
    held = dict(zip(RESULTS, refs[count : 2 * count]))
    rows, sem_in, sem_out = refs[2 * count :]
    experts = outs["ein_down"].shape[0]
    grad_rows = 144
    base = experts * grad_rows

    def fetch(start, size, number):
        return pltpu.make_async_copy(
            packed.at[pl.ds(start, size)], rows.at[pl.ds(start, size)], sem_in.at[number]
        )

    fetches = [fetch(grad_rows * e, grad_rows, e) for e in range(experts)]
    fetches.append(fetch(base, rows.shape[0] - base, experts))
    for copy in fetches:
        copy.start()
    stores = []

    def store(name, number):
        copy = pltpu.make_async_copy(
            held[name] if number is None else held[name].at[number],
            outs[name] if number is None else outs[name].at[number],
            sem_out.at[len(stores)],
        )
        copy.start()
        stores.append(copy)

    for e in range(experts):
        fetches[e].wait()
        part = rows[grad_rows * e : grad_rows * e + grad_rows, :].astype(F32)
        held["ein_down"][e] = part[:64]
        held["ein_up"][e, 0] = part[64:96, :FF]
        held["ein_up"][e, 1] = part[64:96, FF:]
        held["eout_down"][e, :16] = part[96:112, :FF]
        held["eout_down"][e, 16:] = part[96:112, FF:]
        held["eout_up"][e] = part[112:]
        for name in RESULTS[:4]:
            store(name, e)
    fetches[experts].wait()
    late = rows[base : base + 128, :].astype(F32)
    early = rows[base + 384 : base + 448, :].astype(F32)
    held["block_out"][...] = rows[base + 128 : base + 256, :]
    held["in_grad"][...] = rows[base + 256 : base + 384, :]
    held["g_down"][...] = late[:96]
    held["g_q"][:16, :] = late[96:112, :FF]
    held["g_q"][16:, :] = late[96:112, FF:]
    kv = FF // 2
    for side in (0, 1):
        for half in (0, 1):
            first = kv * (2 * half + side)
            held["g_kv"][side, 16 * half : 16 * half + 16, :] = late[112:, first : first + kv]
    held["g_od"][:16, :] = early[32:48, :FF]
    held["g_od"][16:, :] = early[32:48, FF:]
    held["g_ou"][...] = early[:32]
    for name in RESULTS[4:]:
        store(name, None)
    for copy in stores:
        copy.wait()


def per_device(
    resid_in, out_grad, attn_gain, q_weight, key_value_weight, o_weight, moe_gain, router, expert_in,
    expert_out, qkv_down, q_up, key_value_up_factor, o_down, o_up, expert_in_down, expert_in_up,
    expert_out_down, expert_out_up, expert_ids, doc_starts, doc_adapter,
):
    blocks = lax.axis_size("ctx")
    planes = blocks // 4
    rows, width = resid_in.shape
    block = 2 * rows
    heads = q_weight.shape[1]
    kv = key_value_weight.shape[2]
    experts = expert_in.shape[0]
    slots = 6 if planes <= 4 else 4
    kept = planes if planes <= 4 else 2
    grad_rows = 2 * SPAN + SPAN + SPAN // 2 + SPAN
    base = experts * grad_rows
    groups = 3 if planes >= 12 else 1
    piece = (grad_rows // groups, width // 4)
    early_width = max(128, 4 * width // blocks)
    late_width = max(128, 8 * width // blocks)
    freq = np.tile(np.power(10000.0, -2.0 * np.arange(HEAD // 2) / HEAD).astype(np.float32), 4)[None, :]

    def shape(dims, kind=BF16):
        return jax.ShapeDtypeStruct(dims, kind)

    def dma(*dims):
        return pltpu.SemaphoreType.DMA(dims)

    def low(*dims):
        return pltpu.VMEM(dims, BF16)

    def full(*dims):
        return pltpu.VMEM(dims, F32)

    operands = dict(
        resid=resid_in, grad=out_grad, ids=expert_ids.T, starts=doc_starts, adapters=doc_adapter,
        attn_gain=attn_gain[None, :], moe_gain=moe_gain[None, :], freq=jnp.asarray(freq), qkv_down=qkv_down.T,
        q_up=q_up, kv_up=key_value_up_factor, o_down=o_down.T, o_up=o_up, router=router.T, q_hbm=q_weight,
        kv_hbm=key_value_weight, o_hbm=o_weight, in_hbm=expert_in, out_hbm=expert_out,
        in_down_hbm=jnp.swapaxes(expert_in_down, 1, 2), in_up_hbm=expert_in_up,
        out_down_hbm=jnp.swapaxes(expert_out_down, 1, 2), out_up_hbm=expert_out_up,
    )
    results = dict(out=shape((base + 448, width)))
    scratch = dict(
        q_w=low(*q_weight.shape), kv_w=low(*key_value_weight.shape), ow_all=low(2, heads, width),
        od_all=low(2, SPAN, heads), w_in=low(slots, *expert_in.shape[1:]), w_out=low(slots, *expert_out.shape[1:]),
        in_down=low(experts, 2 * SPAN, width), w_in_up=low(slots, *expert_in_up.shape[1:]),
        w_out_down=low(slots, SPAN, FF), out_up=low(experts, SPAN, width),
        mid_in=low(experts, block, 2 * SPAN), lifted=low(experts, block, SPAN),
        d_mid_in=low(experts, block, 2 * SPAN), d_joint=low(2, block, 2 * FF), mid_out=low(experts, block, SPAN),
        x_all=low(block, width), g_all=low(block, width), h1=low(block, width), h2=low(block, width),
        hot_all=low(block, 128), mask=full(block, 128), cosine=full(block, 128), sine=full(block, 128),
        mids=low(block, 3 * SPAN), kvall=low(planes, 4, block, 128), kv_out=low(4, block, 128), q_out=low(4, block, 128),
        q_in=low(4, block, 128), d_out=low(4, block, 128), d_in=low(4, block, 128), o_out=low(4, block, 128),
        dq_out=low(4, block, 128), dq_in=low(4, block, 128), dkv_in=low(4, block, 128), qt=low(4, 128, 2 * block),
        qn=low(4, 2 * block, 128), dt=low(4, 128, 2 * block), dn=low(4, 2 * block, 128),
        m_s=full(4, 1, 2 * block), l_s=full(4, 1, 2 * block), lse=full(4, 1, 2 * block),
        delta=full(4, 1, 2 * block), acc=full(4, HEAD, 2 * block), dqt=full(4, HEAD, 2 * block),
        att_all=low(2, block, heads), halves=full(2, block, width), half_mid=full(2, block, SPAN), mid_o=low(block, SPAN), x2=full(block, width),
        gates=full(block, 2 * experts), dgates=full(block, 128), trade=low(2, block, width), out_trade=low(2, rows, width),
        norm_trade=low(2, rows, width), dg_trade=full(2, 8, block),
        pack=low(2, 4, grad_rows, width), core_land=low(2, 2, grad_rows, width), x_land=low(2, grad_rows, width),
        z_land=low(2, planes, *piece), early=low(64, width), late=low(128, width),
        early_land=low(2 * blocks, 16, early_width), late_land=low(2 * blocks, 16, late_width),
        from_up=low(kept, 4, block, 128), credit=pltpu.SemaphoreType.REGULAR,
        packed=low(base + 448, width), load_sem=dma(5), expert_sem=dma(slots, 4), pair_send=dma(17), pair_recv=dma(17),
        kv_send=dma(3), kv_recv=dma(3), piece_send=dma(4), piece_recv=dma(4), up_send=dma(planes, 3),
        up_recv=dma(planes, 3), ow_send=dma(4, 2), ow_recv=dma(4), att_send=dma(2), att_recv=dma(2), core_send=dma(2, 2), core_recv=dma(2, 2),
        x_send=dma(2), x_recv=dma(2), z_send=dma(2, 2), z_recv=dma(2, 2), last_send=dma(2, 2, 4),
        last_recv=dma(2, 4),
        small_send=dma(2, 2), small_recv=dma(2, 2), down_send=dma(planes),
        down_recv=dma(planes),
    )
    (out,) = pl.pallas_call(
        functools.partial(layer_kernel, planes, slots, INPUTS + OUTPUTS + tuple(scratch)),
        out_shape=[results[name] for name in OUTPUTS],
        in_specs=[
            SMEM if name in ("starts", "adapters") else HBM if name.endswith("hbm") else VMEM for name in INPUTS
        ],
        out_specs=[HBM] * len(OUTPUTS),
        scratch_shapes=list(scratch.values()),
        compiler_params=pltpu.CompilerParams(
            collective_id=1, has_side_effects=True, vmem_limit_bytes=62 << 20
        ),
        name="layer",
    )(*[operands[name] for name in INPUTS])

    unpacked = dict(
        ein_down=shape((experts, 2 * SPAN, width), F32), ein_up=shape((experts, 2, SPAN, FF), F32),
        eout_down=shape((experts, SPAN, FF), F32), eout_up=shape((experts, SPAN, width), F32),
        block_out=shape((rows, width)), in_grad=shape((rows, width)), g_down=shape((3 * SPAN, width), F32),
        g_q=shape((SPAN, heads), F32), g_kv=shape((2, SPAN, kv), F32), g_od=shape((SPAN, heads), F32),
        g_ou=shape((SPAN, width), F32),
    )
    ein_down, ein_up, eout_down, eout_up, block_out, in_grad, g_down, g_q, g_kv, g_od, g_ou = pl.pallas_call(
        unpack_kernel,
        out_shape=[unpacked[name] for name in RESULTS],
        in_specs=[HBM],
        out_specs=[HBM] * len(RESULTS),
        scratch_shapes=[
            *[pltpu.VMEM(unpacked[name].shape, unpacked[name].dtype) for name in RESULTS],
            pltpu.VMEM(out.shape, BF16), dma(experts + 1), dma(4 * experts + 7),
        ],
        compiler_params=pltpu.CompilerParams(vmem_limit_bytes=62 << 20),
        name="unpack",
    )(out)
    return (
        block_out, in_grad, g_down.T, g_q, g_kv, g_od.T, g_ou, jnp.swapaxes(ein_down, 1, 2), ein_up,
        jnp.swapaxes(eout_down, 1, 2), eout_up,
    )


def solution(mesh):
    placed = (
        P(("ctx", "ep"), None),
        P(("ctx", "ep"), None),
        P(),
        P(None, "ep"),
        P(None, None, "ep"),
        P("ep", None),
        P(),
        P(),
        P("ep", None, None),
        P("ep", None, None),
        P(),
        P(None, "ep"),
        P(None, None, "ep"),
        P("ep", None),
        P(),
        P("ep", None, None),
        P("ep", None, None, None),
        P("ep", None, None),
        P("ep", None, None),
        P(("ctx", "ep"), None),
        P(),
        P(),
    )
    return jax.shard_map(
        per_device,
        mesh=mesh,
        in_specs=placed,
        out_specs=(
            P(("ctx", "ep"), None),
            P(("ctx", "ep"), None),
            P(),
            P(None, "ep"),
            P(None, None, "ep"),
            P("ep", None),
            P(),
            P("ep", None, None),
            P("ep", None, None, None),
            P("ep", None, None),
            P("ep", None, None),
        ),
        check_vma=False,
    )
```

```python
import functools

import jax
import jax.numpy as jnp
import numpy as np
from jax import lax
from jax.experimental import pallas as pl
from jax.experimental.pallas import tpu as pltpu
from jax.sharding import PartitionSpec as P

MESH = pl.DeviceIdType.MESH
VMEM = pl.BlockSpec(memory_space=pltpu.VMEM)
SMEM = pl.BlockSpec(memory_space=pltpu.SMEM)
HBM = pl.BlockSpec(memory_space=pl.ANY)
F32 = jnp.float32
BF16 = jnp.bfloat16

HEAD = 64
FF = 512
RANK = 16
SPAN = 32
EPS = 1e-06
LOW = -1e30
SCALE = 0.125

NN = (((1,), (0,)), ((), ()))
NT = (((1,), (1,)), ((), ()))
TN = (((0,), (0,)), ((), ()))


def dot(left, right, dims=NN):
    return lax.dot_general(left, right, dims, preferred_element_type=F32)


def iota(shape, dim):
    return lax.broadcasted_iota(jnp.int32, shape, dim)


def rms(values, gain):
    return values * lax.rsqrt(jnp.mean(values * values, axis=-1, keepdims=True) + EPS) * gain


def rms_back(values, gain, upstream):
    factor = lax.rsqrt(jnp.mean(values * values, axis=-1, keepdims=True) + EPS)
    scaled = upstream * gain
    return factor * scaled - values * factor * factor * factor * jnp.mean(
        scaled * values, axis=-1, keepdims=True
    )


def rotate(values, cosine, sine, sign):
    width = values.shape[1]
    copies = width // 128
    cosine = jnp.concatenate([cosine] * copies, axis=1)
    sine = jnp.concatenate([sine] * copies, axis=1)
    first = iota(values.shape, 1) % HEAD < HEAD // 2
    ahead = pltpu.roll(values, width - HEAD // 2, 1)
    behind = pltpu.roll(values, HEAD // 2, 1)
    return values * cosine + sign * jnp.where(first, -ahead, behind) * sine


def doc_scan(positions, starts_ref, adapters_ref):
    own_start = jnp.zeros(positions.shape, jnp.int32)
    adapter = jnp.zeros(positions.shape, jnp.int32)
    for number in range(starts_ref.shape[0]):
        opened = starts_ref[number] <= positions
        own_start = jnp.where(opened, starts_ref[number], own_start)
        adapter = jnp.where(opened, adapters_ref[number], adapter)
    return own_start, adapter


def place():
    me = lax.axis_index("ctx")
    ep = lax.axis_index("ep")
    return me, ep, me // 4, (me // 2) % 2, me % 2


def block_of(z, x, c):
    return (z * 2 + x) * 2 + c


def signal(device):
    pl.semaphore_signal(
        pltpu.get_barrier_semaphore(), inc=1, device_id=device, device_id_type=MESH
    )


def remote(src, dst, send, recv, device):
    return pltpu.make_async_remote_copy(
        src_ref=src,
        dst_ref=dst,
        send_sem=send,
        recv_sem=recv,
        device_id=device,
        device_id_type=MESH,
    )


def span(start, count):
    return pl.ds(pl.multiple_of(start, count), count)


def stack_rows(piece, upper):
    turned = pltpu.roll(piece, HEAD, 1)
    keep = iota(piece.shape, 1) >= HEAD if upper else iota(piece.shape, 1) < HEAD
    first, second = (turned, piece) if upper else (piece, turned)
    blank = jnp.zeros(piece.shape, piece.dtype)
    return jnp.concatenate([jnp.where(keep, first, blank), jnp.where(keep, second, blank)], axis=0).astype(BF16)


def stack_columns(piece):
    turned = piece.T
    return jnp.concatenate([turned[:HEAD], turned[HEAD:]], axis=1)


def unstack(columns):
    count = columns.shape[1] // 2
    return jnp.concatenate([columns[:, :count], columns[:, count:]], axis=0).T


def fold(wide):
    count = wide.shape[0] // 2
    return jnp.concatenate([wide[:count], wide[count:]], axis=1)


INPUTS = (
    "resid", "grad", "ids", "starts", "adapters", "attn_gain", "moe_gain", "freq",
    "qkv_down", "q_up", "kv_up", "o_down", "o_up", "router",
    "q_hbm", "kv_hbm", "o_hbm", "in_hbm", "out_hbm", "in_down_hbm", "in_up_hbm", "out_down_hbm", "out_up_hbm",
)
OUTPUTS = ("out",)


def layer_kernel(planes, slots, names, *refs):
    r = dict(zip(names, refs))
    r = type("Refs", (), r)
    r.acc_out, r.acc_h2 = r.halves.at[0], r.halves.at[1]
    grad_rows = r.pack.shape[2]
    base = r.in_hbm.shape[0] * grad_rows
    r.late_out = r.packed.at[pl.ds(base, 128)]
    r.block_out = r.packed.at[pl.ds(base + 128, 128)]
    r.in_grad = r.packed.at[pl.ds(base + 256, 128)]
    r.early_out = r.packed.at[pl.ds(base + 384, 64)]
    me, ep, z, x, c = place()
    blocks = 4 * planes
    pair = {"ctx": me, "ep": 1 - ep}
    head = 2 * x + c
    up = {"ctx": jnp.minimum(me + 4, blocks - 1), "ep": ep}
    down = {"ctx": jnp.maximum(me - 4, 0), "ep": ep}
    across = {"ctx": block_of(z, 1 - x, c), "ep": ep}
    beside = {"ctx": block_of(z, x, 1 - c), "ep": ep}
    rows = r.resid.shape[0]
    block = 2 * rows
    mine = span(ep * rows, rows)
    theirs = span(rows - ep * rows, rows)
    experts = r.in_hbm.shape[0]
    groups = 3 if planes >= 12 else 1
    owners = 4 * groups
    piece = (grad_rows // groups, r.pack.shape[3] // 4)
    kept = r.from_up.shape[0]

    load_q = pltpu.make_async_copy(r.q_hbm, r.q_w, r.load_sem.at[0])
    load_kv = pltpu.make_async_copy(r.kv_hbm, r.kv_w, r.load_sem.at[1])
    load_o = pltpu.make_async_copy(r.o_hbm, r.ow_all.at[ep], r.load_sem.at[2])
    load_kv.start()
    load_q.start()
    load_o.start()
    load_in_down = pltpu.make_async_copy(r.in_down_hbm, r.in_down, r.load_sem.at[3])
    load_out_up = pltpu.make_async_copy(r.out_up_hbm, r.out_up, r.load_sem.at[4])
    load_in_down.start()
    load_out_up.start()
    weights = (
        (r.in_hbm, r.w_in), (r.out_hbm, r.w_out), (r.in_up_hbm, r.w_in_up), (r.out_down_hbm, r.w_out_down),
    )

    def quarter_at(turn):
        return jnp.where(turn % 2 == 0, 1 - x, x) * 2 + jnp.where(turn < 2, 1 - c, c)

    def expert_at(turn):
        return 2 * quarter_at(turn % 4) + turn // 4

    def expert_loads(turn):
        e, slot = expert_at(turn), turn % slots
        return [
            pltpu.make_async_copy(source.at[e], held.at[slot], r.expert_sem.at[slot, number])
            for number, (source, held) in enumerate(weights)
        ]

    def begin(turn, carry):
        for copy in expert_loads(turn):
            copy.start()
        return carry

    lax.fori_loop(0, slots, begin, 0)

    def greet(step, carry):
        signal({"ctx": lax.rem(me + step, blocks), "ep": ep})
        signal({"ctx": lax.rem(me + step, blocks), "ep": 1 - ep})
        return carry

    signal(pair)
    lax.fori_loop(1, blocks, greet, 0)
    pl.semaphore_wait(pltpu.get_barrier_semaphore(), 2 * blocks - 1)

    def wait_sent(like, sem):
        remote(like, like, sem, sem, pair).wait_send()

    def wait_received(like, sem):
        remote(like, like, sem, sem, pair).wait_recv()

    def swap(number, src, dst):
        return remote(src, dst, r.pair_send.at[number], r.pair_recv.at[number], pair)

    small = rows // 2
    chunks = (
        (mine, rows),
        (span(rows - ep * rows, small), small),
        (span(rows - ep * rows + small, small), small),
    )
    send_x = []
    for number in (0, 1):
        part = pl.ds(small * number, small)
        copy = swap(number, r.resid.at[part], r.x_all.at[span(ep * rows + small * number, small)])
        copy.start()
        send_x.append(copy)

    hot = jnp.zeros((r.ids.shape[0], rows), F32)
    hot = jnp.zeros((128, rows), F32)
    numbers = iota((128, rows), 0)
    for choice in range(r.ids.shape[0]):
        hot = hot + jnp.where(r.ids[choice : choice + 1, :] == numbers, 1.0, 0.0)
    r.hot_all[mine, :] = hot.T.astype(BF16)
    r.x_all[mine, :] = r.resid[...]
    r.g_all[mine, :] = r.grad[...]
    r.od_all[ep] = r.o_down[...]
    position = me * block + iota((block, 128), 0)
    own_start, adapter = doc_scan(position, r.starts, r.adapters)
    r.mask[...] = jnp.where((iota((block, 128), 1) % SPAN) // RANK == adapter, 1.0, 0.0)
    angles = (position - own_start).astype(F32) * r.freq[...]
    r.cosine[...] = jnp.cos(angles)
    r.sine[...] = jnp.sin(angles)
    pos_rows = [((4 * z + b) * block + iota((8, 2 * block), 1) % block)[:1] for b in range(4)]
    start_rows = [
        doc_scan((4 * z + b) * block + iota((8, 2 * block), 1) % block, r.starts, r.adapters)[0][:1] for b in range(4)
    ]

    def other_head(step):
        return lax.rem(head + step, 4)

    def device_of(number):
        return {"ctx": 4 * z + number, "ep": ep}

    def kv_to(step, chunk):
        number = other_head(step)
        here = chunks[chunk][0]
        return remote(
            r.kv_out.at[number, here, :], r.kvall.at[z, head, here, :],
            r.kv_send.at[chunk], r.kv_recv.at[chunk], device_of(number),
        )

    def three(chunk):
        return r.kv_out.at[pl.ds(0, 3), chunks[chunk][0], :]

    def piece_to(source, landing, send, recv, step):
        number = other_head(step)
        return remote(source.at[number], landing.at[head], send, recv, device_of(number))

    three_pieces = r.q_out.at[pl.ds(0, 3)]

    query_pieces = (r.q_out, r.q_in, r.piece_send.at[0], r.piece_recv.at[0])
    grad_pieces = (r.d_out, r.d_in, r.piece_send.at[1], r.piece_recv.at[1])

    def climb(p, half):
        part = r.kvall.at[p, :, chunks[half][0], :]
        return remote(part, part, r.up_send.at[p, half], r.up_recv.at[p, half], up)

    def climb_on(p, half):
        @pl.when(z < planes - 1)
        def _():
            climb(p, half).start()

    def collect(half):
        wait_received(three(half), r.kv_recv.at[half])
        climb_on(z, half)

    def project(here):
        h1 = rms(r.x_all[here, :].astype(F32), r.attn_gain[...]).astype(BF16)
        r.h1[here, :] = h1
        mids = (dot(h1, r.qkv_down[...], NT) * r.mask[here, : 3 * SPAN]).astype(BF16)
        r.mids[here, :] = mids
        k_lin = dot(h1, r.kv_w[0]) + dot(mids[:, SPAN : 2 * SPAN], r.kv_up[0])
        keys = rotate(k_lin, r.cosine[here, :], r.sine[here, :], 1.0)
        values = dot(h1, r.kv_w[1]) + dot(mids[:, 2 * SPAN :], r.kv_up[1])
        for number in range(4):
            lanes = slice(HEAD * number, HEAD * number + HEAD)
            r.kv_out[number, here, :] = jnp.concatenate([keys[:, lanes], values[:, lanes]], axis=1).astype(BF16)
        r.kvall[z, head, here, :] = r.kv_out[head, here, :]

    load_kv.wait()
    project(mine)
    for step in (1, 2, 3):
        kv_to(step, 0).start()
    send_x[0].wait_recv()
    project(chunks[1][0])
    for step in (1, 2, 3):
        kv_to(step, 1).start()
    collect(0)
    send_x[1].wait_recv()
    load_o.wait()

    def ow_quarter(side, number):
        return r.ow_all.at[side, pl.ds(pl.multiple_of(128 * number, 128), 128), :]

    def hand_on(number, way, target):
        part = ow_quarter(1 - ep, number)
        return remote(part, part, r.ow_send.at[number, way], r.ow_recv.at[number], target)

    sibling = 2 * (1 - x) + c

    def hand_first():
        send_ow.wait_recv()
        hand_on(head, 0, across).start()
        hand_on(head, 1, beside).start()

    def hand_second():
        hand_on(sibling, 0, across).wait_recv()
        hand_on(sibling, 1, beside).start()

    def hand_last():
        hand_on(2 * x + 1 - c, 1, beside).wait_recv()
        hand_on(2 * (1 - x) + 1 - c, 1, beside).wait_recv()

    send_ow = swap(12, ow_quarter(ep, head), ow_quarter(ep, head))
    send_od = swap(4, r.od_all.at[ep], r.od_all.at[ep])
    send_hot = swap(14, r.hot_all.at[mine], r.hot_all.at[mine])
    send_g = swap(2, r.grad, r.g_all.at[mine])
    for copy in (send_ow, send_od, send_hot):
        copy.start()
    project(chunks[2][0])
    for step in (1, 2, 3):
        kv_to(step, 2).start()
    load_q.wait()
    q_lin = dot(r.h1[...], r.q_w[...]) + dot(r.mids[:, :SPAN], r.q_up[...])
    query = rotate(q_lin, r.cosine[...], r.sine[...], 1.0).astype(BF16)
    for number in range(4):
        r.q_out[number] = query[:, 128 * number : 128 * number + 128]
    for step in (1, 2, 3):
        piece_to(*query_pieces, step).start()
    collect(1)
    send_g.start()
    hand_first()
    r.q_in[head] = r.q_out[head]
    r.m_s[...] = jnp.full(r.m_s.shape, LOW, F32)
    r.l_s[...] = jnp.zeros(r.l_s.shape, F32)
    r.acc[...] = jnp.zeros(r.acc.shape, F32)
    r.qt[:, HEAD:, :] = jnp.zeros((4, HEAD, 2 * block), BF16)
    r.dt[:, :HEAD, :] = jnp.zeros((4, HEAD, 2 * block), BF16)
    collect(2)
    wait_received(three_pieces, r.piece_recv.at[0])
    for b in range(4):
        scaled = r.q_in[b].astype(F32) * SCALE
        r.qt[b, :HEAD, :] = stack_columns(scaled).astype(BF16)
        r.qn[b] = stack_rows(scaled, False)

    def attend_step(p, b, keys, kinds):
        pos_row, start_row = pos_rows[b], start_rows[b]
        sees = start_row <= (4 * p + 1) * block
        everything = dot(keys, r.qt[b])
        scores, peak = [], None
        for first, count, position, masked in kinds:
            s = everything[first : first + count]
            if masked:
                key = position + iota(s.shape, 0)
                s = jnp.where((key <= pos_row) & (key >= start_row), s, LOW)
            scores.append(s)
            highest = jnp.max(s, axis=0, keepdims=True)
            if not masked:
                highest = jnp.where(sees, highest, LOW)
            peak = highest if peak is None else jnp.maximum(peak, highest)
        old = r.m_s[b]
        new = jnp.maximum(old, peak)
        r.m_s[b] = new
        blind = jnp.where(sees, new, -LOW)
        decay = jnp.exp(old - new)
        total = r.l_s[b] * decay
        weights = []
        for (first, count, position, masked), s in zip(kinds, scores):
            w = jnp.exp(s - (new if masked else blind))
            total = total + jnp.sum(w, axis=0, keepdims=True)
            weights.append(w.astype(BF16))
        weights = jnp.concatenate(weights, axis=0) if len(weights) > 1 else weights[0]
        r.l_s[b] = total
        r.acc[b] = r.acc[b] * decay + dot(keys, weights, TN)[HEAD:]

    def att_to(b, side):
        return remote(
            r.o_out.at[b], r.att_all.at[ep, :, pl.ds(pl.multiple_of(128 * head, 128), 128)],
            r.att_send.at[jnp.where(side == ep, 0, 1)], r.att_recv.at[ep], {"ctx": 4 * z + b, "ep": side},
        )

    def settle(b):
        r.lse[b] = r.m_s[b] + jnp.log(r.l_s[b])
        done = r.acc[b] / r.l_s[b]
        r.acc[b] = done
        r.o_out[b] = unstack(done).astype(BF16)

        @pl.when(b == head)
        def _():
            r.att_all[ep, :, pl.ds(pl.multiple_of(128 * head, 128), 128)] = r.o_out[b]

        @pl.when(b != head)
        def _():
            att_to(b, ep).start()

        att_to(b, 1 - ep).start()

    def take_chunk(p, chunk):
        @pl.when((p >= 0) & ((p > 0) | (chunk == 0) | (z < planes - 1)))
        def _():
            climb(p, chunk).wait_recv()
            climb_on(p, chunk)

    def whole_plane(p, b, masked):
        count = len(masked) * block
        attend_step(
            p, b, r.kvall[p, : len(masked)].reshape(count, 128),
            [(kb * block, block, (4 * p + kb) * block, masked[kb]) for kb in range(len(masked))],
        )

    def half_plane(b, here, first):
        attend_step(
            0, b, r.kvall[0, :, here, :].reshape(4 * rows, 128),
            [(kb * rows, rows, kb * block + first, kb == 0) for kb in range(4)],
        )

    def plane_forward(turn, carry):
        p = z - turn
        for b in (3, 2, 1, 0):

            @pl.when(turn == 0)
            def _():
                whole_plane(p, b, [kb in (0, b) for kb in range(b + 1)])

            @pl.when((turn > 0) & (p > 0))
            def _():
                whole_plane(p, b, [False] * 4)

            @pl.when((turn > 0) & (p == 0))
            def _():
                half_plane(b, mine, ep * rows)

            if b > 0:
                take_chunk(p - 1, 3 - b)

        @pl.when(turn == 0)
        def _():
            hand_second()

        return carry

    lax.fori_loop(0, z + 1, plane_forward, 0)

    @pl.when((z == planes - 1) & (z > 0))
    def _():
        climb(0, 1).wait_recv()
        climb(0, 2).wait_recv()

    for b in (3, 2, 1, 0):

        @pl.when(z > 0)
        def _():
            half_plane(b, theirs, rows - ep * rows)

        settle(b)

    def drain_forward():
        for chunk in range(3):
            wait_sent(three(chunk), r.kv_send.at[chunk])
        wait_sent(three_pieces, r.piece_send.at[0])

        @pl.when(z < planes - 1)
        def _():
            def left(p, carry):
                for chunk in range(3):
                    climb(p, chunk).wait_send()
                return carry

            lax.fori_loop(0, z + 1, left, 0)

    hand_last()
    send_od.wait_recv()

    def half_product(index, carry):
        which = jnp.where(index == 0, ep, 1 - ep)

        @pl.when(index == 0)
        def _():
            wait_received(r.o_out.at[pl.ds(0, 3)], r.att_recv.at[ep])

        @pl.when(index == 1)
        def _():
            wait_received(r.o_out, r.att_recv.at[1 - ep])

        r.halves[which] = dot(r.att_all[which], r.ow_all[which])
        r.half_mid[which] = dot(r.att_all[which], r.od_all[which], NT)
        return carry

    lax.fori_loop(0, 2, half_product, 0)
    mid_o = ((r.half_mid[0] + r.half_mid[1]) * r.mask[:, :SPAN]).astype(BF16)
    r.mid_o[...] = mid_o
    x2 = r.x_all[...].astype(F32) + (r.halves[0] + r.halves[1]) + dot(mid_o, r.o_up[...])
    r.x2[...] = x2
    h2 = rms(x2, r.moe_gain[...]).astype(BF16)
    r.h2[...] = h2
    send_hot.wait_recv()
    logits = dot(h2, r.router[...], NT)
    chosen = r.hot_all[:, : 2 * experts].astype(F32) > 0.5
    logits = jnp.where(chosen, logits, LOW)
    grown = jnp.where(chosen, jnp.exp(logits - jnp.max(logits, axis=1, keepdims=True)), 0.0)
    gates = grown / jnp.sum(grown, axis=1, keepdims=True)
    r.gates[...] = gates
    r.acc_out[...] = jnp.zeros(r.acc_out.shape, F32)
    r.acc_h2[...] = jnp.zeros(r.acc_h2.shape, F32)
    r.dgates[...] = jnp.zeros(r.dgates.shape, F32)
    lanes = 2 * SPAN
    load_in_down.wait()
    load_out_up.wait()
    send_g.wait_recv()
    in_down = r.in_down[...].reshape(experts * lanes, -1)
    out_up = r.out_up[...].reshape(experts * SPAN, -1)
    all_mids = dot(h2, in_down, NT)
    all_lifted = dot(r.g_all[...], out_up, NT)
    for e in range(experts):
        r.mid_in[e] = (all_mids[:, lanes * e : lanes * e + lanes] * r.mask[:, :lanes]).astype(BF16)
        r.lifted[e] = (all_lifted[:, SPAN * e : SPAN * e + SPAN] * r.mask[:, :SPAN]).astype(BF16)

    quarter = 2 * x + c

    def to_core(half, column):
        return remote(
            r.pack.at[half, 2 * column + 1 - c], r.core_land.at[half, column],
            r.core_send.at[half, column], r.core_recv.at[half, column], beside,
        )

    def to_column(half):
        return remote(
            r.pack.at[half, 2 * (1 - x) + c], r.x_land.at[half], r.x_send.at[half], r.x_recv.at[half], across
        )

    def add_core(half, column):
        to_core(half, column).wait_recv()
        number = 2 * column + c
        r.pack[half, number] = (
            r.pack[half, number].astype(F32) + r.core_land[half, column].astype(F32)
        ).astype(BF16)

    def final_rows(half, number):
        return (2 * number + half) * grad_rows

    def piece_of(owner):
        return (
            pl.multiple_of(owner // 4 * piece[0], piece[0]),
            pl.multiple_of(owner % 4 * piece[1], piece[1]),
        )

    def piece_in_pack(half, owner):
        row, lane = piece_of(owner)
        return r.pack.at[half, quarter, pl.ds(row, piece[0]), pl.ds(lane, piece[1])]

    def piece_in_final(half, owner):
        row, lane = piece_of(owner)
        start = pl.multiple_of(final_rows(half, quarter) + row, 16)
        return r.packed.at[pl.ds(start, piece[0]), pl.ds(lane, piece[1])]

    def plane_of(step):
        return lax.rem(z + step, planes)

    def give(half, step):
        other = plane_of(step)
        return remote(
            piece_in_pack(half, other), r.z_land.at[half, z], r.z_send.at[half, 0],
            r.z_recv.at[half, 0], {"ctx": block_of(other, x, c), "ep": ep},
        )

    def spread(half, step):
        other = plane_of(step)
        part = piece_in_final(half, z % owners)
        return remote(
            part, part, r.z_send.at[half, 1], r.z_recv.at[half, 1],
            {"ctx": block_of(other, x, c), "ep": ep},
        )

    def pieces(count):
        return r.z_land.at[0, pl.ds(0, count)]

    def for_pieces(wait, sem):
        if owners < planes:

            @pl.when(z < owners)
            def _():
                wait(pieces(owners - 1), sem)

            @pl.when(z >= owners)
            def _():
                wait(pieces(owners), sem)

        else:
            wait(pieces(owners - 1), sem)

    def each_plane(act, among_owners):
        def step(number, carry):
            if among_owners and owners < planes:

                @pl.when(plane_of(number) < owners)
                def _():
                    act(number)

            else:
                act(number)
            return carry

        lax.fori_loop(1, planes, step, 0)

    def if_owner(act):
        if owners < planes:
            pl.when(z < owners)(act)
        else:
            act()

    def over_final(half, number, way, target):
        part = r.packed.at[pl.ds(pl.multiple_of(final_rows(half, number), 16), grad_rows)]
        return remote(part, part, r.last_send.at[half, way, number], r.last_recv.at[half, number], target)

    def stage_pieces(half):
        to_column(half).wait_recv()
        r.pack[half, quarter] = (
            r.pack[half, quarter].astype(F32) + r.x_land[half].astype(F32)
        ).astype(BF16)
        each_plane(lambda step: give(half, step).start(), True)

    def stage_own(half):
        def act():
            wait_received(pieces(planes - 1), r.z_recv.at[half, 0])
            r.z_land[half, z] = piece_in_pack(half, z % owners)[...]

            def add(p, total):
                return total + r.z_land[half, p].astype(F32)

            total = lax.fori_loop(0, planes, add, jnp.zeros(piece, F32))
            piece_in_final(half, z % owners)[...] = total.astype(BF16)
            each_plane(lambda step: spread(half, step).start(), False)

        if_owner(act)

    def stage_column(half):
        for_pieces(wait_received, r.z_recv.at[half, 1])
        over_final(half, quarter, 0, across).start()
        over_final(half, quarter, 1, beside).start()

    def stage_core(half):
        over_final(half, 2 * (1 - x) + c, 0, across).wait_recv()
        over_final(half, 2 * (1 - x) + c, 1, beside).start()

    def stage_end(half):
        over_final(half, 2 * x + 1 - c, 1, beside).wait_recv()
        over_final(half, 2 * (1 - x) + 1 - c, 1, beside).wait_recv()

    def stage_drain(half):
        for_pieces(wait_sent, r.z_send.at[half, 0])
        if_owner(lambda: wait_sent(pieces(planes - 1), r.z_send.at[half, 1]))
        over_final(half, quarter, 0, across).wait_send()
        over_final(half, quarter, 1, beside).wait_send()
        over_final(half, 2 * (1 - x) + c, 1, beside).wait_send()
        to_core(half, 0).wait_send()
        to_core(half, 1).wait_send()
        to_column(half).wait_send()

    def one(turn, carry):
        slot = turn % slots
        e = expert_at(turn)
        half, q = turn // 4, quarter_at(turn % 4)
        for copy in expert_loads(turn):
            copy.wait()
        h2, g = r.h2[...], r.g_all[...]
        gate = jnp.sum(
            jnp.where(iota((block, 2 * experts), 1) == e + ep * experts, r.gates[...], 0.0), axis=1, keepdims=True
        )
        mid_in, lifted = r.mid_in[e], r.lifted[e]
        gate_part = dot(h2, r.w_in[slot, :, :FF]) + dot(mid_in[:, :SPAN], r.w_in_up[slot, 0])
        up_part = dot(h2, r.w_in[slot, :, FF:]) + dot(mid_in[:, SPAN:], r.w_in_up[slot, 1])
        d_act = dot(g, r.w_out[slot], NT) + dot(lifted, r.w_out_down[slot])
        squash = 1.0 / (1.0 + jnp.exp(-gate_part))
        silu = gate_part * squash
        act = (silu * up_part).astype(BF16)
        mid_out = dot(act, r.w_out_down[slot], NT) * r.mask[:, :SPAN]
        d_gate = jnp.sum(act.astype(F32) * d_act, axis=1, keepdims=True)
        r.dgates[...] += jnp.where(iota(r.dgates.shape, 1) == e, d_gate, 0.0)
        d_act = d_act * gate
        d_up = (d_act * silu).astype(BF16)
        d_gp = (d_act * up_part * squash * (1.0 + gate_part * (1.0 - squash))).astype(BF16)
        d_mid_in = (
            jnp.concatenate([dot(d_gp, r.w_in_up[slot, 0], NT), dot(d_up, r.w_in_up[slot, 1], NT)], axis=1)
            * r.mask[:, :lanes]
        ).astype(BF16)
        scaled_mid = (mid_out * gate).astype(BF16)
        r.d_mid_in[e] = d_mid_in
        r.mid_out[e] = scaled_mid
        r.acc_out[...] += dot((act.astype(F32) * gate).astype(BF16), r.w_out[slot])

        @pl.when(turn < experts - slots)
        def _():
            r.acc_h2[...] += dot(d_gp, r.w_in[slot, :, :FF], NT) + dot(d_up, r.w_in[slot, :, FF:], NT)

        @pl.when(turn >= experts - slots)
        def _():
            r.d_joint[slot, :, :FF] = d_gp
            r.d_joint[slot, :, FF:] = d_up

        r.pack[half, q, :64, :] = dot(d_mid_in, h2, TN).astype(BF16)
        r.pack[half, q, 64:96, :FF] = dot(mid_in[:, :SPAN], d_gp, TN).astype(BF16)
        r.pack[half, q, 64:96, FF:] = dot(mid_in[:, SPAN:], d_up, TN).astype(BF16)
        r.pack[half, q, 96:112, :] = fold(
            dot((lifted.astype(F32) * gate).astype(BF16), act, TN)
        ).astype(BF16)
        r.pack[half, q, 112:, :] = dot(scaled_mid, g, TN).astype(BF16)

        @pl.when(turn + slots < experts)
        def _():
            for copy in expert_loads(turn + slots):
                copy.start()

        @pl.when(turn % 4 == 0)
        def _():
            to_core(half, 1 - x).start()

        @pl.when(turn % 4 == 1)
        def _():
            to_core(half, x).start()

        @pl.when(turn % 4 == 2)
        def _():
            add_core(half, 1 - x)
            to_column(half).start()

        @pl.when(turn % 4 == 3)
        def _():
            add_core(half, x)

        @pl.when(turn == 5)
        def _():
            stage_pieces(0)

        return carry

    lax.fori_loop(0, experts, one, 0)
    every = range(experts)
    r.dg_trade[ep] = r.dgates[...].T[:8]
    send_dg = swap(9, r.dg_trade.at[ep], r.dg_trade.at[ep])
    send_dg.start()
    all_d_mids = jnp.concatenate([r.d_mid_in[e] for e in every], axis=1)
    tile = 256
    send_h2 = []
    for number in range(r.acc_h2.shape[1] // tile):
        columns = slice(tile * number, tile * number + tile)
        ends = r.acc_h2[:, columns] + dot(all_d_mids, r.in_down[:, :, columns].reshape(experts * lanes, tile))
        for slot in range(slots):
            ends = ends + dot(r.d_joint[slot], r.w_in[slot, columns, :], NT)
        r.trade[ep, :, columns] = ends.astype(BF16)
        part = r.trade.at[ep, :, columns]
        copy = swap((10, 3, 15, 16)[number], part, part)
        copy.start()
        send_h2.append(copy)
    r.acc_out[...] += dot(jnp.concatenate([r.mid_out[e] for e in every], axis=1), r.out_up[...].reshape(experts * SPAN, -1))
    r.out_trade[0] = r.acc_out[theirs, :].astype(BF16)
    send_out = swap(11, r.out_trade.at[0], r.out_trade.at[1])
    send_out.start()
    stage_own(0)
    stage_pieces(1)

    def small_sum(number, source, landing, result, shared):
        tiles = source.shape[0] // 16
        width = landing.shape[2]
        each = source.shape[1] // width
        holders = tiles * each
        shared = shared * each
        private = me >= shared
        mine_too = (me < holders) & (private | (me % 2 == ep))
        send_one, send_two = r.small_send.at[number, 0], r.small_send.at[number, 1]
        recv_one, recv_two = r.small_recv.at[number, 0], r.small_recv.at[number, 1]
        own_index = me + blocks * ep

        def region(ref, owner):
            return ref.at[span(owner // each * 16, 16), span(owner % each * width, width)]

        def several(count):
            return landing.at[pl.ds(0, count)]

        def scatter():
            def step(index, carry):
                owner = lax.rem(me + index, blocks)
                side = jnp.where(owner < shared, owner % 2, ep)

                @pl.when((owner < holders) & ((index > 0) | (side != ep)))
                def _():
                    remote(
                        region(source, owner), landing.at[own_index], send_one, recv_one, {"ctx": owner, "ep": side}
                    ).start()

                return carry

            lax.fori_loop(0, blocks, step, 0)

        def add(first, count):
            def step(p, sums):
                return sums + landing[p].astype(F32)

            return lax.fori_loop(first, first + count, step, jnp.zeros(landing.shape[1:], F32))

        def tell(side):
            part = region(result, me % holders)

            def step(index, carry):
                device = lax.rem(me + index, blocks)

                @pl.when((index > 0) | (side != ep))
                def _():
                    remote(part, part, send_two, recv_two, {"ctx": device, "ep": side}).start()

                return carry

            lax.fori_loop(0, blocks, step, 0)

        def total():
            @pl.when(mine_too)
            def _():
                landing[own_index] = region(source, me % holders)[...]

            @pl.when(mine_too & private)
            def _():
                wait_received(several(blocks - 1), recv_one)
                region(result, me % holders)[...] = add(blocks * ep, blocks).astype(BF16)
                tell(ep)

            if shared:

                @pl.when(mine_too & jnp.logical_not(private))
                def _():
                    wait_received(several(2 * blocks - 1), recv_one)
                    region(result, me % holders)[...] = add(0, 2 * blocks).astype(BF16)
                    tell(ep)
                    tell(1 - ep)

        def finish():
            @pl.when(mine_too)
            def _():
                wait_received(several(holders - 1), recv_two)
                wait_sent(several(holders - 1), send_one)

            @pl.when(jnp.logical_not(mine_too))
            def _():
                wait_received(several(holders), recv_two)
                wait_sent(several(holders), send_one)

            @pl.when(mine_too & private)
            def _():
                wait_sent(several(blocks - 1), send_two)

            if shared:

                @pl.when(mine_too & jnp.logical_not(private))
                def _():
                    wait_sent(several(2 * blocks - 1), send_two)

        return scatter, total, finish

    early_scatter, early_total, early_finish = small_sum(0, r.early, r.early_land, r.early_out, 0)
    late_scatter, late_total, late_finish = small_sum(1, r.late, r.late_land, r.late_out, 6)
    drain_forward()

    send_dg.wait_recv()
    blank = jnp.zeros((112, block), F32)
    table = jnp.concatenate([r.dg_trade[0], r.dg_trade[1], blank], axis=0).T
    d_gates = table[:, : 2 * experts]
    gates = r.gates[...]
    d_logits = (gates * (d_gates - jnp.sum(gates * d_gates, axis=1, keepdims=True))).astype(BF16)
    from_router = dot(d_logits, r.router[...])
    stage_column(0)
    for copy in send_h2:
        copy.wait_recv()
    d_h2 = r.trade[0].astype(F32) + r.trade[1].astype(F32) + from_router
    d_x2 = r.g_all[...].astype(F32) + rms_back(r.x2[...], r.moe_gain[...], d_h2)
    d_attn = d_x2.astype(BF16)
    r.acc_h2[...] = d_x2
    d_mid_o = (dot(d_attn, r.o_up[...], NT) * r.mask[:, :SPAN]).astype(BF16)

    d_att = (dot(d_attn, r.ow_all[ep], NT) + dot(d_mid_o, r.od_all[ep])).astype(BF16)
    for number in range(4):
        r.d_out[number] = d_att[:, 128 * number : 128 * number + 128]
    for step in (1, 2, 3):
        piece_to(*grad_pieces, step).start()
    r.dqt[...] = jnp.zeros(r.dqt.shape, F32)
    r.early[:32, :] = dot(r.mid_o[...], d_attn, TN).astype(BF16)
    r.early[32:48, :] = fold(dot(d_mid_o, r.att_all[ep], TN)).astype(BF16)
    r.early[48:, :] = jnp.zeros((16, r.early.shape[1]), BF16)
    early_scatter()
    stage_own(1)

    r.d_in[head] = r.d_out[head]
    wait_received(three_pieces, r.piece_recv.at[1])
    for b in range(4):
        received = r.d_in[b].astype(F32)
        turned = stack_columns(received)
        r.dt[b, HEAD:, :] = turned.astype(BF16)
        r.delta[b] = jnp.sum(turned * r.acc[b], axis=0, keepdims=True)
        r.dn[b] = stack_rows(received, True)

    def back_step(p, kb, kinds):
        kv = r.kvall[p, kb]
        grown = None
        for b, masked in kinds:
            pos_row, start_row = pos_rows[b], start_rows[b]
            s = dot(kv, r.qt[b])
            base = r.lse[b]
            if masked:
                key = (4 * p + kb) * block + iota(s.shape, 0)
                w = jnp.where((key <= pos_row) & (key >= start_row), jnp.exp(s - base), 0.0)
            else:
                w = jnp.exp(s - jnp.where(start_row <= (4 * p + 1) * block, base, -LOW))
            d_w = dot(kv, r.dt[b])
            d_s = (w * (d_w - r.delta[b])).astype(BF16)
            added = dot(d_s, r.qn[b]) + dot(w.astype(BF16), r.dn[b])
            grown = added if grown is None else grown + added
            r.dqt[b] += dot(kv, d_s, TN)[:HEAD]
        r.kvall[p, kb] = grown.astype(BF16)

    def lower(p, kb):
        return remote(
            r.kvall.at[p, kb], r.from_up.at[p % kept, kb], r.down_send.at[p, kb], r.down_recv.at[p, kb], down
        )

    def back_to(source, landing, send, recv, b):
        return remote(source.at[b], landing.at[head], send, recv, device_of(b))

    def give_back(source, landing, send, recv, b):
        @pl.when(b == head)
        def _():
            landing[b] = source[b]

        @pl.when(b != head)
        def _():
            back_to(source, landing, send, recv, b).start()

    dq_pieces = (r.dq_out, r.dq_in, r.piece_send.at[2], r.piece_recv.at[2])
    dkv_pieces = (r.kvall.at[z], r.dkv_in, r.piece_send.at[3], r.piece_recv.at[3])

    def pass_on(step):
        p, kb = step // 4, step % 4

        @pl.when(z < planes - 1)
        def _():
            lower(p, kb).wait_recv()
            r.kvall[p, kb] = (r.kvall[p, kb].astype(F32) + r.from_up[p % kept, kb].astype(F32)).astype(BF16)
            if planes > kept:

                @pl.when((kb == 3) & (p + kept <= z))
                def _():
                    pl.semaphore_signal(r.credit, inc=1, device_id=up, device_id_type=MESH)

        @pl.when(p < z)
        def _():
            if planes > kept:

                @pl.when((kb == 0) & (p >= kept))
                def _():
                    pl.semaphore_wait(r.credit, 1)

            lower(p, kb).start()

        @pl.when(p == z)
        def _():
            give_back(*dkv_pieces, kb)

    def after(step):
        @pl.when(z == planes - 1)
        def _():
            pass_on(step)

        @pl.when((z < planes - 1) & (step >= 2))
        def _():
            pass_on(step - 2)

    def plane_back(p, carry):
        @pl.when(p < z)
        def _():
            @pl.when(p == 0)
            def _():
                back_step(p, 0, [(b, True) for b in range(4)])
                after(0)

            def middle(kb, inner):
                back_step(p, kb, [(b, False) for b in range(4)])
                after(4 * p + kb)
                return inner

            lax.fori_loop(jnp.where(p == 0, 1, 0), 4, middle, 0)

        @pl.when(p == z)
        def _():
            for kb in range(4):
                back_step(p, kb, [(b, b == kb or kb == 0) for b in range(kb, 4)])
                r.dq_out[kb] = (unstack(r.dqt[kb]) * SCALE).astype(BF16)
                give_back(*dq_pieces, kb)
                after(4 * p + kb)

        @pl.when(p == 0)
        def _():
            stage_core(0)

        @pl.when(p == 1)
        def _():
            stage_column(1)

        @pl.when(p == 2)
        def _():
            early_total()

        return carry

    lax.fori_loop(0, planes, plane_back, 0)

    @pl.when(z < planes - 1)
    def _():
        pass_on(4 * z + 2)
        pass_on(4 * z + 3)

    cosine, sine = r.cosine[...], r.sine[...]
    wait_received(three_pieces, r.piece_recv.at[2])
    wait_received(three_pieces, r.piece_recv.at[3])
    d_query = jnp.concatenate([r.dq_in[number] for number in range(4)], axis=1)
    d_q = rotate(d_query.astype(F32), cosine, sine, -1.0).astype(BF16)
    d_key = jnp.concatenate([r.dkv_in[number, :, :HEAD] for number in range(4)], axis=1)
    d_k = rotate(d_key.astype(F32), cosine, sine, -1.0).astype(BF16)
    d_value = jnp.concatenate([r.dkv_in[number, :, HEAD:] for number in range(4)], axis=1)
    d_mids = jnp.concatenate(
        [dot(d_q, r.q_up[...], NT), dot(d_k, r.kv_up[0], NT), dot(d_value, r.kv_up[1], NT)], axis=1
    )
    d_mids = (d_mids * r.mask[:, : 3 * SPAN]).astype(BF16)
    r.late[:96, :] = dot(d_mids, r.h1[...], TN).astype(BF16)
    r.late[96:112, :] = fold(dot(r.mids[:, :SPAN], d_q, TN)).astype(BF16)
    r.late[112:, :] = fold(
        jnp.concatenate(
            [dot(r.mids[:, SPAN : 2 * SPAN], d_k, TN), dot(r.mids[:, 2 * SPAN :], d_value, TN)], axis=1
        )
    ).astype(BF16)
    late_scatter()
    full = (
        dot(d_q, r.q_w[...], NT) + dot(d_k, r.kv_w[0], NT) + dot(d_value, r.kv_w[1], NT) + dot(d_mids, r.qkv_down[...])
    )
    first, second = full[:rows], full[rows:]
    r.norm_trade[0] = jnp.where(ep == 0, second, first).astype(BF16)
    send_norm = swap(13, r.norm_trade.at[0], r.norm_trade.at[1])
    send_norm.start()
    stage_core(1)
    stage_end(0)
    early_finish()
    send_out.wait_recv()
    r.block_out[...] = (r.x2[mine, :] + (r.acc_out[mine, :] + r.out_trade[1].astype(F32))).astype(BF16)
    own = jnp.where(ep == 0, first, second)
    late_total()
    stage_end(1)

    def store(number, start, count):
        return pltpu.make_async_copy(
            r.packed.at[pl.ds(start, count)], r.out.at[pl.ds(start, count)], r.load_sem.at[number]
        )

    stores = [store(0, 0, base), store(1, base + 128, 128), store(2, base + 384, 64)]
    for copy in stores:
        copy.start()
    send_norm.wait_recv()
    own = own + r.norm_trade[1].astype(F32)
    r.in_grad[...] = (
        r.acc_h2[mine, :] + rms_back(r.x_all[mine, :].astype(F32), r.attn_gain[...], own)
    ).astype(BF16)
    stores.append(store(3, base + 256, 128))
    stores[-1].start()
    stage_drain(0)
    stage_drain(1)

    for copy in (*send_x, send_ow, send_od, send_hot, send_g, send_dg, *send_h2, send_out, send_norm):
        copy.wait_send()
    wait_sent(r.o_out.at[pl.ds(0, 3)], r.att_send.at[0])
    wait_sent(r.o_out, r.att_send.at[1])
    for number in (1, 2, 3):
        wait_sent(three_pieces, r.piece_send.at[number])
    hand_on(head, 0, across).wait_send()
    hand_on(head, 1, beside).wait_send()
    hand_on(sibling, 1, beside).wait_send()

    def drain(p, carry):
        for kb in range(4):
            lower(p, kb).wait_send()
        return carry

    lax.fori_loop(0, z, drain, 0)
    late_finish()
    stores.append(store(4, base, 128))
    stores[-1].start()
    for copy in stores:
        copy.wait()


RESULTS = (
    "ein_down", "ein_up", "eout_down", "eout_up", "block_out", "in_grad", "g_down", "g_q", "g_kv", "g_od", "g_ou",
)


def unpack_kernel(packed, *refs):
    count = len(RESULTS)
    outs = dict(zip(RESULTS, refs[:count]))
    held = dict(zip(RESULTS, refs[count : 2 * count]))
    rows, sem_in, sem_out = refs[2 * count :]
    experts = outs["ein_down"].shape[0]
    grad_rows = 144
    base = experts * grad_rows

    def fetch(start, size, number):
        return pltpu.make_async_copy(
            packed.at[pl.ds(start, size)], rows.at[pl.ds(start, size)], sem_in.at[number]
        )

    fetches = [fetch(grad_rows * e, grad_rows, e) for e in range(experts)]
    fetches.append(fetch(base, rows.shape[0] - base, experts))
    for copy in fetches:
        copy.start()
    stores = []

    def store(name, number):
        copy = pltpu.make_async_copy(
            held[name] if number is None else held[name].at[number],
            outs[name] if number is None else outs[name].at[number],
            sem_out.at[len(stores)],
        )
        copy.start()
        stores.append(copy)

    for e in range(experts):
        fetches[e].wait()
        part = rows[grad_rows * e : grad_rows * e + grad_rows, :].astype(F32)
        held["ein_down"][e] = part[:64]
        held["ein_up"][e, 0] = part[64:96, :FF]
        held["ein_up"][e, 1] = part[64:96, FF:]
        held["eout_down"][e, :16] = part[96:112, :FF]
        held["eout_down"][e, 16:] = part[96:112, FF:]
        held["eout_up"][e] = part[112:]
        for name in RESULTS[:4]:
            store(name, e)
    fetches[experts].wait()
    late = rows[base : base + 128, :].astype(F32)
    early = rows[base + 384 : base + 448, :].astype(F32)
    held["block_out"][...] = rows[base + 128 : base + 256, :]
    held["in_grad"][...] = rows[base + 256 : base + 384, :]
    held["g_down"][...] = late[:96]
    held["g_q"][:16, :] = late[96:112, :FF]
    held["g_q"][16:, :] = late[96:112, FF:]
    kv = FF // 2
    for side in (0, 1):
        for half in (0, 1):
            first = kv * (2 * half + side)
            held["g_kv"][side, 16 * half : 16 * half + 16, :] = late[112:, first : first + kv]
    held["g_od"][:16, :] = early[32:48, :FF]
    held["g_od"][16:, :] = early[32:48, FF:]
    held["g_ou"][...] = early[:32]
    for name in RESULTS[4:]:
        store(name, None)
    for copy in stores:
        copy.wait()


def per_device(
    resid_in, out_grad, attn_gain, q_weight, key_value_weight, o_weight, moe_gain, router, expert_in,
    expert_out, qkv_down, q_up, key_value_up_factor, o_down, o_up, expert_in_down, expert_in_up,
    expert_out_down, expert_out_up, expert_ids, doc_starts, doc_adapter,
):
    blocks = lax.axis_size("ctx")
    planes = blocks // 4
    rows, width = resid_in.shape
    block = 2 * rows
    heads = q_weight.shape[1]
    kv = key_value_weight.shape[2]
    experts = expert_in.shape[0]
    slots = 6 if planes <= 4 else 4
    kept = planes if planes <= 4 else 2
    grad_rows = 2 * SPAN + SPAN + SPAN // 2 + SPAN
    base = experts * grad_rows
    groups = 3 if planes >= 12 else 1
    piece = (grad_rows // groups, width // 4)
    early_width = max(128, 4 * width // blocks)
    late_width = max(128, 8 * width // blocks)
    freq = np.tile(np.power(10000.0, -2.0 * np.arange(HEAD // 2) / HEAD).astype(np.float32), 4)[None, :]

    def shape(dims, kind=BF16):
        return jax.ShapeDtypeStruct(dims, kind)

    def dma(*dims):
        return pltpu.SemaphoreType.DMA(dims)

    def low(*dims):
        return pltpu.VMEM(dims, BF16)

    def full(*dims):
        return pltpu.VMEM(dims, F32)

    operands = dict(
        resid=resid_in, grad=out_grad, ids=expert_ids.T, starts=doc_starts, adapters=doc_adapter,
        attn_gain=attn_gain[None, :], moe_gain=moe_gain[None, :], freq=jnp.asarray(freq), qkv_down=qkv_down.T,
        q_up=q_up, kv_up=key_value_up_factor, o_down=o_down.T, o_up=o_up, router=router.T, q_hbm=q_weight,
        kv_hbm=key_value_weight, o_hbm=o_weight, in_hbm=expert_in, out_hbm=expert_out,
        in_down_hbm=jnp.swapaxes(expert_in_down, 1, 2), in_up_hbm=expert_in_up,
        out_down_hbm=jnp.swapaxes(expert_out_down, 1, 2), out_up_hbm=expert_out_up,
    )
    results = dict(out=shape((base + 448, width)))
    scratch = dict(
        q_w=low(*q_weight.shape), kv_w=low(*key_value_weight.shape), ow_all=low(2, heads, width),
        od_all=low(2, SPAN, heads), w_in=low(slots, *expert_in.shape[1:]), w_out=low(slots, *expert_out.shape[1:]),
        in_down=low(experts, 2 * SPAN, width), w_in_up=low(slots, *expert_in_up.shape[1:]),
        w_out_down=low(slots, SPAN, FF), out_up=low(experts, SPAN, width),
        mid_in=low(experts, block, 2 * SPAN), lifted=low(experts, block, SPAN),
        d_mid_in=low(experts, block, 2 * SPAN), d_joint=low(slots, block, 2 * FF), mid_out=low(experts, block, SPAN),
        x_all=low(block, width), g_all=low(block, width), h1=low(block, width), h2=low(block, width),
        hot_all=low(block, 128), mask=full(block, 128), cosine=full(block, 128), sine=full(block, 128),
        mids=low(block, 3 * SPAN), kvall=low(planes, 4, block, 128), kv_out=low(4, block, 128), q_out=low(4, block, 128),
        q_in=low(4, block, 128), d_out=low(4, block, 128), d_in=low(4, block, 128), o_out=low(4, block, 128),
        dq_out=low(4, block, 128), dq_in=low(4, block, 128), dkv_in=low(4, block, 128), qt=low(4, 128, 2 * block),
        qn=low(4, 2 * block, 128), dt=low(4, 128, 2 * block), dn=low(4, 2 * block, 128),
        m_s=full(4, 1, 2 * block), l_s=full(4, 1, 2 * block), lse=full(4, 1, 2 * block),
        delta=full(4, 1, 2 * block), acc=full(4, HEAD, 2 * block), dqt=full(4, HEAD, 2 * block),
        att_all=low(2, block, heads), halves=full(2, block, width), half_mid=full(2, block, SPAN), mid_o=low(block, SPAN), x2=full(block, width),
        gates=full(block, 2 * experts), dgates=full(block, 128), trade=low(2, block, width), out_trade=low(2, rows, width),
        norm_trade=low(2, rows, width), dg_trade=full(2, 8, block),
        pack=low(2, 4, grad_rows, width), core_land=low(2, 2, grad_rows, width), x_land=low(2, grad_rows, width),
        z_land=low(2, planes, *piece), early=low(64, width), late=low(128, width),
        early_land=low(2 * blocks, 16, early_width), late_land=low(2 * blocks, 16, late_width),
        from_up=low(kept, 4, block, 128), credit=pltpu.SemaphoreType.REGULAR,
        packed=low(base + 448, width), load_sem=dma(5), expert_sem=dma(slots, 4), pair_send=dma(17), pair_recv=dma(17),
        kv_send=dma(3), kv_recv=dma(3), piece_send=dma(4), piece_recv=dma(4), up_send=dma(planes, 3),
        up_recv=dma(planes, 3), ow_send=dma(4, 2), ow_recv=dma(4), att_send=dma(2), att_recv=dma(2), core_send=dma(2, 2), core_recv=dma(2, 2),
        x_send=dma(2), x_recv=dma(2), z_send=dma(2, 2), z_recv=dma(2, 2), last_send=dma(2, 2, 4),
        last_recv=dma(2, 4),
        small_send=dma(2, 2), small_recv=dma(2, 2), down_send=dma(planes, 4),
        down_recv=dma(planes, 4),
    )
    (out,) = pl.pallas_call(
        functools.partial(layer_kernel, planes, slots, INPUTS + OUTPUTS + tuple(scratch)),
        out_shape=[results[name] for name in OUTPUTS],
        in_specs=[
            SMEM if name in ("starts", "adapters") else HBM if name.endswith("hbm") else VMEM for name in INPUTS
        ],
        out_specs=[HBM] * len(OUTPUTS),
        scratch_shapes=list(scratch.values()),
        compiler_params=pltpu.CompilerParams(
            collective_id=1, has_side_effects=True, vmem_limit_bytes=62 << 20
        ),
        name="layer",
    )(*[operands[name] for name in INPUTS])

    unpacked = dict(
        ein_down=shape((experts, 2 * SPAN, width), F32), ein_up=shape((experts, 2, SPAN, FF), F32),
        eout_down=shape((experts, SPAN, FF), F32), eout_up=shape((experts, SPAN, width), F32),
        block_out=shape((rows, width)), in_grad=shape((rows, width)), g_down=shape((3 * SPAN, width), F32),
        g_q=shape((SPAN, heads), F32), g_kv=shape((2, SPAN, kv), F32), g_od=shape((SPAN, heads), F32),
        g_ou=shape((SPAN, width), F32),
    )
    ein_down, ein_up, eout_down, eout_up, block_out, in_grad, g_down, g_q, g_kv, g_od, g_ou = pl.pallas_call(
        unpack_kernel,
        out_shape=[unpacked[name] for name in RESULTS],
        in_specs=[HBM],
        out_specs=[HBM] * len(RESULTS),
        scratch_shapes=[
            *[pltpu.VMEM(unpacked[name].shape, unpacked[name].dtype) for name in RESULTS],
            pltpu.VMEM(out.shape, BF16), dma(experts + 1), dma(4 * experts + 7),
        ],
        compiler_params=pltpu.CompilerParams(vmem_limit_bytes=62 << 20),
        name="unpack",
    )(out)
    return (
        block_out, in_grad, g_down.T, g_q, g_kv, g_od.T, g_ou, jnp.swapaxes(ein_down, 1, 2), ein_up,
        jnp.swapaxes(eout_down, 1, 2), eout_up,
    )


def solution(mesh):
    placed = (
        P(("ctx", "ep"), None),
        P(("ctx", "ep"), None),
        P(),
        P(None, "ep"),
        P(None, None, "ep"),
        P("ep", None),
        P(),
        P(),
        P("ep", None, None),
        P("ep", None, None),
        P(),
        P(None, "ep"),
        P(None, None, "ep"),
        P("ep", None),
        P(),
        P("ep", None, None),
        P("ep", None, None, None),
        P("ep", None, None),
        P("ep", None, None),
        P(("ctx", "ep"), None),
        P(),
        P(),
    )
    return jax.shard_map(
        per_device,
        mesh=mesh,
        in_specs=placed,
        out_specs=(
            P(("ctx", "ep"), None),
            P(("ctx", "ep"), None),
            P(),
            P(None, "ep"),
            P(None, None, "ep"),
            P("ep", None),
            P(),
            P("ep", None, None),
            P("ep", None, None, None),
            P("ep", None, None),
            P("ep", None, None),
        ),
        check_vma=False,
    )
```

```python
import functools

import jax
import jax.numpy as jnp
import numpy as np
from jax import lax
from jax.experimental import pallas as pl
from jax.experimental.pallas import tpu as pltpu
from jax.sharding import PartitionSpec as P

MESH = pl.DeviceIdType.MESH
VMEM = pl.BlockSpec(memory_space=pltpu.VMEM)
SMEM = pl.BlockSpec(memory_space=pltpu.SMEM)
HBM = pl.BlockSpec(memory_space=pl.ANY)
F32 = jnp.float32
BF16 = jnp.bfloat16

HEAD = 64
FF = 512
RANK = 16
SPAN = 32
EPS = 1e-06
LOW = -1e30
SCALE = 0.125

NN = (((1,), (0,)), ((), ()))
NT = (((1,), (1,)), ((), ()))
TN = (((0,), (0,)), ((), ()))


def dot(left, right, dims=NN):
    return lax.dot_general(left, right, dims, preferred_element_type=F32)


def iota(shape, dim):
    return lax.broadcasted_iota(jnp.int32, shape, dim)


def rms(values, gain):
    return values * lax.rsqrt(jnp.mean(values * values, axis=-1, keepdims=True) + EPS) * gain


def rms_back(values, gain, upstream):
    factor = lax.rsqrt(jnp.mean(values * values, axis=-1, keepdims=True) + EPS)
    scaled = upstream * gain
    return factor * scaled - values * factor * factor * factor * jnp.mean(
        scaled * values, axis=-1, keepdims=True
    )


def rotate(values, cosine, sine, sign):
    width = values.shape[1]
    copies = width // 128
    cosine = jnp.concatenate([cosine] * copies, axis=1)
    sine = jnp.concatenate([sine] * copies, axis=1)
    first = iota(values.shape, 1) % HEAD < HEAD // 2
    ahead = pltpu.roll(values, width - HEAD // 2, 1)
    behind = pltpu.roll(values, HEAD // 2, 1)
    return values * cosine + sign * jnp.where(first, -ahead, behind) * sine


def doc_scan(positions, starts_ref, adapters_ref):
    own_start = jnp.zeros(positions.shape, jnp.int32)
    adapter = jnp.zeros(positions.shape, jnp.int32)
    for number in range(starts_ref.shape[0]):
        opened = starts_ref[number] <= positions
        own_start = jnp.where(opened, starts_ref[number], own_start)
        adapter = jnp.where(opened, adapters_ref[number], adapter)
    return own_start, adapter


def place():
    me = lax.axis_index("ctx")
    ep = lax.axis_index("ep")
    return me, ep, me // 4, (me // 2) % 2, me % 2


def block_of(z, x, c):
    return (z * 2 + x) * 2 + c


def signal(device):
    pl.semaphore_signal(
        pltpu.get_barrier_semaphore(), inc=1, device_id=device, device_id_type=MESH
    )


def remote(src, dst, send, recv, device):
    return pltpu.make_async_remote_copy(
        src_ref=src,
        dst_ref=dst,
        send_sem=send,
        recv_sem=recv,
        device_id=device,
        device_id_type=MESH,
    )


def span(start, count):
    return pl.ds(pl.multiple_of(start, count), count)


def stack_rows(piece, upper):
    turned = pltpu.roll(piece, HEAD, 1)
    keep = iota(piece.shape, 1) >= HEAD if upper else iota(piece.shape, 1) < HEAD
    first, second = (turned, piece) if upper else (piece, turned)
    blank = jnp.zeros(piece.shape, piece.dtype)
    return jnp.concatenate([jnp.where(keep, first, blank), jnp.where(keep, second, blank)], axis=0).astype(BF16)


def stack_columns(piece):
    turned = piece.T
    return jnp.concatenate([turned[:HEAD], turned[HEAD:]], axis=1)


def unstack(columns):
    count = columns.shape[1] // 2
    return jnp.concatenate([columns[:, :count], columns[:, count:]], axis=0).T


def fold(wide):
    count = wide.shape[0] // 2
    return jnp.concatenate([wide[:count], wide[count:]], axis=1)


INPUTS = (
    "resid", "grad", "ids", "starts", "adapters", "attn_gain", "moe_gain", "freq",
    "qkv_down", "q_up", "kv_up", "o_down", "o_up", "router",
    "q_hbm", "kv_hbm", "o_hbm", "in_hbm", "out_hbm", "in_down_hbm", "in_up_hbm", "out_down_hbm", "out_up_hbm",
)
OUTPUTS = ("out",)


def layer_kernel(planes, slots, names, *refs):
    r = dict(zip(names, refs))
    r = type("Refs", (), r)
    r.acc_out, r.acc_h2 = r.halves.at[0], r.halves.at[1]
    grad_rows = r.pack.shape[2]
    base = r.in_hbm.shape[0] * grad_rows
    r.late_out = r.packed.at[pl.ds(base, 128)]
    r.block_out = r.packed.at[pl.ds(base + 128, 128)]
    r.in_grad = r.packed.at[pl.ds(base + 256, 128)]
    r.early_out = r.packed.at[pl.ds(base + 384, 64)]
    me, ep, z, x, c = place()
    blocks = 4 * planes
    pair = {"ctx": me, "ep": 1 - ep}
    head = 2 * x + c
    up = {"ctx": jnp.minimum(me + 4, blocks - 1), "ep": ep}
    down = {"ctx": jnp.maximum(me - 4, 0), "ep": ep}
    across = {"ctx": block_of(z, 1 - x, c), "ep": ep}
    beside = {"ctx": block_of(z, x, 1 - c), "ep": ep}
    rows = r.resid.shape[0]
    block = 2 * rows
    mine = span(ep * rows, rows)
    theirs = span(rows - ep * rows, rows)
    experts = r.in_hbm.shape[0]
    groups = 3 if planes >= 12 else 1
    owners = 4 * groups
    piece = (grad_rows // groups, r.pack.shape[3] // 4)
    kept = r.from_up.shape[0]
    deferred = r.d_joint.shape[0]
    heads = r.q_hbm.shape[1]

    load_q = pltpu.make_async_copy(r.q_hbm, r.q_w, r.load_sem.at[0])
    load_kv = pltpu.make_async_copy(r.kv_hbm, r.kv_w, r.load_sem.at[1])
    load_o = pltpu.make_async_copy(r.o_hbm, r.ow_all.at[ep], r.load_sem.at[2])
    load_kv.start()
    load_q.start()
    load_o.start()
    load_in_down = pltpu.make_async_copy(r.in_down_hbm, r.in_down, r.load_sem.at[3])
    load_out_up = pltpu.make_async_copy(r.out_up_hbm, r.out_up, r.load_sem.at[4])
    load_in_down.start()
    load_out_up.start()
    weights = (
        (r.in_hbm, r.w_in), (r.out_hbm, r.w_out), (r.in_up_hbm, r.w_in_up), (r.out_down_hbm, r.w_out_down),
    )

    def quarter_at(turn):
        return jnp.where(turn % 2 == 0, 1 - x, x) * 2 + jnp.where(turn < 2, 1 - c, c)

    def expert_at(turn):
        return 2 * quarter_at(turn % 4) + turn // 4

    def expert_loads(turn):
        e, slot = expert_at(turn), turn % slots
        return [
            pltpu.make_async_copy(source.at[e], held.at[slot], r.expert_sem.at[slot, number])
            for number, (source, held) in enumerate(weights)
        ]

    def begin(turn, carry):
        for copy in expert_loads(turn):
            copy.start()
        return carry

    lax.fori_loop(0, slots, begin, 0)

    def greet(step, carry):
        signal({"ctx": lax.rem(me + step, blocks), "ep": ep})
        signal({"ctx": lax.rem(me + step, blocks), "ep": 1 - ep})
        return carry

    signal(pair)
    lax.fori_loop(1, blocks, greet, 0)
    pl.semaphore_wait(pltpu.get_barrier_semaphore(), 2 * blocks - 1)

    def wait_sent(like, sem):
        remote(like, like, sem, sem, pair).wait_send()

    def wait_received(like, sem):
        remote(like, like, sem, sem, pair).wait_recv()

    def swap(number, src, dst):
        return remote(src, dst, r.pair_send.at[number], r.pair_recv.at[number], pair)

    small = rows // 2
    chunks = (
        (mine, rows),
        (span(rows - ep * rows, small), small),
        (span(rows - ep * rows + small, small), small),
    )
    send_x = []
    for number in (0, 1):
        part = pl.ds(small * number, small)
        copy = swap(number, r.resid.at[part], r.x_all.at[span(ep * rows + small * number, small)])
        copy.start()
        send_x.append(copy)

    hot = jnp.zeros((r.ids.shape[0], rows), F32)
    hot = jnp.zeros((128, rows), F32)
    numbers = iota((128, rows), 0)
    for choice in range(r.ids.shape[0]):
        hot = hot + jnp.where(r.ids[choice : choice + 1, :] == numbers, 1.0, 0.0)
    r.hot_all[mine, :] = hot.T.astype(BF16)
    r.x_all[mine, :] = r.resid[...]
    r.g_all[mine, :] = r.grad[...]
    r.od_all[ep] = r.o_down[...]
    position = me * block + iota((block, 128), 0)
    own_start, adapter = doc_scan(position, r.starts, r.adapters)
    r.mask[...] = jnp.where((iota((block, 128), 1) % SPAN) // RANK == adapter, 1.0, 0.0)
    angles = (position - own_start).astype(F32) * r.freq[...]
    r.cosine[...] = jnp.cos(angles)
    r.sine[...] = jnp.sin(angles)
    pos_rows = [((4 * z + b) * block + iota((8, 2 * block), 1) % block)[:1] for b in range(4)]
    start_rows = [
        doc_scan((4 * z + b) * block + iota((8, 2 * block), 1) % block, r.starts, r.adapters)[0][:1] for b in range(4)
    ]

    def other_head(step):
        return lax.rem(head + step, 4)

    def device_of(number):
        return {"ctx": 4 * z + number, "ep": ep}

    def kv_to(step, chunk):
        number = other_head(step)
        here = chunks[chunk][0]
        return remote(
            r.kv_out.at[number, here, :], r.kvall.at[z, head, here, :],
            r.kv_send.at[chunk], r.kv_recv.at[chunk], device_of(number),
        )

    def three(chunk):
        return r.kv_out.at[pl.ds(0, 3), chunks[chunk][0], :]

    def piece_to(source, landing, send, recv, step):
        number = other_head(step)
        return remote(source.at[number], landing.at[head], send, recv, device_of(number))

    three_pieces = r.q_out.at[pl.ds(0, 3)]

    query_pieces = (r.q_out, r.q_in, r.piece_send.at[0], r.piece_recv.at[0])

    def climb(p, half):
        part = r.kvall.at[p, :, chunks[half][0], :]
        return remote(part, part, r.up_send.at[p, half], r.up_recv.at[p, half], up)

    def climb_on(p, half):
        @pl.when(z < planes - 1)
        def _():
            climb(p, half).start()

    def collect(half):
        wait_received(three(half), r.kv_recv.at[half])
        climb_on(z, half)

    def project(here):
        h1 = rms(r.x_all[here, :].astype(F32), r.attn_gain[...]).astype(BF16)
        r.h1[here, :] = h1
        mids = (dot(h1, r.qkv_down[...], NT) * r.mask[here, : 3 * SPAN]).astype(BF16)
        r.mids[here, :] = mids
        k_lin = dot(h1, r.kv_w[0]) + dot(mids[:, SPAN : 2 * SPAN], r.kv_up[0])
        keys = rotate(k_lin, r.cosine[here, :], r.sine[here, :], 1.0)
        values = dot(h1, r.kv_w[1]) + dot(mids[:, 2 * SPAN :], r.kv_up[1])
        for number in range(4):
            lanes = slice(HEAD * number, HEAD * number + HEAD)
            r.kv_out[number, here, :] = jnp.concatenate([keys[:, lanes], values[:, lanes]], axis=1).astype(BF16)
        r.kvall[z, head, here, :] = r.kv_out[head, here, :]

    load_kv.wait()
    project(mine)
    for step in (1, 2, 3):
        kv_to(step, 0).start()
    send_x[0].wait_recv()
    project(chunks[1][0])
    for step in (1, 2, 3):
        kv_to(step, 1).start()
    collect(0)
    send_x[1].wait_recv()
    load_o.wait()

    def ow_quarter(side, number):
        return r.ow_all.at[side, pl.ds(pl.multiple_of(128 * number, 128), 128), :]

    def hand_on(number, way, target):
        part = ow_quarter(1 - ep, number)
        return remote(part, part, r.ow_send.at[number, way], r.ow_recv.at[number], target)

    sibling = 2 * (1 - x) + c

    def hand_first():
        send_ow.wait_recv()
        hand_on(head, 0, across).start()
        hand_on(head, 1, beside).start()

    def hand_second():
        hand_on(sibling, 0, across).wait_recv()
        hand_on(sibling, 1, beside).start()

    def hand_last():
        hand_on(2 * x + 1 - c, 1, beside).wait_recv()
        hand_on(2 * (1 - x) + 1 - c, 1, beside).wait_recv()

    send_ow = swap(12, ow_quarter(ep, head), ow_quarter(ep, head))
    send_od = swap(4, r.od_all.at[ep], r.od_all.at[ep])
    send_hot = swap(14, r.hot_all.at[mine], r.hot_all.at[mine])
    send_g = swap(2, r.grad, r.g_all.at[mine])
    for copy in (send_ow, send_od, send_hot):
        copy.start()
    project(chunks[2][0])
    for step in (1, 2, 3):
        kv_to(step, 2).start()
    load_q.wait()
    q_lin = dot(r.h1[...], r.q_w[...]) + dot(r.mids[:, :SPAN], r.q_up[...])
    query = rotate(q_lin, r.cosine[...], r.sine[...], 1.0).astype(BF16)
    for number in range(4):
        r.q_out[number] = query[:, 128 * number : 128 * number + 128]
    for step in (1, 2, 3):
        piece_to(*query_pieces, step).start()
    collect(1)
    send_g.start()
    hand_first()
    r.q_in[head] = r.q_out[head]
    r.m_s[...] = jnp.full(r.m_s.shape, LOW, F32)
    r.l_s[...] = jnp.zeros(r.l_s.shape, F32)
    r.acc[...] = jnp.zeros(r.acc.shape, F32)
    r.qt[:, HEAD:, :] = jnp.zeros((4, HEAD, 2 * block), BF16)
    r.dt[:, :HEAD, :] = jnp.zeros((4, HEAD, 2 * block), BF16)
    collect(2)
    wait_received(three_pieces, r.piece_recv.at[0])
    for b in range(4):
        scaled = r.q_in[b].astype(F32) * SCALE
        r.qt[b, :HEAD, :] = stack_columns(scaled).astype(BF16)
        r.qn[b] = stack_rows(scaled, False)

    def attend_step(p, b, keys, kinds):
        pos_row, start_row = pos_rows[b], start_rows[b]
        sees = start_row <= (4 * p + 1) * block
        everything = dot(keys, r.qt[b])
        scores, peak = [], None
        for first, count, position, masked in kinds:
            s = everything[first : first + count]
            if masked:
                key = position + iota(s.shape, 0)
                s = jnp.where((key <= pos_row) & (key >= start_row), s, LOW)
            scores.append(s)
            highest = jnp.max(s, axis=0, keepdims=True)
            if not masked:
                highest = jnp.where(sees, highest, LOW)
            peak = highest if peak is None else jnp.maximum(peak, highest)
        old = r.m_s[b]
        new = jnp.maximum(old, peak)
        r.m_s[b] = new
        blind = jnp.where(sees, new, -LOW)
        decay = jnp.exp(old - new)
        total = r.l_s[b] * decay
        weights = []
        for (first, count, position, masked), s in zip(kinds, scores):
            w = jnp.exp(s - (new if masked else blind))
            total = total + jnp.sum(w, axis=0, keepdims=True)
            weights.append(w.astype(BF16))
        weights = jnp.concatenate(weights, axis=0) if len(weights) > 1 else weights[0]
        r.l_s[b] = total
        r.acc[b] = r.acc[b] * decay + dot(keys, weights, TN)[HEAD:]

    def att_to(b, side):
        return remote(
            r.o_out.at[b], r.att_all.at[ep, :, pl.ds(pl.multiple_of(128 * head, 128), 128)],
            r.att_send.at[jnp.where(side == ep, 0, 1)], r.att_recv.at[ep], {"ctx": 4 * z + b, "ep": side},
        )

    def settle(b):
        r.lse[b] = r.m_s[b] + jnp.log(r.l_s[b])
        done = r.acc[b] / r.l_s[b]
        r.acc[b] = done
        r.o_out[b] = unstack(done).astype(BF16)

        @pl.when(b == head)
        def _():
            r.att_all[ep, :, pl.ds(pl.multiple_of(128 * head, 128), 128)] = r.o_out[b]

        @pl.when(b != head)
        def _():
            att_to(b, ep).start()

        att_to(b, 1 - ep).start()

    def take_chunk(p, chunk):
        @pl.when((p >= 0) & ((p > 0) | (chunk == 0) | (z < planes - 1)))
        def _():
            climb(p, chunk).wait_recv()
            climb_on(p, chunk)

    def whole_plane(p, b, masked):
        count = len(masked) * block
        attend_step(
            p, b, r.kvall[p, : len(masked)].reshape(count, 128),
            [(kb * block, block, (4 * p + kb) * block, masked[kb]) for kb in range(len(masked))],
        )

    def half_plane(b, here, first):
        attend_step(
            0, b, r.kvall[0, :, here, :].reshape(4 * rows, 128),
            [(kb * rows, rows, kb * block + first, kb == 0) for kb in range(4)],
        )

    def plane_forward(turn, carry):
        p = z - turn
        for b in (3, 2, 1, 0):

            @pl.when(turn == 0)
            def _():
                whole_plane(p, b, [kb in (0, b) for kb in range(b + 1)])

            @pl.when((turn > 0) & (p > 0))
            def _():
                whole_plane(p, b, [False] * 4)

            @pl.when((turn > 0) & (p == 0))
            def _():
                half_plane(b, mine, ep * rows)

            if b > 0:
                take_chunk(p - 1, 3 - b)

        @pl.when(turn == 0)
        def _():
            hand_second()

        return carry

    lax.fori_loop(0, z + 1, plane_forward, 0)

    @pl.when((z == planes - 1) & (z > 0))
    def _():
        climb(0, 1).wait_recv()
        climb(0, 2).wait_recv()

    for b in (3, 2, 1, 0):

        @pl.when(z > 0)
        def _():
            half_plane(b, theirs, rows - ep * rows)

        settle(b)

    def drain_forward():
        for chunk in range(3):
            wait_sent(three(chunk), r.kv_send.at[chunk])
        wait_sent(three_pieces, r.piece_send.at[0])

        @pl.when(z < planes - 1)
        def _():
            def left(p, carry):
                for chunk in range(3):
                    climb(p, chunk).wait_send()
                return carry

            lax.fori_loop(0, z + 1, left, 0)

    hand_last()
    send_od.wait_recv()

    def half_product(index, carry):
        which = jnp.where(index == 0, ep, 1 - ep)

        @pl.when(index == 0)
        def _():
            wait_received(r.o_out.at[pl.ds(0, 3)], r.att_recv.at[ep])

        @pl.when(index == 1)
        def _():
            wait_received(r.o_out, r.att_recv.at[1 - ep])

        r.halves[which] = dot(r.att_all[which], r.ow_all[which])
        r.half_mid[which] = dot(r.att_all[which], r.od_all[which], NT)
        return carry

    lax.fori_loop(0, 2, half_product, 0)
    mid_o = ((r.half_mid[0] + r.half_mid[1]) * r.mask[:, :SPAN]).astype(BF16)
    r.mid_o[...] = mid_o
    x2 = r.x_all[...].astype(F32) + (r.halves[0] + r.halves[1]) + dot(mid_o, r.o_up[...])
    r.x2[...] = x2
    h2 = rms(x2, r.moe_gain[...]).astype(BF16)
    r.h2[...] = h2
    send_hot.wait_recv()
    logits = dot(h2, r.router[...], NT)
    chosen = r.hot_all[:, : 2 * experts].astype(F32) > 0.5
    logits = jnp.where(chosen, logits, LOW)
    grown = jnp.where(chosen, jnp.exp(logits - jnp.max(logits, axis=1, keepdims=True)), 0.0)
    gates = grown / jnp.sum(grown, axis=1, keepdims=True)
    r.gates[...] = gates
    r.acc_out[...] = jnp.zeros(r.acc_out.shape, F32)
    r.acc_h2[...] = jnp.zeros(r.acc_h2.shape, F32)
    r.dgates[...] = jnp.zeros(r.dgates.shape, F32)
    lanes = 2 * SPAN
    load_in_down.wait()
    load_out_up.wait()
    send_g.wait_recv()
    in_down = r.in_down[...].reshape(experts * lanes, -1)
    out_up = r.out_up[...].reshape(experts * SPAN, -1)
    all_mids = dot(h2, in_down, NT)
    all_lifted = dot(r.g_all[...], out_up, NT)
    for e in range(experts):
        r.mid_in[e] = (all_mids[:, lanes * e : lanes * e + lanes] * r.mask[:, :lanes]).astype(BF16)
        r.lifted[e] = (all_lifted[:, SPAN * e : SPAN * e + SPAN] * r.mask[:, :SPAN]).astype(BF16)

    quarter = 2 * x + c

    def to_core(half, column):
        return remote(
            r.pack.at[half, 2 * column + 1 - c], r.core_land.at[half, column],
            r.core_send.at[half, column], r.core_recv.at[half, column], beside,
        )

    def to_column(half):
        return remote(
            r.pack.at[half, 2 * (1 - x) + c], r.x_land.at[half], r.x_send.at[half], r.x_recv.at[half], across
        )

    def add_core(half, column):
        to_core(half, column).wait_recv()
        number = 2 * column + c
        r.pack[half, number] = (
            r.pack[half, number].astype(F32) + r.core_land[half, column].astype(F32)
        ).astype(BF16)

    def final_rows(half, number):
        return (2 * number + half) * grad_rows

    def piece_of(owner):
        return (
            pl.multiple_of(owner // 4 * piece[0], piece[0]),
            pl.multiple_of(owner % 4 * piece[1], piece[1]),
        )

    def piece_in_pack(half, owner):
        row, lane = piece_of(owner)
        return r.pack.at[half, quarter, pl.ds(row, piece[0]), pl.ds(lane, piece[1])]

    def piece_in_final(half, owner):
        row, lane = piece_of(owner)
        start = pl.multiple_of(final_rows(half, quarter) + row, 16)
        return r.packed.at[pl.ds(start, piece[0]), pl.ds(lane, piece[1])]

    def plane_of(step):
        return lax.rem(z + step, planes)

    def give(half, step):
        other = plane_of(step)
        return remote(
            piece_in_pack(half, other), r.z_land.at[half, z], r.z_send.at[half, 0],
            r.z_recv.at[half, 0], {"ctx": block_of(other, x, c), "ep": ep},
        )

    def spread(half, step):
        other = plane_of(step)
        part = piece_in_final(half, z % owners)
        return remote(
            part, part, r.z_send.at[half, 1], r.z_recv.at[half, 1],
            {"ctx": block_of(other, x, c), "ep": ep},
        )

    def pieces(count):
        return r.z_land.at[0, pl.ds(0, count)]

    def for_pieces(wait, sem):
        if owners < planes:

            @pl.when(z < owners)
            def _():
                wait(pieces(owners - 1), sem)

            @pl.when(z >= owners)
            def _():
                wait(pieces(owners), sem)

        else:
            wait(pieces(owners - 1), sem)

    def each_plane(act, among_owners):
        def step(number, carry):
            if among_owners and owners < planes:

                @pl.when(plane_of(number) < owners)
                def _():
                    act(number)

            else:
                act(number)
            return carry

        lax.fori_loop(1, planes, step, 0)

    def if_owner(act):
        if owners < planes:
            pl.when(z < owners)(act)
        else:
            act()

    def over_final(half, number, way, target):
        part = r.packed.at[pl.ds(pl.multiple_of(final_rows(half, number), 16), grad_rows)]
        return remote(part, part, r.last_send.at[half, way, number], r.last_recv.at[half, number], target)

    def stage_pieces(half):
        to_column(half).wait_recv()
        r.pack[half, quarter] = (
            r.pack[half, quarter].astype(F32) + r.x_land[half].astype(F32)
        ).astype(BF16)
        each_plane(lambda step: give(half, step).start(), True)

    def stage_own(half):
        def act():
            wait_received(pieces(planes - 1), r.z_recv.at[half, 0])
            r.z_land[half, z] = piece_in_pack(half, z % owners)[...]

            total = jnp.sum(r.z_land[half].astype(F32), axis=0)
            piece_in_final(half, z % owners)[...] = total.astype(BF16)
            each_plane(lambda step: spread(half, step).start(), False)

        if_owner(act)

    def stage_column(half):
        for_pieces(wait_received, r.z_recv.at[half, 1])
        over_final(half, quarter, 0, across).start()
        over_final(half, quarter, 1, beside).start()

    def stage_core(half):
        over_final(half, 2 * (1 - x) + c, 0, across).wait_recv()
        over_final(half, 2 * (1 - x) + c, 1, beside).start()

    def stage_end(half):
        over_final(half, 2 * x + 1 - c, 1, beside).wait_recv()
        over_final(half, 2 * (1 - x) + 1 - c, 1, beside).wait_recv()

    def stage_drain(half):
        for_pieces(wait_sent, r.z_send.at[half, 0])
        if_owner(lambda: wait_sent(pieces(planes - 1), r.z_send.at[half, 1]))
        over_final(half, quarter, 0, across).wait_send()
        over_final(half, quarter, 1, beside).wait_send()
        over_final(half, 2 * (1 - x) + c, 1, beside).wait_send()
        to_core(half, 0).wait_send()
        to_core(half, 1).wait_send()
        to_column(half).wait_send()

    def one(turn, carry):
        slot = turn % slots
        e = expert_at(turn)
        half, q = turn // 4, quarter_at(turn % 4)
        for copy in expert_loads(turn):
            copy.wait()
        h2, g = r.h2[...], r.g_all[...]
        gate = jnp.sum(
            jnp.where(iota((block, 2 * experts), 1) == e + ep * experts, r.gates[...], 0.0), axis=1, keepdims=True
        )
        mid_in, lifted = r.mid_in[e], r.lifted[e]
        gate_part = dot(h2, r.w_in[slot, :, :FF]) + dot(mid_in[:, :SPAN], r.w_in_up[slot, 0])
        up_part = dot(h2, r.w_in[slot, :, FF:]) + dot(mid_in[:, SPAN:], r.w_in_up[slot, 1])
        d_act = dot(g, r.w_out[slot], NT) + dot(lifted, r.w_out_down[slot])
        squash = 1.0 / (1.0 + jnp.exp(-gate_part))
        silu = gate_part * squash
        act = (silu * up_part).astype(BF16)
        mid_out = dot(act, r.w_out_down[slot], NT) * r.mask[:, :SPAN]
        d_gate = jnp.sum(act.astype(F32) * d_act, axis=1, keepdims=True)
        r.dgates[...] += jnp.where(iota(r.dgates.shape, 1) == e, d_gate, 0.0)
        d_act = d_act * gate
        d_up = (d_act * silu).astype(BF16)
        d_gp = (d_act * up_part * squash * (1.0 + gate_part * (1.0 - squash))).astype(BF16)
        d_mid_in = (
            jnp.concatenate([dot(d_gp, r.w_in_up[slot, 0], NT), dot(d_up, r.w_in_up[slot, 1], NT)], axis=1)
            * r.mask[:, :lanes]
        ).astype(BF16)
        scaled_mid = (mid_out * gate).astype(BF16)
        r.d_mid_in[e] = d_mid_in
        r.mid_out[e] = scaled_mid
        r.acc_out[...] += dot((act.astype(F32) * gate).astype(BF16), r.w_out[slot])

        @pl.when(turn < experts - deferred)
        def _():
            r.acc_h2[...] += dot(d_gp, r.w_in[slot, :, :FF], NT) + dot(d_up, r.w_in[slot, :, FF:], NT)

        @pl.when(turn >= experts - deferred)
        def _():
            r.d_joint[turn - (experts - deferred), :, :FF] = d_gp
            r.d_joint[turn - (experts - deferred), :, FF:] = d_up

        r.pack[half, q, :64, :] = dot(d_mid_in, h2, TN).astype(BF16)
        r.pack[half, q, 64:96, :FF] = dot(mid_in[:, :SPAN], d_gp, TN).astype(BF16)
        r.pack[half, q, 64:96, FF:] = dot(mid_in[:, SPAN:], d_up, TN).astype(BF16)
        r.pack[half, q, 96:112, :] = fold(
            dot((lifted.astype(F32) * gate).astype(BF16), act, TN)
        ).astype(BF16)
        r.pack[half, q, 112:, :] = dot(scaled_mid, g, TN).astype(BF16)

        @pl.when(turn + slots < experts)
        def _():
            for copy in expert_loads(turn + slots):
                copy.start()

        @pl.when(turn % 4 == 0)
        def _():
            to_core(half, 1 - x).start()

        @pl.when(turn % 4 == 1)
        def _():
            to_core(half, x).start()

        @pl.when(turn % 4 == 2)
        def _():
            add_core(half, 1 - x)
            to_column(half).start()

        @pl.when(turn % 4 == 3)
        def _():
            add_core(half, x)

        @pl.when(turn == 5)
        def _():
            stage_pieces(0)

        return carry

    lax.fori_loop(0, experts, one, 0)
    every = range(experts)
    r.dg_trade[ep] = r.dgates[...].T[:8]
    send_dg = swap(9, r.dg_trade.at[ep], r.dg_trade.at[ep])
    send_dg.start()
    all_d_mids = jnp.concatenate([r.d_mid_in[e] for e in every], axis=1)
    tile = 256
    send_h2 = []
    for number in range(r.acc_h2.shape[1] // tile):
        columns = slice(tile * number, tile * number + tile)
        ends = r.acc_h2[:, columns] + dot(all_d_mids, r.in_down[:, :, columns].reshape(experts * lanes, tile))
        for index in range(deferred):
            ends = ends + dot(r.d_joint[index], r.w_in[(experts - deferred + index) % slots, columns, :], NT)
        r.trade[0, :, columns] = jnp.where(ep == 0, ends[rows:], ends[:rows]).astype(BF16)
        r.own_h2[:, columns] = jnp.where(ep == 0, ends[:rows], ends[rows:])
        copy = swap((10, 3, 15, 16)[number], r.trade.at[0, :, columns], r.trade.at[1, :, columns])
        copy.start()
        send_h2.append(copy)
    r.acc_out[...] += dot(jnp.concatenate([r.mid_out[e] for e in every], axis=1), r.out_up[...].reshape(experts * SPAN, -1))
    r.out_trade[0] = r.acc_out[theirs, :].astype(BF16)
    send_out = swap(11, r.out_trade.at[0], r.out_trade.at[1])
    stage_own(0)
    stage_pieces(1)

    def small_sum(number, source, landing, result, shared):
        tiles = source.shape[0] // 16
        width = landing.shape[2]
        each = source.shape[1] // width
        holders = tiles * each
        shared = shared * each
        private = me >= shared
        mine_too = (me < holders) & (private | (me % 2 == ep))
        send_one, send_two = r.small_send.at[number, 0], r.small_send.at[number, 1]
        recv_one, recv_two = r.small_recv.at[number, 0], r.small_recv.at[number, 1]
        own_index = me + blocks * ep

        def region(ref, owner):
            return ref.at[span(owner // each * 16, 16), span(owner % each * width, width)]

        def several(count):
            return landing.at[pl.ds(0, count)]

        def scatter():
            def act(index):
                owner = lax.rem(me + index, blocks)
                side = jnp.where(owner < shared, owner % 2, ep)

                @pl.when((owner < holders) & ((index > 0) | (side != ep)))
                def _():
                    remote(
                        region(source, owner), landing.at[own_index], send_one, recv_one, {"ctx": owner, "ep": side}
                    ).start()

            each_block(act)

        def add(pieces):
            return jnp.sum(pieces.astype(F32), axis=0).astype(BF16)

        def each_block(act):
            if blocks <= 16:
                for index in range(blocks):
                    act(index)
            else:

                def step(index, carry):
                    act(index)
                    return carry

                lax.fori_loop(0, blocks, step, 0)

        def tell(side):
            part = region(result, me % holders)

            def act(index):
                device = lax.rem(me + index, blocks)

                @pl.when((index > 0) | (side != ep))
                def _():
                    remote(part, part, send_two, recv_two, {"ctx": device, "ep": side}).start()

            each_block(act)

        def total():
            @pl.when(mine_too)
            def _():
                landing[own_index] = region(source, me % holders)[...]

            @pl.when(mine_too & private)
            def _():
                wait_received(several(blocks - 1), recv_one)
                region(result, me % holders)[...] = add(landing[pl.ds(blocks * ep, blocks)])
                tell(ep)

            if shared:

                @pl.when(mine_too & jnp.logical_not(private))
                def _():
                    wait_received(several(2 * blocks - 1), recv_one)
                    region(result, me % holders)[...] = add(landing[...])
                    tell(ep)
                    tell(1 - ep)

        def finish():
            @pl.when(mine_too)
            def _():
                wait_received(several(holders - 1), recv_two)
                wait_sent(several(holders - 1), send_one)

            @pl.when(jnp.logical_not(mine_too))
            def _():
                wait_received(several(holders), recv_two)
                wait_sent(several(holders), send_one)

            @pl.when(mine_too & private)
            def _():
                wait_sent(several(blocks - 1), send_two)

            if shared:

                @pl.when(mine_too & jnp.logical_not(private))
                def _():
                    wait_sent(several(2 * blocks - 1), send_two)

        return scatter, total, finish

    early_scatter, early_total, early_finish = small_sum(0, r.early, r.early_land, r.early_out, 4)
    late_scatter, late_total, late_finish = small_sum(1, r.late, r.late_land, r.late_out, 6)
    drain_forward()

    send_dg.wait_recv()
    blank = jnp.zeros((112, block), F32)
    table = jnp.concatenate([r.dg_trade[0], r.dg_trade[1], blank], axis=0).T
    r.dgates[:, : 2 * experts] = table[:, : 2 * experts]
    d_gates = r.dgates[mine, : 2 * experts]
    gates = r.gates[mine, :]
    d_logits = (gates * (d_gates - jnp.sum(gates * d_gates, axis=1, keepdims=True))).astype(BF16)
    from_router = dot(d_logits, r.router[...])
    stage_column(0)
    for copy in send_h2:
        copy.wait_recv()
    d_h2 = r.own_h2[...] + r.trade[1].astype(F32) + from_router
    d_x2 = r.grad[...].astype(F32) + rms_back(r.x2[mine, :], r.moe_gain[...], d_h2)
    d_attn = d_x2.astype(BF16)
    r.own_h2[...] = d_x2
    d_mid_o = (dot(d_attn, r.o_up[...], NT) * r.mask[mine, :SPAN]).astype(BF16)

    def grad_to(side, number):
        return remote(
            r.d_out.at[side, number], r.d_in.at[2 * head + ep], r.piece_send.at[1], r.piece_recv.at[1],
            {"ctx": 4 * z + number, "ep": side},
        )

    for side in (0, 1):
        d_att = (dot(d_attn, r.ow_all[side], NT) + dot(d_mid_o, r.od_all[side])).astype(BF16)
        for number in range(4):
            r.d_out[side, number] = d_att[:, 128 * number : 128 * number + 128]

            @pl.when((side != ep) | (number != head))
            def _():
                grad_to(side, number).start()

    send_out.start()
    r.dqt[...] = jnp.zeros(r.dqt.shape, F32)
    r.early[:32, :] = dot(r.mid_o[mine, :], d_attn, TN).astype(BF16)
    for side in (0, 1):
        r.early[32:, heads * side : heads * side + heads] = dot(d_mid_o, r.att_all[side, mine, :], TN).astype(BF16)
    early_scatter()
    stage_own(1)

    r.d_in[2 * head + ep] = r.d_out[ep, head]
    wait_received(r.d_in.at[pl.ds(0, 7)], r.piece_recv.at[1])
    for b in range(4):
        received = r.d_in[2 * b : 2 * b + 2].reshape(block, 128).astype(F32)
        turned = stack_columns(received)
        r.dt[b, HEAD:, :] = turned.astype(BF16)
        r.delta[b] = jnp.sum(turned * r.acc[b], axis=0, keepdims=True)
        r.dn[b] = stack_rows(received, True)

    def back_step(p, kb, kinds):
        kv = r.kvall[p, kb]
        grown = None
        for b, masked in kinds:
            pos_row, start_row = pos_rows[b], start_rows[b]
            s = dot(kv, r.qt[b])
            base = r.lse[b]
            if masked:
                key = (4 * p + kb) * block + iota(s.shape, 0)
                w = jnp.where((key <= pos_row) & (key >= start_row), jnp.exp(s - base), 0.0)
            else:
                w = jnp.exp(s - jnp.where(start_row <= (4 * p + 1) * block, base, -LOW))
            d_w = dot(kv, r.dt[b])
            d_s = (w * (d_w - r.delta[b])).astype(BF16)
            added = dot(d_s, r.qn[b]) + dot(w.astype(BF16), r.dn[b])
            grown = added if grown is None else grown + added
            r.dqt[b] += dot(kv, d_s, TN)[:HEAD]
        r.kvall[p, kb] = grown.astype(BF16)

    def lower(p, kb):
        return remote(
            r.kvall.at[p, kb], r.from_up.at[p % kept, kb], r.down_send.at[p, kb], r.down_recv.at[p, kb], down
        )

    def back_to(source, landing, send, recv, b):
        return remote(source.at[b], landing.at[head], send, recv, device_of(b))

    def give_back(source, landing, send, recv, b):
        @pl.when(b == head)
        def _():
            landing[b] = source[b]

        @pl.when(b != head)
        def _():
            back_to(source, landing, send, recv, b).start()

    dq_pieces = (r.dq_out, r.dq_in, r.piece_send.at[2], r.piece_recv.at[2])
    dkv_pieces = (r.kvall.at[z], r.dkv_in, r.piece_send.at[3], r.piece_recv.at[3])

    def pass_on(step):
        p, kb = step // 4, step % 4

        @pl.when(z < planes - 1)
        def _():
            lower(p, kb).wait_recv()
            r.kvall[p, kb] = (r.kvall[p, kb].astype(F32) + r.from_up[p % kept, kb].astype(F32)).astype(BF16)
            if planes > kept:

                @pl.when((kb == 3) & (p + kept <= z))
                def _():
                    pl.semaphore_signal(r.credit, inc=1, device_id=up, device_id_type=MESH)

        @pl.when(p < z)
        def _():
            if planes > kept:

                @pl.when((kb == 0) & (p >= kept))
                def _():
                    pl.semaphore_wait(r.credit, 1)

            lower(p, kb).start()

        @pl.when(p == z)
        def _():
            give_back(*dkv_pieces, kb)

    def after(step):
        @pl.when(z == planes - 1)
        def _():
            pass_on(step)

        @pl.when((z < planes - 1) & (step >= 2))
        def _():
            pass_on(step - 2)

    def plane_back(p, carry):
        @pl.when(p < z)
        def _():
            @pl.when(p == 0)
            def _():
                back_step(p, 0, [(b, True) for b in range(4)])
                after(0)

            def middle(kb, inner):
                back_step(p, kb, [(b, False) for b in range(4)])
                after(4 * p + kb)
                return inner

            lax.fori_loop(jnp.where(p == 0, 1, 0), 4, middle, 0)

        @pl.when(p == z)
        def _():
            for kb in range(4):
                back_step(p, kb, [(b, b == kb or kb == 0) for b in range(kb, 4)])
                r.dq_out[kb] = (unstack(r.dqt[kb]) * SCALE).astype(BF16)
                give_back(*dq_pieces, kb)
                after(4 * p + kb)

        @pl.when(p == 0)
        def _():
            stage_core(0)

        @pl.when(p == 1)
        def _():
            stage_column(1)

        @pl.when(p == 2)
        def _():
            early_total()

        return carry

    lax.fori_loop(0, planes, plane_back, 0)

    @pl.when(z < planes - 1)
    def _():
        pass_on(4 * z + 2)
        pass_on(4 * z + 3)

    cosine, sine = r.cosine[...], r.sine[...]
    wait_received(three_pieces, r.piece_recv.at[2])
    wait_received(three_pieces, r.piece_recv.at[3])
    d_query = jnp.concatenate([r.dq_in[number] for number in range(4)], axis=1)
    d_q = rotate(d_query.astype(F32), cosine, sine, -1.0).astype(BF16)
    d_key = jnp.concatenate([r.dkv_in[number, :, :HEAD] for number in range(4)], axis=1)
    d_k = rotate(d_key.astype(F32), cosine, sine, -1.0).astype(BF16)
    d_value = jnp.concatenate([r.dkv_in[number, :, HEAD:] for number in range(4)], axis=1)
    d_mids = jnp.concatenate(
        [dot(d_q, r.q_up[...], NT), dot(d_k, r.kv_up[0], NT), dot(d_value, r.kv_up[1], NT)], axis=1
    )
    d_mids = (d_mids * r.mask[:, : 3 * SPAN]).astype(BF16)
    r.late[:96, :] = dot(d_mids, r.h1[...], TN).astype(BF16)
    r.late[96:112, :] = fold(dot(r.mids[:, :SPAN], d_q, TN)).astype(BF16)
    r.late[112:, :] = fold(
        jnp.concatenate(
            [dot(r.mids[:, SPAN : 2 * SPAN], d_k, TN), dot(r.mids[:, 2 * SPAN :], d_value, TN)], axis=1
        )
    ).astype(BF16)
    late_scatter()
    full = (
        dot(d_q, r.q_w[...], NT) + dot(d_k, r.kv_w[0], NT) + dot(d_value, r.kv_w[1], NT) + dot(d_mids, r.qkv_down[...])
    )
    first, second = full[:rows], full[rows:]
    r.norm_trade[0] = jnp.where(ep == 0, second, first).astype(BF16)
    send_norm = swap(13, r.norm_trade.at[0], r.norm_trade.at[1])
    send_norm.start()
    stage_core(1)
    stage_end(0)
    early_finish()
    both = r.early_out[32:64, :]
    own_half = jnp.where(ep == 0, both[:, :heads].astype(F32), both[:, heads:].astype(F32))
    r.early_out[32:48, :] = fold(own_half).astype(BF16)
    send_out.wait_recv()
    r.block_out[...] = (r.x2[mine, :] + (r.acc_out[mine, :] + r.out_trade[1].astype(F32))).astype(BF16)
    own = jnp.where(ep == 0, first, second)
    late_total()
    stage_end(1)

    def store(number, start, count):
        return pltpu.make_async_copy(
            r.packed.at[pl.ds(start, count)], r.out.at[pl.ds(start, count)], r.load_sem.at[number]
        )

    stores = [store(0, 0, base), store(1, base + 128, 128), store(2, base + 384, 64)]
    for copy in stores:
        copy.start()
    send_norm.wait_recv()
    own = own + r.norm_trade[1].astype(F32)
    r.in_grad[...] = (
        r.own_h2[...] + rms_back(r.x_all[mine, :].astype(F32), r.attn_gain[...], own)
    ).astype(BF16)
    stores.append(store(3, base + 256, 128))
    stores[-1].start()
    stage_drain(0)
    stage_drain(1)

    for copy in (*send_x, send_ow, send_od, send_hot, send_g, send_dg, *send_h2, send_out, send_norm):
        copy.wait_send()
    wait_sent(r.o_out.at[pl.ds(0, 3)], r.att_send.at[0])
    wait_sent(r.o_out, r.att_send.at[1])
    wait_sent(r.d_in.at[pl.ds(0, 7)], r.piece_send.at[1])
    for number in (2, 3):
        wait_sent(three_pieces, r.piece_send.at[number])
    hand_on(head, 0, across).wait_send()
    hand_on(head, 1, beside).wait_send()
    hand_on(sibling, 1, beside).wait_send()

    def drain(p, carry):
        for kb in range(4):
            lower(p, kb).wait_send()
        return carry

    lax.fori_loop(0, z, drain, 0)
    late_finish()
    stores.append(store(4, base, 128))
    stores[-1].start()
    for copy in stores:
        copy.wait()


RESULTS = (
    "ein_down", "ein_up", "eout_down", "eout_up", "block_out", "in_grad", "g_down", "g_q", "g_kv", "g_od", "g_ou",
)


def unpack_kernel(packed, *refs):
    count = len(RESULTS)
    outs = dict(zip(RESULTS, refs[:count]))
    held = dict(zip(RESULTS, refs[count : 2 * count]))
    rows, sem_in, sem_out = refs[2 * count :]
    experts = outs["ein_down"].shape[0]
    grad_rows = 144
    base = experts * grad_rows

    def fetch(start, size, number):
        return pltpu.make_async_copy(
            packed.at[pl.ds(start, size)], rows.at[pl.ds(start, size)], sem_in.at[number]
        )

    fetches = [fetch(grad_rows * e, grad_rows, e) for e in range(experts)]
    fetches.append(fetch(base, rows.shape[0] - base, experts))
    for copy in fetches:
        copy.start()
    stores = []

    def store(name, number):
        copy = pltpu.make_async_copy(
            held[name] if number is None else held[name].at[number],
            outs[name] if number is None else outs[name].at[number],
            sem_out.at[len(stores)],
        )
        copy.start()
        stores.append(copy)

    for e in range(experts):
        fetches[e].wait()
        part = rows[grad_rows * e : grad_rows * e + grad_rows, :].astype(F32)
        held["ein_down"][e] = part[:64]
        held["ein_up"][e, 0] = part[64:96, :FF]
        held["ein_up"][e, 1] = part[64:96, FF:]
        held["eout_down"][e, :16] = part[96:112, :FF]
        held["eout_down"][e, 16:] = part[96:112, FF:]
        held["eout_up"][e] = part[112:]
        for name in RESULTS[:4]:
            store(name, e)
    fetches[experts].wait()
    late = rows[base : base + 128, :].astype(F32)
    early = rows[base + 384 : base + 448, :].astype(F32)
    held["block_out"][...] = rows[base + 128 : base + 256, :]
    held["in_grad"][...] = rows[base + 256 : base + 384, :]
    held["g_down"][...] = late[:96]
    held["g_q"][:16, :] = late[96:112, :FF]
    held["g_q"][16:, :] = late[96:112, FF:]
    kv = FF // 2
    for side in (0, 1):
        for half in (0, 1):
            first = kv * (2 * half + side)
            held["g_kv"][side, 16 * half : 16 * half + 16, :] = late[112:, first : first + kv]
    held["g_od"][:16, :] = early[32:48, :FF]
    held["g_od"][16:, :] = early[32:48, FF:]
    held["g_ou"][...] = early[:32]
    for name in RESULTS[4:]:
        store(name, None)
    for copy in stores:
        copy.wait()


def per_device(
    resid_in, out_grad, attn_gain, q_weight, key_value_weight, o_weight, moe_gain, router, expert_in,
    expert_out, qkv_down, q_up, key_value_up_factor, o_down, o_up, expert_in_down, expert_in_up,
    expert_out_down, expert_out_up, expert_ids, doc_starts, doc_adapter,
):
    blocks = lax.axis_size("ctx")
    planes = blocks // 4
    rows, width = resid_in.shape
    block = 2 * rows
    heads = q_weight.shape[1]
    kv = key_value_weight.shape[2]
    experts = expert_in.shape[0]
    slots = 6 if planes <= 4 else 4
    kept = planes if planes <= 4 else 2
    grad_rows = 2 * SPAN + SPAN + SPAN // 2 + SPAN
    base = experts * grad_rows
    groups = 3 if planes >= 12 else 1
    piece = (grad_rows // groups, width // 4)
    early_width = max(128, 4 * width // blocks)
    late_width = max(128, 8 * width // blocks)
    freq = np.tile(np.power(10000.0, -2.0 * np.arange(HEAD // 2) / HEAD).astype(np.float32), 4)[None, :]

    def shape(dims, kind=BF16):
        return jax.ShapeDtypeStruct(dims, kind)

    def dma(*dims):
        return pltpu.SemaphoreType.DMA(dims)

    def low(*dims):
        return pltpu.VMEM(dims, BF16)

    def full(*dims):
        return pltpu.VMEM(dims, F32)

    operands = dict(
        resid=resid_in, grad=out_grad, ids=expert_ids.T, starts=doc_starts, adapters=doc_adapter,
        attn_gain=attn_gain[None, :], moe_gain=moe_gain[None, :], freq=jnp.asarray(freq), qkv_down=qkv_down.T,
        q_up=q_up, kv_up=key_value_up_factor, o_down=o_down.T, o_up=o_up, router=router.T, q_hbm=q_weight,
        kv_hbm=key_value_weight, o_hbm=o_weight, in_hbm=expert_in, out_hbm=expert_out,
        in_down_hbm=jnp.swapaxes(expert_in_down, 1, 2), in_up_hbm=expert_in_up,
        out_down_hbm=jnp.swapaxes(expert_out_down, 1, 2), out_up_hbm=expert_out_up,
    )
    results = dict(out=shape((base + 448, width)))
    scratch = dict(
        q_w=low(*q_weight.shape), kv_w=low(*key_value_weight.shape), ow_all=low(2, heads, width),
        od_all=low(2, SPAN, heads), w_in=low(slots, *expert_in.shape[1:]), w_out=low(slots, *expert_out.shape[1:]),
        in_down=low(experts, 2 * SPAN, width), w_in_up=low(slots, *expert_in_up.shape[1:]),
        w_out_down=low(slots, SPAN, FF), out_up=low(experts, SPAN, width),
        mid_in=low(experts, block, 2 * SPAN), lifted=low(experts, block, SPAN),
        d_mid_in=low(experts, block, 2 * SPAN), d_joint=low(2, block, 2 * FF), mid_out=low(experts, block, SPAN),
        x_all=low(block, width), g_all=low(block, width), h1=low(block, width), h2=low(block, width),
        hot_all=low(block, 128), mask=full(block, 128), cosine=full(block, 128), sine=full(block, 128),
        mids=low(block, 3 * SPAN), kvall=low(planes, 4, block, 128), kv_out=low(4, block, 128), q_out=low(4, block, 128),
        q_in=low(4, block, 128), d_out=low(2, 4, rows, 128), d_in=low(8, rows, 128), own_h2=full(rows, width), o_out=low(4, block, 128),
        dq_out=low(4, block, 128), dq_in=low(4, block, 128), dkv_in=low(4, block, 128), qt=low(4, 128, 2 * block),
        qn=low(4, 2 * block, 128), dt=low(4, 128, 2 * block), dn=low(4, 2 * block, 128),
        m_s=full(4, 1, 2 * block), l_s=full(4, 1, 2 * block), lse=full(4, 1, 2 * block),
        delta=full(4, 1, 2 * block), acc=full(4, HEAD, 2 * block), dqt=full(4, HEAD, 2 * block),
        att_all=low(2, block, heads), halves=full(2, block, width), half_mid=full(2, block, SPAN), mid_o=low(block, SPAN), x2=full(block, width),
        gates=full(block, 2 * experts), dgates=full(block, 128), trade=low(2, rows, width), out_trade=low(2, rows, width),
        norm_trade=low(2, rows, width), dg_trade=full(2, 8, block),
        pack=low(2, 4, grad_rows, width), core_land=low(2, 2, grad_rows, width), x_land=low(2, grad_rows, width),
        z_land=low(2, planes, *piece), early=low(64, width), late=low(128, width),
        early_land=low(2 * blocks, 16, early_width), late_land=low(2 * blocks, 16, late_width),
        from_up=low(kept, 4, block, 128), credit=pltpu.SemaphoreType.REGULAR,
        packed=low(base + 448, width), load_sem=dma(5), expert_sem=dma(slots, 4), pair_send=dma(17), pair_recv=dma(17),
        kv_send=dma(3), kv_recv=dma(3), piece_send=dma(4), piece_recv=dma(4), up_send=dma(planes, 3),
        up_recv=dma(planes, 3), ow_send=dma(4, 2), ow_recv=dma(4), att_send=dma(2), att_recv=dma(2), core_send=dma(2, 2), core_recv=dma(2, 2),
        x_send=dma(2), x_recv=dma(2), z_send=dma(2, 2), z_recv=dma(2, 2), last_send=dma(2, 2, 4),
        last_recv=dma(2, 4),
        small_send=dma(2, 2), small_recv=dma(2, 2), down_send=dma(planes, 4),
        down_recv=dma(planes, 4),
    )
    (out,) = pl.pallas_call(
        functools.partial(layer_kernel, planes, slots, INPUTS + OUTPUTS + tuple(scratch)),
        out_shape=[results[name] for name in OUTPUTS],
        in_specs=[
            SMEM if name in ("starts", "adapters") else HBM if name.endswith("hbm") else VMEM for name in INPUTS
        ],
        out_specs=[HBM] * len(OUTPUTS),
        scratch_shapes=list(scratch.values()),
        compiler_params=pltpu.CompilerParams(
            collective_id=1, has_side_effects=True, vmem_limit_bytes=62 << 20
        ),
        name="layer",
    )(*[operands[name] for name in INPUTS])

    unpacked = dict(
        ein_down=shape((experts, 2 * SPAN, width), F32), ein_up=shape((experts, 2, SPAN, FF), F32),
        eout_down=shape((experts, SPAN, FF), F32), eout_up=shape((experts, SPAN, width), F32),
        block_out=shape((rows, width)), in_grad=shape((rows, width)), g_down=shape((3 * SPAN, width), F32),
        g_q=shape((SPAN, heads), F32), g_kv=shape((2, SPAN, kv), F32), g_od=shape((SPAN, heads), F32),
        g_ou=shape((SPAN, width), F32),
    )
    ein_down, ein_up, eout_down, eout_up, block_out, in_grad, g_down, g_q, g_kv, g_od, g_ou = pl.pallas_call(
        unpack_kernel,
        out_shape=[unpacked[name] for name in RESULTS],
        in_specs=[HBM],
        out_specs=[HBM] * len(RESULTS),
        scratch_shapes=[
            *[pltpu.VMEM(unpacked[name].shape, unpacked[name].dtype) for name in RESULTS],
            pltpu.VMEM(out.shape, BF16), dma(experts + 1), dma(4 * experts + 7),
        ],
        compiler_params=pltpu.CompilerParams(vmem_limit_bytes=62 << 20),
        name="unpack",
    )(out)
    return (
        block_out, in_grad, g_down.T, g_q, g_kv, g_od.T, g_ou, jnp.swapaxes(ein_down, 1, 2), ein_up,
        jnp.swapaxes(eout_down, 1, 2), eout_up,
    )


def solution(mesh):
    placed = (
        P(("ctx", "ep"), None),
        P(("ctx", "ep"), None),
        P(),
        P(None, "ep"),
        P(None, None, "ep"),
        P("ep", None),
        P(),
        P(),
        P("ep", None, None),
        P("ep", None, None),
        P(),
        P(None, "ep"),
        P(None, None, "ep"),
        P("ep", None),
        P(),
        P("ep", None, None),
        P("ep", None, None, None),
        P("ep", None, None),
        P("ep", None, None),
        P(("ctx", "ep"), None),
        P(),
        P(),
    )
    return jax.shard_map(
        per_device,
        mesh=mesh,
        in_specs=placed,
        out_specs=(
            P(("ctx", "ep"), None),
            P(("ctx", "ep"), None),
            P(),
            P(None, "ep"),
            P(None, None, "ep"),
            P("ep", None),
            P(),
            P("ep", None, None),
            P("ep", None, None, None),
            P("ep", None, None),
            P("ep", None, None),
        ),
        check_vma=False,
    )
```
